32 devices in a mesh: wide: 8 (over z, x), narrow: 4 (over y, core).
Axes of the slice: x: 2, y: 2, z: 4, core: 2. Of those that a mesh axis runs over, the one named last changes fastest.
Arguments:
- data_x: bfloat16 [8192, 1024], P(('wide', 'narrow')), may hold values from -6 to 6
- data_group: int32 [8192], P(('wide', 'narrow')), may hold values from 0 to 7
- batch_x: bfloat16 [64, 1024], P(('wide', 'narrow')), may hold values from -6 to 6
- batch_group: int32 [64], P('wide'), may hold values from 0 to 7
- batch_index: int32 [64], P('wide'), may hold values from 0 to 8191
- prec_index: int32 [64], P('wide'), may hold values from 0 to 15
- prec_table: float32 [16], replicated, may hold values from 0.5 to 4
- targets: float32 [64, 16], P('wide'), may hold values from -6 to 6
- omega: bfloat16 [2048, 2048], replicated, may hold values from -0.125 to 0.125
- phase: float32 [2048], replicated, may hold values from -3.140625 to 3.140625
- prior_w: float32 [2048, 16], replicated, may hold values from -6 to 6
- w1_master: float32 [1024, 2048], P(None, 'narrow'), may hold values from -0.1875 to 0.1875
- w1_moment: float32 [1024, 2048], P(None, 'narrow'), may hold values from -6.1035156e-05 to 6.1035156e-05
- w1_second: float32 [1024, 2048], P(None, 'narrow'), may hold values from 1.5894572e-12 to 6.3578288e-12
- w2_master: float32 [2048, 2048], P(None, 'narrow'), may hold values from -0.125 to 0.125
- w2_moment: float32 [2048, 2048], P(None, 'narrow'), may hold values from -6.1035156e-05 to 6.1035156e-05
- w2_second: float32 [2048, 2048], P(None, 'narrow'), may hold values from 1.5894572e-12 to 6.3578288e-12
- alpha: float32 [8192, 16], P(('wide', 'narrow')), may hold values from -4 to 4
- alpha_moment: float32 [8192, 16], P(('wide', 'narrow')), may hold values from -4.5776367e-05 to 4.5776367e-05
- alpha_second: float32 [8192, 16], P(('wide', 'narrow')), may hold values from 7.6293946e-13 to 3.0517578e-12
Outputs:
- loss_sum: float32 [], replicated
- weight_total: float32 [], replicated
- norm_sq: float32 [], replicated
- w1_moment_new: float32 [1024, 2048], P(None, 'narrow')
- w1_second_new: float32 [1024, 2048], P(None, 'narrow')
- w1_new: float32 [1024, 2048], P(None, 'narrow')
- w1_copy: bfloat16 [1024, 2048], P(None, 'narrow')
- w2_moment_new: float32 [2048, 2048], P(None, 'narrow')
- w2_second_new: float32 [2048, 2048], P(None, 'narrow')
- w2_new: float32 [2048, 2048], P(None, 'narrow')
- w2_copy: bfloat16 [2048, 2048], P(None, 'narrow')
- alpha_moment_new: float32 [8192, 16], P(('wide', 'narrow'))
- alpha_second_new: float32 [8192, 16], P(('wide', 'narrow'))
- alpha_new: float32 [8192, 16], P(('wide', 'narrow'))
The draws below stay inside these ranges and needn't reach their ends.
All inputs are finite; a program needn't handle non-finite values.
Results may differ from the reference program's by a relative error of at most 0.0065.
Values may be sent and summed in bfloat16 or wider, within the bound.
A program may use at most 320 MiB of HBM per device.

```python
import math
import jax
import jax.numpy as jnp
from jax import lax

DIN = 1024
HID = 2048
FEAT = 2048
MFEAT = 2048
SAMPLES = 16
GROUPS = 8
PTABLE = 16
STEP_NUM = 10
N_ROWS = 8192
BATCH = 64


def set_ends(array, own_key, smallest, largest):
    longest = array.shape.index(max(array.shape))
    spots = []
    for shift in (0, 1):
        where = [jax.random.randint(jax.random.fold_in(own_key, axis), (), 0, length) for axis, length in enumerate(array.shape)]
        where[longest] = (where[longest] + shift) % array.shape[longest]
        spots.append(tuple(where))
    return array.at[spots[0]].set(smallest).at[spots[1]].set(largest)


def steps_of(own_key, dims, pieces, least, high):
    def one(position, blocks):
        draws = jax.random.uniform(jax.random.fold_in(jax.random.fold_in(own_key, 6), position), (blocks,), jnp.float32, least / len(pieces), high / len(pieces))
        return jnp.repeat(jnp.exp(draws), dims[position] // blocks).reshape((-1,) + (1,) * (len(dims) - position - 1))

    level = one(*pieces[0])
    for cut in pieces[1:]:
        level = level * one(*cut)
    return level


def normal_values(key, shape, scale, limit, shards=(), held_as=jnp.bfloat16):
    result = scale * jax.random.normal(key, shape, jnp.float32)
    if shards:
        result = result * steps_of(key, shape, shards, -0.22, 0.18)
    return jnp.clip(result, -limit, limit).astype(held_as)


def setup_inputs(seed: int = 0) -> dict:
    key_list = jax.random.split(jax.random.key(seed), 21)
    return {
        "data_x": normal_values(key_list[0], (N_ROWS, DIN), 1.0, 6.0, ((0, 32),)),
        "data_group": set_ends(jax.random.randint(key_list[1], (N_ROWS,), 0, GROUPS), jax.random.fold_in(key_list[1], 1), 0, GROUPS - 1).astype(jnp.int32),
        "batch_x": normal_values(key_list[2], (BATCH, DIN), 1.0, 6.0, ((0, 32),)),
        "batch_group": set_ends(jax.random.randint(key_list[3], (BATCH,), 0, GROUPS), jax.random.fold_in(key_list[3], 1), 0, GROUPS - 1).astype(jnp.int32),
        "batch_index": set_ends(jax.random.randint(key_list[4], (BATCH,), 0, N_ROWS), jax.random.fold_in(key_list[4], 1), 0, N_ROWS - 1).astype(jnp.int32),
        "prec_index": set_ends(jax.random.randint(key_list[5], (BATCH,), 0, PTABLE), jax.random.fold_in(key_list[5], 1), 0, PTABLE - 1).astype(jnp.int32),
        "prec_table": jnp.clip(jnp.exp(jax.random.uniform(key_list[6], (PTABLE,), jnp.float32, math.log(0.5), math.log(4.0))), 0.5, 4.0),
        "targets": normal_values(key_list[7], (BATCH, SAMPLES), 1.0, 6.0, ((0, 8),), jnp.float32),
        "omega": normal_values(key_list[8], (FEAT, MFEAT), FEAT ** -0.5, 0.125),
        "phase": jnp.clip(jax.random.uniform(key_list[9], (MFEAT,), jnp.float32, -3.140625, 3.140625), -3.140625, 3.140625),
        "prior_w": normal_values(key_list[10], (MFEAT, SAMPLES), 1.0, 6.0, (), jnp.float32),
        "w1_master": normal_values(key_list[11], (DIN, HID), DIN ** -0.5, 0.1875, ((1, 4),), jnp.float32),
        "w1_moment": normal_values(key_list[12], (DIN, HID), (0.011 / (DIN * HID + HID * FEAT) ** 0.5), 6.103515625e-05, ((1, 4),), jnp.float32),
        "w1_second": jnp.clip(jnp.exp(math.log(6.357828759989692e-12) - 1.3862944 * jax.random.uniform(key_list[13], (DIN, HID), jnp.float32) ** steps_of(key_list[13], (DIN, HID), ((1, 4),), -0.2, 0.2)), 1.589457189997423e-12, 6.357828759989692e-12),
        "w2_master": normal_values(key_list[14], (HID, FEAT), HID ** -0.5, 0.125, ((1, 4),), jnp.float32),
        "w2_moment": normal_values(key_list[15], (HID, FEAT), (0.011 / (DIN * HID + HID * FEAT) ** 0.5), 6.103515625e-05, ((1, 4),), jnp.float32),
        "w2_second": jnp.clip(jnp.exp(math.log(6.357828759989692e-12) - 1.3862944 * jax.random.uniform(key_list[16], (HID, FEAT), jnp.float32) ** steps_of(key_list[16], (HID, FEAT), ((1, 4),), -0.2, 0.2)), 1.589457189997423e-12, 6.357828759989692e-12),
        "alpha": normal_values(key_list[17], (N_ROWS, SAMPLES), 0.5, 4.0, ((0, 32),), jnp.float32),
        "alpha_moment": normal_values(key_list[18], (N_ROWS, SAMPLES), (0.0011 / (N_ROWS * SAMPLES) ** 0.5), 4.57763671875e-05, ((0, 32),), jnp.float32),
        "alpha_second": jnp.clip(jnp.exp(math.log(3.051757848163139e-12) - 1.3862944 * jax.random.uniform(key_list[19], (N_ROWS, SAMPLES), jnp.float32) ** steps_of(key_list[19], (N_ROWS, SAMPLES), ((0, 32),), -0.2, 0.2)), 7.629394620407848e-13, 3.051757848163139e-12),
    }


@jax.custom_vjp
def low(v):
    return lax.optimization_barrier(v.astype(jnp.bfloat16)).astype(jnp.float32)

@jax.custom_vjp
def low_back(v):
    return v

def low_keep(v):
    return (low(v), None)

def low_pass(kept, grad):
    return (grad,)

def back_keep(v):
    return (v, None)

def back_low(kept, grad):
    return (low(grad),)
low.defvjp(low_keep, low_pass)
low_back.defvjp(back_keep, back_low)
HIGH = lax.Precision.HIGHEST

def matmul(left, right):
    return jnp.dot(left, right, precision=HIGH, preferred_element_type=jnp.float32)

def feature_map(inputs, w1r, w2r):
    pre_act = low_back(matmul(inputs, w1r))
    hid_act = low(jax.nn.gelu(pre_act))
    return low(low_back(matmul(hid_act, w2r)))

def adamw(weight, grad, moment, second, rate, decay):
    moment_new = 0.9 * moment + 0.1 * grad
    second_new = 0.999 * second + 0.001 * grad * grad
    m_hat = moment_new / (1.0 - 0.9 ** STEP_NUM)
    v_hat = second_new / (1.0 - 0.999 ** STEP_NUM)
    new = weight - rate * (m_hat / (jnp.sqrt(v_hat) + 1e-08) + decay * weight)
    return (moment_new, second_new, new)

def reference(data_x, data_group, batch_x, batch_group, batch_index, prec_index, prec_table, targets, omega, phase, prior_w, w1_master, w1_moment, w1_second, w2_master, w2_moment, w2_second, alpha, alpha_moment, alpha_second):
    xdata = data_x.astype(jnp.float32)
    xbatch = batch_x.astype(jnp.float32)
    omega_f = omega.astype(jnp.float32)
    noise_prec = prec_table[prec_index]
    weight_total = jnp.sum(noise_prec)
    pmask = (0.5 + (batch_group[:, None] == data_group[None, :]).astype(jnp.float32)) / FEAT
    columns = jnp.arange(N_ROWS, dtype=jnp.int32)
    nugget = jnp.where(batch_index[:, None] == columns[None, :], 1.0 / noise_prec[:, None], 0.0)
    scale_rff = math.sqrt(2.0 / MFEAT)

    def forward(w1, w2, alpha_w):
        w1r = low(w1)
        w2r = low(w2)
        data_feat = feature_map(xdata, w1r, w2r)
        batch_feat = feature_map(xbatch, w1r, w2r)
        scores = low_back(matmul(batch_feat, data_feat.T))
        amat = pmask * scores + nugget
        kalpha = matmul(amat, alpha_w)
        zeta = low_back(matmul(batch_feat, omega_f))
        prior = scale_rff * matmul(jnp.cos(zeta + phase[None, :]), prior_w)
        resid = targets - prior - kalpha
        loss_total = 0.5 * jnp.sum(noise_prec * lax.optimization_barrier(jnp.sum(resid * resid, axis=1)))
        return (loss_total / weight_total, loss_total)
    value, pullback = jax.vjp(lambda a, b, c: forward(a, b, c)[0], w1_master, w2_master, alpha)
    loss_total = forward(w1_master, w2_master, alpha)[1]
    w1_grad, w2_grad, alpha_grad = pullback(jnp.ones((), jnp.float32))
    norm_sq = jnp.sum(w1_grad * w1_grad) + jnp.sum(w2_grad * w2_grad) + jnp.sum(alpha_grad * alpha_grad)
    clip = jnp.minimum(1.0, 0.1 / jnp.sqrt(norm_sq))
    w1_mn, w1_sn, w1_new = adamw(w1_master, clip * w1_grad, w1_moment, w1_second, 0.03, 0.01)
    w2_mn, w2_sn, w2_new = adamw(w2_master, clip * w2_grad, w2_moment, w2_second, 0.03, 0.01)
    al_mn, al_sn, al_new = adamw(alpha, clip * alpha_grad, alpha_moment, alpha_second, 0.2, 0.0)
    return (loss_total, weight_total, norm_sq, w1_mn, w1_sn, w1_new, w1_new.astype(jnp.bfloat16), w2_mn, w2_sn, w2_new, w2_new.astype(jnp.bfloat16), al_mn, al_sn, al_new)
```

```python
import math

import jax
import jax.numpy as jnp
from jax import lax
from jax.sharding import PartitionSpec as P

STEP_NUM = 10
HIGH = lax.Precision.HIGHEST
GC = math.sqrt(2.0 / math.pi)


def precise(left, right):
    return jnp.dot(left, right, precision=HIGH, preferred_element_type=jnp.float32)


def mm(left, right):
    return jnp.dot(left, right, preferred_element_type=jnp.float32)


def adamw(weight, grad, moment, second, rate, decay):
    moment_new = 0.9 * moment + 0.1 * grad
    second_new = 0.999 * second + 0.001 * grad * grad
    m_hat = moment_new / (1.0 - 0.9**STEP_NUM)
    v_hat = second_new / (1.0 - 0.999**STEP_NUM)
    new = weight - rate * (m_hat / (jnp.sqrt(v_hat) + 1e-08) + decay * weight)
    return (moment_new, second_new, new)


def gelu_pair(pre):
    t = jnp.tanh(GC * (pre + 0.044715 * pre * pre * pre))
    out = 0.5 * pre * (1.0 + t)
    grad = 0.5 * (1.0 + t) + 0.5 * pre * (1.0 - t * t) * (GC * (1.0 + 3 * 0.044715 * pre * pre))
    return out, grad


def on_device(
    data_x, data_group, batch_x, batch_group, batch_index, prec_index, prec_table, targets,
    omega, phase, prior_w, w1_master, w1_moment, w1_second, w2_master, w2_moment, w2_second,
    alpha, alpha_moment, alpha_second,
):
    bf = jnp.bfloat16
    wide = lax.axis_size("wide")
    narrow = lax.axis_size("narrow")
    wi = lax.axis_index("wide")
    ni = lax.axis_index("narrow")
    feat, mfeat = omega.shape
    w1b, w2b = w1_master.astype(bf), w2_master.astype(bf)
    fown = w2b.shape[1]
    xg = lax.all_gather(data_x, "narrow", axis=0, tiled=True)
    xb = lax.all_gather(batch_x, ("wide", "narrow"), axis=0, tiled=True)
    hits = prec_index[:, None] == jnp.arange(prec_table.shape[0], dtype=jnp.int32)[None, :]
    prec_own = jnp.sum(jnp.where(hits, prec_table[None, :], 0.0), axis=1)
    meta_own = jnp.concatenate(
        [batch_group[:, None].astype(jnp.float32), batch_index[:, None].astype(jnp.float32), prec_own[:, None], targets], axis=1)
    meta = lax.all_gather(meta_own, "wide", axis=0, tiled=True)
    dmeta = lax.all_gather(jnp.concatenate([alpha, data_group[:, None].astype(jnp.float32)], axis=1), "narrow", axis=0, tiled=True)
    alpha_g, group_g = dmeta[:, :-1], dmeta[:, -1]
    bgroup, bindex, prec, targ = meta[:, 0], meta[:, 1], meta[:, 2], meta[:, 3:]
    weight_total = jnp.sum(prec)
    batch = xb.shape[0]
    rows = xg.shape[0]

    pre_b = mm(xb, w1b)
    hb, gb = gelu_pair(pre_b)
    hid_b = lax.all_gather(hb.astype(bf), "narrow", axis=1, tiled=True)
    bfeat = mm(hid_b, w2b).astype(bf)
    om_own = lax.dynamic_slice_in_dim(omega, ni * fown, fown, 0)
    gpart = jnp.einsum("if,hf->ih", bfeat, w2b, preferred_element_type=jnp.float32)
    zpart = mm(bfeat, om_own)
    both = jnp.concatenate([gpart.reshape(batch, narrow, -1), zpart.reshape(batch, narrow, -1)], axis=2)
    both = lax.psum_scatter(both, "narrow", scatter_dimension=1, tiled=True)[:, 0]
    hown = gpart.shape[1] // narrow
    gmat = both[:, :hown].astype(bf)
    mown = mfeat // narrow
    angle = both[:, hown:] + lax.dynamic_slice_in_dim(phase, ni * mown, mown, 0)[None, :]
    pw_own = lax.dynamic_slice_in_dim(prior_w, ni * mown, mown, 0)
    scale_rff = math.sqrt(2.0 / mfeat)

    pre = mm(xg, w1b)
    hd, gd = gelu_pair(pre)
    hid = hd.astype(bf)
    scores = jnp.einsum("ih,jh->ij", gmat, hid, preferred_element_type=jnp.float32)
    pmask = (0.5 + (bgroup[:, None] == group_g[None, :]).astype(jnp.float32)) / feat
    cols = (wi * rows + jnp.arange(rows, dtype=jnp.int32)).astype(jnp.float32)
    nug = jnp.where((bindex[:, None] == cols[None, :]) & (ni == 0), 1.0 / prec[:, None], 0.0)
    amat = pmask * scores + nug
    ksum = lax.psum(precise(amat, alpha_g) + (scale_rff / wide) * precise(jnp.cos(angle), pw_own), ("wide", "narrow"))
    resid = targ - ksum
    loss_sum = 0.5 * jnp.sum(prec * jnp.sum(resid * resid, axis=1))
    gr = prec[:, None] * resid / weight_total
    agrad = lax.psum_scatter(precise(amat.T, -gr), "narrow", scatter_dimension=0, tiled=True)
    dscore = (pmask * precise(-gr, alpha_g.T)).astype(bf)
    dz = (scale_rff * jnp.sin(angle) * precise(gr, pw_own.T)).astype(bf)
    u_own = lax.psum(mm(dscore, hid), "wide").astype(bf)
    uz = lax.all_gather(jnp.stack([u_own, dz]), "narrow", axis=2, tiled=True)
    umat, dzeta = uz[0], uz[1]
    dbatch = (mm(umat, w2b) + jnp.einsum("im,fm->if", dzeta, om_own, preferred_element_type=jnp.float32)).astype(bf)
    dhid_b = lax.psum_scatter(
        jnp.einsum("if,hf->ih", dbatch, w2b, preferred_element_type=jnp.float32), "narrow", scatter_dimension=1, tiled=True)
    dpre_b = (dhid_b * gb).astype(bf)
    w2_grad = jnp.einsum("ih,if->hf", hid_b, dbatch, preferred_element_type=jnp.float32) + jnp.einsum(
        "ih,if->hf", umat, bfeat, preferred_element_type=jnp.float32)
    dhid = jnp.einsum("ij,ih->jh", dscore, gmat, preferred_element_type=jnp.float32)
    dpre = (dhid * gd).astype(bf)
    w1p = jnp.einsum("jd,jh->dh", xg, dpre, preferred_element_type=jnp.float32).astype(bf)
    w1_grad = lax.psum(w1p, "wide").astype(jnp.float32) + jnp.einsum("id,ih->dh", xb, dpre_b, preferred_element_type=jnp.float32)

    local_sq = (jnp.sum(w1_grad * w1_grad) + jnp.sum(w2_grad * w2_grad)) / wide + jnp.sum(agrad * agrad)
    norm_sq = lax.psum(local_sq, ("wide", "narrow"))
    clip = jnp.minimum(1.0, 0.1 / jnp.sqrt(norm_sq))
    w1_mn, w1_sn, w1_new = adamw(w1_master, clip * w1_grad, w1_moment, w1_second, 0.03, 0.01)
    w2_mn, w2_sn, w2_new = adamw(w2_master, clip * w2_grad, w2_moment, w2_second, 0.03, 0.01)
    al_mn, al_sn, al_new = adamw(alpha, clip * agrad, alpha_moment, alpha_second, 0.2, 0.0)
    return (
        loss_sum, weight_total, norm_sq,
        w1_mn, w1_sn, w1_new, w1_new.astype(bf),
        w2_mn, w2_sn, w2_new, w2_new.astype(bf),
        al_mn, al_sn, al_new,
    )


def solution(mesh):
    both = P(("wide", "narrow"))
    both2 = P(("wide", "narrow"), None)
    col = P(None, "narrow")
    return jax.shard_map(
        on_device,
        mesh=mesh,
        in_specs=(both2, both, both2, P("wide"), P("wide"), P("wide"), P(), P("wide", None), P(), P(), P())
        + (col,) * 6 + (both2,) * 3,
        out_specs=(P(), P(), P()) + (col,) * 8 + (both2,) * 3,
        check_vma=False,
    )
```

```python
import math
from types import SimpleNamespace

import jax
import jax.numpy as jnp
from jax import lax
from jax.experimental import pallas as pl
from jax.experimental.pallas import tpu as pltpu
from jax.sharding import PartitionSpec as P

STEP_NUM = 10
HIGH = lax.Precision.HIGHEST
MESH = pl.DeviceIdType.MESH
GC = math.sqrt(2.0 / math.pi)
F32 = jnp.float32
BF = jnp.bfloat16


def adamw(weight, grad, moment, second, rate, decay):
    moment_new = 0.9 * moment + 0.1 * grad
    second_new = 0.999 * second + 0.001 * grad * grad
    m_hat = moment_new / (1.0 - 0.9**STEP_NUM)
    v_hat = second_new / (1.0 - 0.999**STEP_NUM)
    new = weight - rate * (m_hat / (jnp.sqrt(v_hat) + 1e-08) + decay * weight)
    return (moment_new, second_new, new)


def gelu_pair(pre):
    square = pre * pre
    t = jnp.tanh(pre * (GC + (GC * 0.044715) * square))
    half = 0.5 * (1.0 + t)
    slope = half + 0.5 * pre * (1.0 - t * t) * (GC + (3 * GC * 0.044715) * square)
    return pre * half, slope


def dot(left, right, dims=((1,), (0,)), precision=None):
    return lax.dot_general(left, right, (dims, ((), ())), precision=precision, preferred_element_type=F32)


NT = ((1,), (1,))
TN = ((0,), (0,))


class Exchange:
    def __init__(self, axis, size, me, send, recv):
        self.axis, self.size, self.me, self.send, self.recv = axis, size, me, send, recv

    def copy(self, src, dst, p, slot):
        return pltpu.make_async_remote_copy(
            src_ref=src, dst_ref=dst, send_sem=self.send.at[p], recv_sem=self.recv.at[slot],
            device_id={self.axis: p}, device_id_type=MESH)

    def loop(self, body):
        def step(k, carry):
            body(lax.rem(self.me + k, self.size))
            return carry

        lax.fori_loop(1, self.size, step, 0)

    def gather(self, buf):
        self.loop(lambda p: self.copy(buf.at[self.me], buf.at[self.me], p, self.me).start())

    def scatter(self, src, buf):
        self.loop(lambda p: self.copy(src.at[p], buf.at[self.me], p, self.me).start())

    def wait(self, buf):
        self.loop(lambda p: self.copy(buf.at[p], buf.at[p], p, p).wait_recv())

    def drain(self, buf):
        self.loop(lambda p: self.copy(buf.at[p], buf.at[p], p, p).wait_send())


WIDE_EX = ("meta", "xbw", "hgw", "bfw", "gw", "kw", "ur", "uz", "nw")
NARROW_EX = ("xbn", "ad", "hbn", "gzr", "kn", "agr", "uzn", "dhr", "nn")


def step_kernel(W, N, names, *refs):
    r = SimpleNamespace(**dict(zip(names, refs)))
    wi, ni = lax.axis_index("wide"), lax.axis_index("narrow")
    A = W // 2
    a, b = wi // 2, lax.rem(wi, 2)
    pair = wi + 1 - 2 * b
    n1 = ni + 1 - 2 * lax.rem(ni, 2)
    n2 = lax.rem(ni + 2, N)
    n3 = lax.rem(n1 + 2, N)
    xg, hid, gd, xT, dpre = r.xg, r.hid, r.gd, r.xT, r.dpre
    w1b, w2b, om = r.w1b, r.w2b, r.om
    _, R, D = xg.shape
    Bg, S = r.targets.shape
    brow = r.batch_x.shape[0]
    Hn, Fn = w1b.shape[1], w2b.shape[1]
    H, F, M = w2b.shape[0], r.omega.shape[0], r.omega.shape[1]
    Mn = M // N
    B = W * Bg
    half = D // 2
    Ck = half // A
    scale = math.sqrt(2.0 / M)
    lsem = r.lsem
    ex = SimpleNamespace()
    for name in WIDE_EX:
        vars(ex)[name] = Exchange("wide", W, wi, getattr(r, name + "_s"), getattr(r, name + "_r"))
    for name in NARROW_EX:
        vars(ex)[name] = Exchange("narrow", N, ni, getattr(r, name + "_s"), getattr(r, name + "_r"))

    own_f = pl.ds(pl.multiple_of(ni * Fn, Fn), Fn)
    own_m = pl.ds(pl.multiple_of(ni * Mn, Mn), Mn)
    loads = [
        pltpu.make_async_copy(r.w1, r.w1f, lsem.at[0]),
        pltpu.make_async_copy(r.data_x, xg.at[ni], lsem.at[1]),
        pltpu.make_async_copy(r.w2, r.w2f, lsem.at[2]),
        pltpu.make_async_copy(r.omega.at[own_f], om, lsem.at[3]),
        pltpu.make_async_copy(r.prior_wt.at[:, own_m], r.pwt, lsem.at[4]),
    ]
    for load in loads:
        load.start()

    barrier = pltpu.get_barrier_semaphore()

    def greet(axis, size, me):
        def step(k, carry):
            pl.semaphore_signal(barrier, inc=1, device_id={axis: lax.rem(me + k, size)}, device_id_type=MESH)
            return carry

        lax.fori_loop(1, size, step, 0)

    greet("narrow", N, ni)
    greet("wide", W, wi)

    r.xbn[ni] = r.batch_x[...].astype(F32)
    lane = lax.broadcasted_iota(jnp.int32, (1, 128), 1)
    for k in range(Bg):
        prec_k = r.ptable[r.pindex[k]]
        r.meta[wi, k : k + 1, :] = jnp.where(
            lane == 0, r.bgroup[k].astype(F32),
            jnp.where(lane == 1, r.bindex[k].astype(F32), jnp.where(lane == 2, prec_k, 0.0)))
    r.meta[wi, :, S : 2 * S] = r.targets[...]
    r.ad[ni, 0:S, :] = r.alphat_own[...]
    r.ad[ni, S : S + 8, :] = jnp.broadcast_to(r.dgroup[...].astype(F32), (8, R))

    pl.semaphore_wait(barrier, W - 1 + N - 1)

    def xcopy(src, dst, k, p):
        return pltpu.make_async_remote_copy(
            src_ref=src, dst_ref=dst, send_sem=r.x_s.at[k], recv_sem=r.x_r.at[k],
            device_id={"narrow": p}, device_id_type=MESH)

    ex.xbn.gather(r.xbn)
    xcopy(r.data_x, xg.at[ni], 0, n1).start()
    xcopy(r.data_x, xg.at[ni], 1, n2).start()
    ex.meta.gather(r.meta)
    ex.ad.gather(r.ad)

    loads[0].wait()

    def cast1(k, carry):
        rows = pl.ds(pl.multiple_of(k * 128, 128), 128)
        w1b[rows, :] = r.w1f[rows, :].astype(BF)
        return carry

    lax.fori_loop(0, D // 128, cast1, 0)
    ex.xbn.wait(r.xbn)
    for n in range(N):
        r.xbg[n * brow : (n + 1) * brow, :] = r.xbn[n]
    xbg = r.xbg[...]
    hb, gb = gelu_pair(dot(xbg.astype(BF), w1b[...]))
    hb = hb.astype(BF).astype(F32)
    r.hbn[ni] = hb
    ex.hbn.gather(r.hbn)
    r.hgw[wi] = jnp.concatenate([hb, gb], axis=0).astype(BF)
    ex.hgw.gather(r.hgw)
    r.xbw[wi] = jnp.concatenate([xbg[:, : D // 2], xbg[:, D // 2 :]], axis=0).astype(BF)
    ex.xbw.gather(r.xbw)
    loads[2].wait()

    def cast2(k, carry):
        rows = pl.ds(pl.multiple_of(k * 128, 128), 128)
        w2b[rows, :] = r.w2f[rows, :].astype(BF)
        return carry

    lax.fori_loop(0, H // 128, cast2, 0)

    def block(q):
        base = q * R
        r.pre[...] = dot(xg[q], w1b[...])

        def part(k, carry):
            src = pl.ds(pl.multiple_of(k * 32, 32), 32)
            dst = pl.ds(pl.multiple_of(base + k * 32, 32), 32)
            out, slope = gelu_pair(r.pre[src, :])
            hid[dst, :] = out.astype(BF)
            gd[dst, :] = slope
            return carry

        lax.fori_loop(0, R // 32, part, 0)

    def turn(q):
        xT[:, pl.ds(pl.multiple_of(q * R, R), R)] = xg[q].T

    loads[3].wait()
    ex.hbn.wait(r.hbn)
    hid_g = jnp.concatenate([r.hbn[n] for n in range(N)], axis=1).astype(BF)
    bfeat = dot(hid_g, w2b[...]).astype(BF)
    gpart = dot(bfeat, w2b[...], NT)
    zpart = dot(bfeat, om[...])
    for n in range(N):
        r.gzs[n, :, :Hn] = gpart[:, n * Hn : (n + 1) * Hn]
        r.gzs[n, :, Hn:] = zpart[:, n * Mn : (n + 1) * Mn]
    ex.gzr.scatter(r.gzs, r.gzr)
    r.gzr[ni] = r.gzs[ni]
    bf32 = bfeat.astype(F32)
    r.bfw[wi] = jnp.concatenate([bf32[:, : Fn // 2], bf32[:, Fn // 2 :]], axis=0).astype(BF)
    ex.bfw.gather(r.bfw)
    loads[1].wait()
    block(ni)
    ex.gzr.wait(r.gzr)
    gz = jnp.sum(r.gzr[...], axis=0)
    r.gw[wi] = jnp.concatenate([gz[:, : Hn // 2], gz[:, Hn // 2 : Hn]], axis=0).astype(BF)
    ex.gw.gather(r.gw)
    own_b = pl.ds(pl.multiple_of(wi * Bg, Bg), Bg)
    angle = gz[:, Hn:] + r.phase[:, own_m]
    r.cz[...] = jnp.zeros_like(r.cz)
    r.cz[own_b, :] = scale * jnp.cos(angle)
    r.sz[...] = scale * jnp.sin(angle)
    loads[4].wait()
    r.prior[...] = dot(r.pwt[...], r.cz[...], NT, HIGH)

    xcopy(r.data_x, xg.at[n1], 0, n1).wait_recv()
    block(n1)
    xcopy(r.data_x, xg.at[n2], 1, n2).wait_recv()
    xcopy(xg.at[n2], xg.at[n2], 2, n1).start()
    block(n2)
    turn(ni)
    turn(n1)
    ex.meta.wait(r.meta)
    ex.ad.wait(r.ad)
    meta = r.meta[...].reshape(B, 128)
    r.metat[...] = meta.T
    alphat = jnp.concatenate([r.ad[n, 0:S, :] for n in range(N)], axis=1)
    r.alphat[...] = alphat
    group = jnp.concatenate([r.ad[n, S : S + 1, :] for n in range(N)], axis=1)
    pmask = (0.5 + (meta[:, 0:1] == group).astype(F32)) / F
    r.pmask[...] = pmask
    col = lax.broadcasted_iota(jnp.int32, (1, N * R), 1) + wi * (N * R)
    first = (ni == 0).astype(F32)
    r.amat[...] = jnp.where(meta[:, 1:2] == col.astype(F32), first / meta[:, 2:3], 0.0)
    xcopy(r.data_x, xg.at[n3], 2, n1).wait_recv()
    block(n3)

    ex.gw.wait(r.gw)
    gw = r.gw[...].astype(F32)
    gmat = jnp.concatenate([gw[:, :Bg].reshape(B, Hn // 2), gw[:, Bg:].reshape(B, Hn // 2)], axis=1).astype(BF)
    r.gmat[...] = gmat
    amat = r.pmask[...] * dot(gmat, hid[...], NT) + r.amat[...]
    r.amat[...] = amat
    r.kn[ni] = dot(r.alphat[...], amat, NT, HIGH) + r.prior[...]
    ex.kn.gather(r.kn)
    turn(n2)
    turn(n3)
    ex.kn.wait(r.kn)
    r.kw[wi] = jnp.sum(r.kn[...], axis=0)
    ex.kw.gather(r.kw)
    ex.xbw.wait(r.xbw)
    xbw = r.xbw[...].astype(F32)
    r.xbt[...] = jnp.concatenate([xbw[:, :Bg].reshape(B, D // 2), xbw[:, Bg:].reshape(B, D // 2)], axis=1).T.astype(BF)
    ex.kw.wait(r.kw)
    prec = r.metat[2:3, :]
    resid = r.metat[S : 2 * S, :] - jnp.sum(r.kw[...], axis=0)
    total = jnp.sum(prec, axis=1, keepdims=True)
    loss = 0.5 * jnp.sum(jnp.sum(prec * (resid * resid), axis=1, keepdims=True), axis=0, keepdims=True)
    grt = prec * resid / total

    ds = (-r.pmask[...] * dot(grt, r.alphat[...], TN, HIGH)).astype(BF)
    upart = dot(ds, hid[...])
    r.us[...] = upart.reshape(W, Bg, Hn)
    ex.ur.scatter(r.us, r.ur)
    for q in range(N):
        rows = slice(q * R, (q + 1) * R)
        dpre[rows, :] = (dot(ds[:, rows], r.gmat[...], TN) * gd[rows, :]).astype(BF)

    def wcopy(src, dst, kind, k, slot, p):
        return pltpu.make_async_remote_copy(
            src_ref=src, dst_ref=dst, send_sem=getattr(r, kind + "_s").at[k], recv_sem=getattr(r, kind + "_r").at[slot],
            device_id={"wide": p}, device_id_type=MESH)

    psend, precv, zsend, zrecv, gat = r.psend, r.precv, r.zsend, r.zrecv, r.gat

    def grad_rows(row):
        return dot(xT[pl.ds(pl.multiple_of(row, Ck), Ck), :], dpre[...])

    def pair_send(step, carry):
        ap = lax.rem(a + 1 + step, A)
        psend[ap] = grad_rows((1 - b) * half + ap * Ck).astype(BF)
        wcopy(psend.at[ap], precv.at[ap], "p", ap, ap, pair).start()
        return carry

    lax.fori_loop(0, A, pair_send, 0)

    def z_sum(ap):
        v = grad_rows(b * half + ap * Ck)
        wcopy(psend.at[ap], precv.at[ap], "p", ap, ap, pair).wait_recv()
        return v + precv[ap].astype(F32)

    def z_send(step, carry):
        ap = lax.rem(a + 1 + step, A)
        zsend[ap] = z_sum(ap).astype(BF)
        wcopy(zsend.at[ap], zrecv.at[a], "z", ap, a, 2 * ap + b).start()
        return carry

    agt = -dot(grt, r.amat[...], precision=HIGH)
    for n in range(N):
        r.ags[n] = agt[:, n * R : (n + 1) * R]
    ex.agr.scatter(r.ags, r.agr)
    r.agr[ni] = r.ags[ni]
    r.gp[...] = dot(grt, r.pwt[...], TN, HIGH)
    dz = r.sz[...] * r.gp[own_b, :]
    ex.ur.wait(r.ur)
    r.ur[wi] = r.us[wi]
    uown = jnp.sum(r.ur[...], axis=0)
    r.uz[wi] = jnp.concatenate([uown, dz], axis=0).astype(BF)
    ex.uz.gather(r.uz)

    lax.fori_loop(0, 1, z_send, 0)

    ex.hgw.wait(r.hgw)
    ex.bfw.wait(r.bfw)
    ex.uz.wait(r.uz)
    uz, hg = r.uz[...].astype(F32), r.hgw[...].astype(F32)
    r.uzn[ni] = jnp.concatenate(
        [uz[:, :Bg].reshape(B, Hn), uz[:, Bg:].reshape(B, Mn), hg[:, :Bg].reshape(B, Hn)], axis=1).astype(BF)
    ex.uzn.gather(r.uzn)

    lax.fori_loop(1, min(2, A - 1), z_send, 0)

    ex.uzn.wait(r.uzn)
    acc = jnp.zeros((B, Fn), F32)
    for n in range(N):
        acc = acc + dot(r.uzn[n, :, :Hn], w2b[n * Hn : (n + 1) * Hn, :])
        acc = acc + dot(r.uzn[n, :, Hn : Hn + Mn], om[:, n * Mn : (n + 1) * Mn], NT)
    bfw = r.bfw[...].astype(F32)
    bfall = jnp.concatenate([bfw[:, :Bg].reshape(B, Fn // 2), bfw[:, Bg:].reshape(B, Fn // 2)], axis=1)
    r.db[...] = jnp.concatenate([acc, bfall], axis=0).astype(BF)
    for n in range(N):
        r.dhs[n] = dot(r.db[:B, :], w2b[n * Hn : (n + 1) * Hn, :], NT).astype(BF)
    ex.dhr.scatter(r.dhs, r.dhr)
    r.dhr[ni] = r.dhs[ni]

    lax.fori_loop(min(2, A - 1), A - 1, z_send, 0)
    own_row = b * half + a * Ck
    fin = z_sum(a)

    ex.agr.wait(r.agr)
    agt = jnp.sum(r.agr[...], axis=0)
    r.agrad[...] = agt
    ex.dhr.wait(r.dhr)
    dhb = jnp.sum(r.dhr[...].astype(F32), axis=0)
    dpre_b = (dhb * hg[:, Bg:].reshape(B, Hn)).astype(BF)
    fin = fin + dot(r.xbt[pl.ds(pl.multiple_of(own_row, Ck), Ck), :], dpre_b)

    def z_gain(k, total_rows):
        ap = lax.rem(a + k, A)
        wcopy(zsend.at[ap], zrecv.at[ap], "z", ap, ap, 2 * ap + b).wait_recv()
        return total_rows + zrecv[ap].astype(F32)

    fin = lax.fori_loop(1, A, z_gain, fin)
    mine = b * A + a
    gat[mine] = fin.astype(BF)

    def fcopy(slot, k):
        return wcopy(gat.at[slot], gat.at[slot], "f", k, k, pair)

    fcopy(mine, a).start()

    def g_send(k, carry):
        ap = lax.rem(a + k, A)
        wcopy(gat.at[mine], gat.at[mine], "g", ap, a, 2 * ap + b).start()
        return carry

    lax.fori_loop(1, A, g_send, 0)

    def two(v):
        return jnp.sum(jnp.sum(v * v, axis=1, keepdims=True), axis=0, keepdims=True)

    square = jnp.zeros((1, 1), F32)
    for n in range(N):
        hu = jnp.concatenate([r.uzn[n, :, Hn + Mn :], r.uzn[n, :, :Hn]], axis=0)
        g2 = dot(hu, r.db[...], TN)
        r.w2f[n * Hn : (n + 1) * Hn, :] = g2
        square = square + two(g2)
    g2_out = pltpu.make_async_copy(r.w2f, r.g2, lsem.at[2])
    g2_out.start()
    square = square * (1.0 / W) + two(fin) + two(agt)
    r.nn[ni] = jnp.broadcast_to(square, (8, 128))
    ex.nn.gather(r.nn)

    def g_pass(k, carry):
        ap = lax.rem(a + k, A)
        wcopy(gat.at[b * A + ap], gat.at[b * A + ap], "g", ap, ap, 2 * ap + b).wait_recv()
        fcopy(b * A + ap, ap).start()
        return carry

    lax.fori_loop(1, min(2, A), g_pass, 0)
    ex.nn.wait(r.nn)
    r.nw[wi] = jnp.sum(r.nn[...], axis=0)
    ex.nw.gather(r.nw)
    lax.fori_loop(min(2, A), A, g_pass, 0)
    ex.nw.wait(r.nw)
    norm = jnp.sum(r.nw[...], axis=0)
    lanes = lax.broadcasted_iota(jnp.int32, (8, 128), 1)
    r.scal[...] = jnp.where(lanes == 0, loss, jnp.where(lanes == 1, total, norm))

    def g_last(k, carry):
        slot = (1 - b) * A + k
        wcopy(gat.at[slot], gat.at[slot], "f", k, k, pair).wait_recv()
        return carry

    lax.fori_loop(0, A, g_last, 0)
    g1_out = pltpu.make_async_copy(gat, r.g1, lsem.at[0])
    g1_out.start()

    for name in WIDE_EX:
        vars(ex)[name].drain(getattr(r, name))
    for name in NARROW_EX:
        vars(ex)[name].drain(getattr(r, name))
    xcopy(r.data_x, xg.at[ni], 0, n1).wait_send()
    xcopy(r.data_x, xg.at[ni], 1, n2).wait_send()
    xcopy(xg.at[n2], xg.at[n2], 2, n1).wait_send()

    def left(k, carry):
        wcopy(psend.at[k], precv.at[k], "p", k, k, pair).wait_send()
        fcopy(b * A + k, k).wait_send()
        return carry

    def left_z(k, carry):
        ap = lax.rem(a + k, A)
        wcopy(zsend.at[ap], zrecv.at[a], "z", ap, a, 2 * ap + b).wait_send()
        wcopy(gat.at[mine], gat.at[mine], "g", ap, a, 2 * ap + b).wait_send()
        return carry

    lax.fori_loop(0, A, left, 0)
    lax.fori_loop(1, A, left_z, 0)
    g2_out.wait()
    g1_out.wait()


def on_device(
    data_x, data_group, batch_x, batch_group, batch_index, prec_index, prec_table, targets,
    omega, phase, prior_w, w1_master, w1_moment, w1_second, w2_master, w2_moment, w2_second,
    alpha, alpha_moment, alpha_second,
):
    W, N = lax.axis_size("wide"), lax.axis_size("narrow")
    A = W // 2
    R, D = data_x.shape
    brow, Bg, S = batch_x.shape[0], targets.shape[0], targets.shape[1]
    F, M = omega.shape
    Hn, Fn, Mn, H = w1_master.shape[1], w2_master.shape[1], M // N, w2_master.shape[0]
    B, Ck = W * Bg, D // 2 // A
    hbm, vmem, smem = (pl.BlockSpec(memory_space=m) for m in (pl.ANY, pltpu.VMEM, pltpu.SMEM))
    args = dict(
        data_x=(data_x, hbm), dgroup=(data_group.reshape(1, R), vmem), batch_x=(batch_x, vmem),
        bgroup=(batch_group, smem), bindex=(batch_index, smem), pindex=(prec_index, smem),
        ptable=(prec_table, smem), targets=(targets, vmem), omega=(omega, hbm),
        phase=(phase.reshape(1, M), vmem), prior_wt=(prior_w.T, hbm), w1=(w1_master, hbm),
        w2=(w2_master, hbm), alphat_own=(alpha.T, vmem),
    )
    outs = dict(
        scal=((8, 128), F32, vmem), g1=((2 * A, Ck, Hn), BF, hbm), g2=((H, Fn), F32, hbm), agrad=((S, R), F32, vmem),
    )
    scratch = dict(
        xg=((N, R, D), BF), xT=((D, N * R), BF), hid=((N * R, Hn), BF), gd=((N * R, Hn), F32),
        dpre=((N * R, Hn), BF), pre=((R, Hn), F32), w1f=((D, Hn), F32), w1b=((D, Hn), BF),
        w2f=((H, Fn), F32), w2b=((H, Fn), BF), om=((Fn, M), BF), pwt=((S, Mn), F32),
        xbg=((Bg, D), F32), gzs=((N, Bg, Hn + Mn), F32), us=((W, Bg, Hn), F32), ags=((N, S, R), F32),
        dhs=((N, B, Hn), BF), cz=((B, Mn), F32), sz=((Bg, Mn), F32), prior=((S, B), F32), gp=((B, Mn), F32),
        metat=((128, B), F32), alphat=((S, N * R), F32), pmask=((B, N * R), F32), amat=((B, N * R), F32),
        gmat=((B, Hn), BF), xbt=((D, B), BF), db=((2 * B, Fn), BF),
        psend=((A, Ck, Hn), BF), precv=((A, Ck, Hn), BF), zsend=((A, Ck, Hn), BF), zrecv=((A, Ck, Hn), BF),
        gat=((2 * A, Ck, Hn), BF),
        meta=((W, Bg, 128), F32), xbw=((W, 2 * Bg, D // 2), BF), hgw=((W, 2 * Bg, Hn), BF),
        bfw=((W, 2 * Bg, Fn // 2), BF), gw=((W, 2 * Bg, Hn // 2), BF), kw=((W, S, B), F32),
        ur=((W, Bg, Hn), F32), uz=((W, 2 * Bg, Hn), BF), nw=((W, 8, 128), F32),
        xbn=((N, brow, D), F32), ad=((N, S + 8, R), F32), hbn=((N, Bg, Hn), F32), gzr=((N, Bg, Hn + Mn), F32),
        kn=((N, S, B), F32), agr=((N, S, R), F32), uzn=((N, B, 2 * Hn + Mn), BF), dhr=((N, B, Hn), BF),
        nn=((N, 8, 128), F32),
    )
    sems = [("lsem", 5), ("x_s", 3), ("x_r", 3)]
    sems += [(name + end, W) for name in WIDE_EX for end in ("_s", "_r")]
    sems += [(name + end, N) for name in NARROW_EX for end in ("_s", "_r")]
    sems += [(name + end, A) for name in ("p", "z", "g", "f") for end in ("_s", "_r")]
    names = [*args, *outs, *scratch] + [n for n, _ in sems]
    scal, g1, g2, agrad = pl.pallas_call(
        lambda *refs: step_kernel(W, N, names, *refs),
        out_shape=[jax.ShapeDtypeStruct(s, t) for s, t, _ in outs.values()],
        in_specs=[spec for _, spec in args.values()],
        out_specs=[spec for _, _, spec in outs.values()],
        scratch_shapes=[pltpu.VMEM(s, t) for s, t in scratch.values()] + [pltpu.SemaphoreType.DMA((k,)) for _, k in sems],
        compiler_params=pltpu.CompilerParams(collective_id=0, has_side_effects=True, vmem_limit_bytes=56 * 2**20),
        name="gradients",
    )(*[v for v, _ in args.values()])
    loss_sum, weight_total, norm_sq = scal[0, 0], scal[0, 1], scal[0, 2]
    clip = jnp.minimum(1.0, 0.1 / jnp.sqrt(norm_sq))
    w1_grad = g1.reshape(D, Hn).astype(F32)
    w1_mn, w1_sn, w1_new = adamw(w1_master, clip * w1_grad, w1_moment, w1_second, 0.03, 0.01)
    w2_mn, w2_sn, w2_new = adamw(w2_master, clip * g2, w2_moment, w2_second, 0.03, 0.01)
    al_mn, al_sn, al_new = adamw(alpha, clip * agrad.T, alpha_moment, alpha_second, 0.2, 0.0)
    return (
        loss_sum, weight_total, norm_sq,
        w1_mn, w1_sn, w1_new, w1_new.astype(BF),
        w2_mn, w2_sn, w2_new, w2_new.astype(BF),
        al_mn, al_sn, al_new,
    )


def solution(mesh):
    both = P(("wide", "narrow"))
    both2 = P(("wide", "narrow"), None)
    col = P(None, "narrow")
    return jax.shard_map(
        on_device,
        mesh=mesh,
        in_specs=(both2, both, both2, P("wide"), P("wide"), P("wide"), P(), P("wide", None), P(), P(), P())
        + (col,) * 6 + (both2,) * 3,
        out_specs=(P(), P(), P()) + (col,) * 8 + (both2,) * 3,
        check_vma=False,
    )
```

```python
import math
from types import SimpleNamespace

import jax
import jax.numpy as jnp
from jax import lax
from jax.experimental import pallas as pl
from jax.experimental.pallas import tpu as pltpu
from jax.sharding import PartitionSpec as P

STEP_NUM = 10
HIGH = lax.Precision.HIGHEST
MESH = pl.DeviceIdType.MESH
GC = math.sqrt(2.0 / math.pi)
F32 = jnp.float32
BF = jnp.bfloat16


def adamw(weight, grad, moment, second, rate, decay):
    moment_new = 0.9 * moment + 0.1 * grad
    second_new = 0.999 * second + 0.001 * grad * grad
    m_hat = moment_new / (1.0 - 0.9**STEP_NUM)
    v_hat = second_new / (1.0 - 0.999**STEP_NUM)
    new = weight - rate * (m_hat / (jnp.sqrt(v_hat) + 1e-08) + decay * weight)
    return (moment_new, second_new, new)


def gelu_pair(pre):
    square = pre * pre
    t = jnp.tanh(pre * (GC + (GC * 0.044715) * square))
    half = 0.5 * (1.0 + t)
    slope = half + 0.5 * pre * (1.0 - t * t) * (GC + (3 * GC * 0.044715) * square)
    return pre * half, slope


def dot(left, right, dims=((1,), (0,)), precision=None):
    return lax.dot_general(left, right, (dims, ((), ())), precision=precision, preferred_element_type=F32)


NT = ((1,), (1,))
TN = ((0,), (0,))


class Exchange:
    def __init__(self, axis, size, me, send, recv):
        self.axis, self.size, self.me, self.send, self.recv = axis, size, me, send, recv

    def copy(self, src, dst, p, slot):
        return pltpu.make_async_remote_copy(
            src_ref=src, dst_ref=dst, send_sem=self.send.at[p], recv_sem=self.recv.at[slot],
            device_id={self.axis: p}, device_id_type=MESH)

    def loop(self, body):
        def step(k, carry):
            body(lax.rem(self.me + k, self.size))
            return carry

        lax.fori_loop(1, self.size, step, 0)

    def gather(self, buf):
        self.loop(lambda p: self.copy(buf.at[self.me], buf.at[self.me], p, self.me).start())

    def scatter(self, src, buf):
        self.loop(lambda p: self.copy(src.at[p], buf.at[self.me], p, self.me).start())

    def wait(self, buf):
        self.loop(lambda p: self.copy(buf.at[p], buf.at[p], p, p).wait_recv())

    def drain(self, buf):
        self.loop(lambda p: self.copy(buf.at[p], buf.at[p], p, p).wait_send())


WIDE_EX = ("meta", "xbw", "hgw", "bfw", "gw", "kw", "ur", "uz", "nw")
NARROW_EX = ("xbn", "ad", "hbn", "gzr", "kn", "agr", "uzn", "hbx", "dhr", "nn")


def step_kernel(W, N, names, *refs):
    r = SimpleNamespace(**dict(zip(names, refs)))
    wi, ni = lax.axis_index("wide"), lax.axis_index("narrow")
    A = W // 2
    a, b = wi // 2, lax.rem(wi, 2)
    pair = wi + 1 - 2 * b
    n1 = ni + 1 - 2 * lax.rem(ni, 2)
    n2 = lax.rem(ni + 2, N)
    n3 = lax.rem(n1 + 2, N)
    xg, hid, gd, xT, dpre = r.xg, r.hid, r.gd, r.xT, r.dpre
    w1b, w2b, om = r.w1b, r.w2b, r.om
    _, R, D = xg.shape
    Bg, S = r.targets.shape
    brow = r.batch_x.shape[0]
    Hn, Fn = w1b.shape[1], w2b.shape[1]
    H, F, M = w2b.shape[0], r.omega.shape[0], r.omega.shape[1]
    Mn = M // N
    B = W * Bg
    half = D // 2
    Ck = half // A
    scale = math.sqrt(2.0 / M)
    lsem = r.lsem
    ex = SimpleNamespace()
    for name in WIDE_EX:
        vars(ex)[name] = Exchange("wide", W, wi, getattr(r, name + "_s"), getattr(r, name + "_r"))
    for name in NARROW_EX:
        vars(ex)[name] = Exchange("narrow", N, ni, getattr(r, name + "_s"), getattr(r, name + "_r"))

    own_f = pl.ds(pl.multiple_of(ni * Fn, Fn), Fn)
    own_m = pl.ds(pl.multiple_of(ni * Mn, Mn), Mn)
    loads = [
        pltpu.make_async_copy(r.w1, r.w1f, lsem.at[0]),
        pltpu.make_async_copy(r.data_x, xg.at[ni], lsem.at[1]),
        pltpu.make_async_copy(r.w2, r.w2f, lsem.at[2]),
        pltpu.make_async_copy(r.omega.at[own_f], om, lsem.at[3]),
        pltpu.make_async_copy(r.prior_wt.at[:, own_m], r.pwt, lsem.at[4]),
    ]
    for load in loads:
        load.start()

    barrier = pltpu.get_barrier_semaphore()

    def greet(axis, size, me):
        def step(k, carry):
            pl.semaphore_signal(barrier, inc=1, device_id={axis: lax.rem(me + k, size)}, device_id_type=MESH)
            return carry

        lax.fori_loop(1, size, step, 0)

    greet("narrow", N, ni)
    greet("wide", W, wi)

    r.xbn[ni] = r.batch_x[...].astype(F32)
    lane = lax.broadcasted_iota(jnp.int32, (1, 128), 1)
    for k in range(Bg):
        prec_k = r.ptable[r.pindex[k]]
        r.meta[wi, k : k + 1, :] = jnp.where(
            lane == 0, r.bgroup[k].astype(F32),
            jnp.where(lane == 1, r.bindex[k].astype(F32), jnp.where(lane == 2, prec_k, 0.0)))
    r.meta[wi, :, S : 2 * S] = r.targets[...]
    r.ad[ni, 0:S, :] = r.alphat_own[...]
    r.ad[ni, S : S + 8, :] = jnp.broadcast_to(r.dgroup[...].astype(F32), (8, R))

    pl.semaphore_wait(barrier, W - 1 + N - 1)

    def xcopy(src, dst, k, p):
        return pltpu.make_async_remote_copy(
            src_ref=src, dst_ref=dst, send_sem=r.x_s.at[k], recv_sem=r.x_r.at[k],
            device_id={"narrow": p}, device_id_type=MESH)

    cut = R * 5 // 16 // 16 * 16
    cuts = (0, cut, 2 * cut, R)

    def piece(k, src=None, slot=None):
        rows = pl.ds(cuts[k], cuts[k + 1] - cuts[k])
        slot = ni if slot is None else slot
        src = xg.at[slot, rows] if src is None else src.at[rows]
        return src, xg.at[slot, rows]

    def x_side():
        return xcopy(r.data_x, xg.at[ni], 0, n1)

    def x_over(k):
        return xcopy(*piece(k, r.data_x), 1 + k, n2)

    def x_pass(k):
        return xcopy(*piece(k, slot=n2), 4 + k, n1)

    ex.xbn.gather(r.xbn)
    x_over(0).start()
    ex.meta.gather(r.meta)
    ex.ad.gather(r.ad)

    loads[0].wait()

    def cast1(k, carry):
        rows = pl.ds(pl.multiple_of(k * 128, 128), 128)
        w1b[rows, :] = r.w1f[rows, :].astype(BF)
        return carry

    lax.fori_loop(0, D // 128, cast1, 0)
    ex.xbn.wait(r.xbn)
    for n in range(N):
        r.xbg[n * brow : (n + 1) * brow, :] = r.xbn[n]
    xbg = r.xbg[...]
    hb, gb = gelu_pair(dot(xbg.astype(BF), w1b[...]))
    hb = hb.astype(BF).astype(F32)
    r.hbn[ni] = hb
    ex.hbn.gather(r.hbn)
    x_over(1).start()
    x_side().start()
    r.hgw[wi] = jnp.concatenate([hb, gb], axis=0).astype(BF)
    ex.hgw.gather(r.hgw)
    r.xbw[wi] = jnp.concatenate([xbg[:, : D // 2], xbg[:, D // 2 :]], axis=0).astype(BF)
    ex.xbw.gather(r.xbw)
    loads[2].wait()

    def cast2(k, carry):
        rows = pl.ds(pl.multiple_of(k * 128, 128), 128)
        w2b[rows, :] = r.w2f[rows, :].astype(BF)
        return carry

    lax.fori_loop(0, H // 128, cast2, 0)

    def block(q):
        base = q * R
        r.pre[...] = dot(xg[q], w1b[...])

        def part(k, carry):
            src = pl.ds(pl.multiple_of(k * 32, 32), 32)
            dst = pl.ds(pl.multiple_of(base + k * 32, 32), 32)
            out, slope = gelu_pair(r.pre[src, :])
            hid[dst, :] = out.astype(BF)
            gd[dst, :] = slope
            return carry

        lax.fori_loop(0, R // 32, part, 0)

    def turn(q):
        xT[:, pl.ds(pl.multiple_of(q * R, R), R)] = xg[q].T

    loads[3].wait()
    ex.hbn.wait(r.hbn)
    hid_g = jnp.concatenate([r.hbn[n] for n in range(N)], axis=1).astype(BF)
    bfeat = dot(hid_g, w2b[...]).astype(BF)
    gpart = dot(bfeat, w2b[...], NT)
    zpart = dot(bfeat, om[...])
    for n in range(N):
        r.gzs[n, :, :Hn] = gpart[:, n * Hn : (n + 1) * Hn]
        r.gzs[n, :, Hn:] = zpart[:, n * Mn : (n + 1) * Mn]
    ex.gzr.scatter(r.gzs, r.gzr)
    x_over(2).start()
    for k in range(2):
        xcopy(*piece(k, slot=n2), 1 + k, n2).wait_recv()
        x_pass(k).start()
    r.gzr[ni] = r.gzs[ni]
    bf32 = bfeat.astype(F32)
    r.bfw[wi] = jnp.concatenate([bf32[:, : Fn // 2], bf32[:, Fn // 2 :]], axis=0).astype(BF)
    ex.bfw.gather(r.bfw)
    loads[1].wait()
    block(ni)
    ex.gzr.wait(r.gzr)
    gz = jnp.sum(r.gzr[...], axis=0)
    r.gw[wi] = jnp.concatenate([gz[:, : Hn // 2], gz[:, Hn // 2 : Hn]], axis=0).astype(BF)
    ex.gw.gather(r.gw)
    own_b = pl.ds(pl.multiple_of(wi * Bg, Bg), Bg)
    angle = gz[:, Hn:] + r.phase[:, own_m]
    r.cz[...] = jnp.zeros_like(r.cz)
    r.cz[own_b, :] = scale * jnp.cos(angle)
    r.sz[...] = scale * jnp.sin(angle)
    loads[4].wait()
    r.prior[...] = dot(r.pwt[...], r.cz[...], NT, HIGH)

    xcopy(r.data_x, xg.at[n1], 0, n1).wait_recv()
    block(n1)
    turn(ni)
    turn(n1)
    ex.meta.wait(r.meta)
    ex.ad.wait(r.ad)
    meta = r.meta[...].reshape(B, 128)
    r.metat[...] = meta.T
    alphat = jnp.concatenate([r.ad[n, 0:S, :] for n in range(N)], axis=1)
    r.alphat[...] = alphat
    group = jnp.concatenate([r.ad[n, S : S + 1, :] for n in range(N)], axis=1)
    pmask = (0.5 + (meta[:, 0:1] == group).astype(F32)) / F
    r.pmask[...] = pmask
    col = lax.broadcasted_iota(jnp.int32, (1, N * R), 1) + wi * (N * R)
    first = (ni == 0).astype(F32)
    r.amat[...] = jnp.where(meta[:, 1:2] == col.astype(F32), first / meta[:, 2:3], 0.0)
    xcopy(*piece(2, slot=n2), 3, n2).wait_recv()
    x_pass(2).start()
    block(n2)
    for k in range(3):
        xcopy(*piece(k, slot=n3), 4 + k, n1).wait_recv()
    block(n3)

    ex.gw.wait(r.gw)
    gw = r.gw[...].astype(F32)
    gmat = jnp.concatenate([gw[:, :Bg].reshape(B, Hn // 2), gw[:, Bg:].reshape(B, Hn // 2)], axis=1).astype(BF)
    r.gmat[...] = gmat
    amat = r.pmask[...] * dot(gmat, hid[...], NT) + r.amat[...]
    r.amat[...] = amat
    r.kn[ni] = dot(r.alphat[...], amat, NT, HIGH) + r.prior[...]
    ex.kn.gather(r.kn)
    turn(n2)
    turn(n3)
    ex.kn.wait(r.kn)
    r.kw[wi] = jnp.sum(r.kn[...], axis=0)
    ex.kw.gather(r.kw)
    ex.hgw.wait(r.hgw)
    hg = r.hgw[...].astype(F32)
    r.hbx[ni] = hg[:, :Bg].reshape(B, Hn).astype(BF)
    r.gb[...] = hg[:, Bg:].reshape(B, Hn)
    ex.hbx.gather(r.hbx)
    ex.xbw.wait(r.xbw)
    xbw = r.xbw[...].astype(F32)
    r.xbt[...] = jnp.concatenate([xbw[:, :Bg].reshape(B, D // 2), xbw[:, Bg:].reshape(B, D // 2)], axis=1).T.astype(BF)
    ex.kw.wait(r.kw)
    prec = r.metat[2:3, :]
    resid = r.metat[S : 2 * S, :] - jnp.sum(r.kw[...], axis=0)
    total = jnp.sum(prec, axis=1, keepdims=True)
    loss = 0.5 * jnp.sum(jnp.sum(prec * (resid * resid), axis=1, keepdims=True), axis=0, keepdims=True)
    grt = prec * resid / total

    ds = (-r.pmask[...] * dot(grt, r.alphat[...], TN, HIGH)).astype(BF)
    r.us[...] = dot(ds, hid[...]).reshape(W, Bg, Hn)
    ex.ur.scatter(r.us, r.ur)
    for q in range(N):
        rows = slice(q * R, (q + 1) * R)
        dpre[rows, :] = (dot(ds[:, rows], r.gmat[...], TN) * gd[rows, :]).astype(BF)

    def wcopy(src, dst, kind, k, slot, p):
        return pltpu.make_async_remote_copy(
            src_ref=src, dst_ref=dst, send_sem=getattr(r, kind + "_s").at[k], recv_sem=getattr(r, kind + "_r").at[slot],
            device_id={"wide": p}, device_id_type=MESH)

    psend, precv, zsend, zrecv, gat = r.psend, r.precv, r.zsend, r.zrecv, r.gat

    def grad_rows(row):
        return dot(xT[pl.ds(pl.multiple_of(row, Ck), Ck), :], dpre[...])

    def target(step):
        off = lax.rem(A // 2 + step - 1, max(A - 1, 1)) + 1
        return lax.rem(a + off + lax.rem(a, 2) * (A - 2 * off), A)

    def pair_chunk(ap):
        psend[ap] = grad_rows((1 - b) * half + ap * Ck).astype(BF)
        wcopy(psend.at[ap], precv.at[ap], "p", ap, ap, pair).start()

    def pair_send(step, carry):
        pair_chunk(target(step))
        return carry

    def z_sum(ap):
        v = grad_rows(b * half + ap * Ck)
        wcopy(psend.at[ap], precv.at[ap], "p", ap, ap, pair).wait_recv()
        return v + precv[ap].astype(F32)

    def z_send(step, carry):
        ap = target(step)
        zsend[ap] = z_sum(ap).astype(BF)
        wcopy(zsend.at[ap], zrecv.at[a], "z", ap, a, 2 * ap + b).start()
        return carry

    lax.fori_loop(0, min(1, A - 1), pair_send, 0)

    agt = -dot(grt, r.amat[...], precision=HIGH)
    for n in range(N):
        r.ags[n] = agt[:, n * R : (n + 1) * R]
    ex.agr.scatter(r.ags, r.agr)
    r.agr[ni] = r.ags[ni]
    r.gp[...] = dot(grt, r.pwt[...], TN, HIGH)
    dz = r.sz[...] * r.gp[own_b, :]
    ex.ur.wait(r.ur)
    r.ur[wi] = r.us[wi]
    uown = jnp.sum(r.ur[...], axis=0)
    r.uz[wi] = jnp.concatenate([uown, dz], axis=0).astype(BF)
    ex.uz.gather(r.uz)
    lax.fori_loop(min(1, A - 1), A - 1, pair_send, 0)
    pair_chunk(a)

    lax.fori_loop(0, min(1, A - 1), z_send, 0)

    ex.bfw.wait(r.bfw)
    ex.uz.wait(r.uz)
    uz = r.uz[...].astype(F32)
    r.uzn[ni] = jnp.concatenate([uz[:, :Bg].reshape(B, Hn), uz[:, Bg:].reshape(B, Mn)], axis=1).astype(BF)
    ex.uzn.gather(r.uzn)

    lax.fori_loop(min(1, A - 1), A - 1, z_send, 0)
    fin = z_sum(a)

    ex.uzn.wait(r.uzn)
    acc = jnp.zeros((B, Fn), F32)
    for n in range(N):
        acc = acc + dot(r.uzn[n, :, :Hn], w2b[n * Hn : (n + 1) * Hn, :])
        acc = acc + dot(r.uzn[n, :, Hn:], om[:, n * Mn : (n + 1) * Mn], NT)
    bfw = r.bfw[...].astype(F32)
    bfall = jnp.concatenate([bfw[:, :Bg].reshape(B, Fn // 2), bfw[:, Bg:].reshape(B, Fn // 2)], axis=1)
    r.db[...] = jnp.concatenate([acc, bfall], axis=0).astype(BF)
    for n in range(N):
        r.dhs[n] = dot(r.db[:B, :], w2b[n * Hn : (n + 1) * Hn, :], NT).astype(BF)
    ex.dhr.scatter(r.dhs, r.dhr)
    r.dhr[ni] = r.dhs[ni]

    def z_gain(k, total_rows):
        ap = lax.rem(a + k, A)
        wcopy(zsend.at[ap], zrecv.at[ap], "z", ap, ap, 2 * ap + b).wait_recv()
        return total_rows + zrecv[ap].astype(F32)

    fin = lax.fori_loop(1, A, z_gain, fin)
    mine = b * A + a
    gat[mine] = fin.astype(BF)

    def fcopy(ap, side):
        slot = side * A + ap
        return wcopy(gat.at[slot], gat.at[slot], "f", ap, ap, pair)

    def gcopy(ap, way):
        slot = b * A + ap
        k = ap if way > 0 else A + ap
        return wcopy(gat.at[slot], gat.at[slot], "g", k, k, 2 * (a + way) + b)

    fcopy(a, b).start()

    @pl.when(a + 1 < A)
    def _():
        gcopy(a, 1).start()

    @pl.when(a > 0)
    def _():
        gcopy(a, -1).start()

    def g_pass(step, carry):
        below, above = a - 1 - step, a + 1 + step

        @pl.when(below >= 0)
        def _():
            gcopy(below, 1).wait_recv()

            @pl.when(a + 1 < A)
            def _():
                gcopy(below, 1).start()

            fcopy(below, b).start()

        @pl.when(above < A)
        def _():
            gcopy(above, -1).wait_recv()

            @pl.when(a > 0)
            def _():
                gcopy(above, -1).start()

            fcopy(above, b).start()

        return carry

    def two(v):
        return jnp.sum(jnp.sum(v * v, axis=1, keepdims=True), axis=0, keepdims=True)

    square = jnp.zeros((1, 1), F32)
    for n in range(N):
        if n == 0:
            ex.hbx.wait(r.hbx)
        hu = jnp.concatenate([r.hbx[n], r.uzn[n, :, :Hn]], axis=0)
        g2 = dot(hu, r.db[...], TN)
        r.w2f[n * Hn : (n + 1) * Hn, :] = g2
        square = square + two(g2)
    g2_out = pltpu.make_async_copy(r.w2f, r.g2, lsem.at[2])
    g2_out.start()

    ex.agr.wait(r.agr)
    agt = jnp.sum(r.agr[...], axis=0)
    r.agrad[...] = agt
    ex.dhr.wait(r.dhr)
    r.dpb[...] = (jnp.sum(r.dhr[...].astype(F32), axis=0) * r.gb[...]).astype(BF)

    def batch_part(slot):
        return dot(r.xbt[pl.ds(pl.multiple_of(slot * Ck, Ck), Ck), :], r.dpb[...])

    square = square * (1.0 / W) + two(fin + batch_part(mine)) + two(agt)
    r.nn[ni] = jnp.broadcast_to(square, (8, 128))
    ex.nn.gather(r.nn)
    lax.fori_loop(0, min(1, A - 1), g_pass, 0)
    ex.nn.wait(r.nn)
    r.nw[wi] = jnp.sum(r.nn[...], axis=0)
    ex.nw.gather(r.nw)
    lax.fori_loop(min(1, A - 1), A - 1, g_pass, 0)

    def finish(slot):
        r.w1f[pl.ds(pl.multiple_of(slot * Ck, Ck), Ck), :] = gat[slot].astype(F32) + batch_part(slot)

    def own_side(k, carry):
        finish(b * A + k)
        return carry

    lax.fori_loop(0, A, own_side, 0)
    ex.nw.wait(r.nw)
    norm = jnp.sum(r.nw[...], axis=0)
    lanes = lax.broadcasted_iota(jnp.int32, (8, 128), 1)
    r.scal[...] = jnp.where(lanes == 0, loss, jnp.where(lanes == 1, total, norm))

    def g_last(k, carry):
        ap = lax.rem(a + k, A)
        fcopy(ap, 1 - b).wait_recv()
        finish((1 - b) * A + ap)
        return carry

    lax.fori_loop(0, A, g_last, 0)
    g1_out = pltpu.make_async_copy(r.w1f, r.g1, lsem.at[0])
    g1_out.start()

    for name in WIDE_EX:
        vars(ex)[name].drain(getattr(r, name))
    for name in NARROW_EX:
        vars(ex)[name].drain(getattr(r, name))
    x_side().wait_send()
    for k in range(3):
        x_over(k).wait_send()
        x_pass(k).wait_send()

    def left(k, carry):
        wcopy(psend.at[k], precv.at[k], "p", k, k, pair).wait_send()
        fcopy(k, b).wait_send()

        @pl.when((k <= a) & (a + 1 < A))
        def _():
            gcopy(k, 1).wait_send()

        @pl.when((k >= a) & (a > 0))
        def _():
            gcopy(k, -1).wait_send()

        return carry

    def left_z(k, carry):
        ap = lax.rem(a + k, A)
        wcopy(zsend.at[ap], zrecv.at[a], "z", ap, a, 2 * ap + b).wait_send()
        return carry

    lax.fori_loop(0, A, left, 0)
    lax.fori_loop(1, A, left_z, 0)
    g2_out.wait()
    g1_out.wait()


def on_device(
    data_x, data_group, batch_x, batch_group, batch_index, prec_index, prec_table, targets,
    omega, phase, prior_w, w1_master, w1_moment, w1_second, w2_master, w2_moment, w2_second,
    alpha, alpha_moment, alpha_second,
):
    W, N = lax.axis_size("wide"), lax.axis_size("narrow")
    A = W // 2
    R, D = data_x.shape
    brow, Bg, S = batch_x.shape[0], targets.shape[0], targets.shape[1]
    F, M = omega.shape
    Hn, Fn, Mn, H = w1_master.shape[1], w2_master.shape[1], M // N, w2_master.shape[0]
    B, Ck = W * Bg, D // 2 // A
    hbm, vmem, smem = (pl.BlockSpec(memory_space=m) for m in (pl.ANY, pltpu.VMEM, pltpu.SMEM))
    args = dict(
        data_x=(data_x, hbm), dgroup=(data_group.reshape(1, R), vmem), batch_x=(batch_x, vmem),
        bgroup=(batch_group, smem), bindex=(batch_index, smem), pindex=(prec_index, smem),
        ptable=(prec_table, smem), targets=(targets, vmem), omega=(omega, hbm),
        phase=(phase.reshape(1, M), vmem), prior_wt=(prior_w.T, hbm), w1=(w1_master, hbm),
        w2=(w2_master, hbm), alphat_own=(alpha.T, vmem),
    )
    outs = dict(
        scal=((8, 128), F32, vmem), g1=((D, Hn), F32, hbm), g2=((H, Fn), F32, hbm), agrad=((S, R), F32, vmem),
    )
    scratch = dict(
        xg=((N, R, D), BF), xT=((D, N * R), BF), hid=((N * R, Hn), BF), gd=((N * R, Hn), F32),
        dpre=((N * R, Hn), BF), pre=((R, Hn), F32), w1f=((D, Hn), F32), w1b=((D, Hn), BF),
        w2f=((H, Fn), F32), w2b=((H, Fn), BF), om=((Fn, M), BF), pwt=((S, Mn), F32),
        xbg=((Bg, D), F32), gzs=((N, Bg, Hn + Mn), F32), us=((W, Bg, Hn), F32), ags=((N, S, R), F32),
        dhs=((N, B, Hn), BF), cz=((B, Mn), F32), sz=((Bg, Mn), F32), prior=((S, B), F32), gp=((B, Mn), F32),
        metat=((128, B), F32), alphat=((S, N * R), F32), pmask=((B, N * R), F32), amat=((B, N * R), F32),
        gmat=((B, Hn), BF), xbt=((D, B), BF), db=((2 * B, Fn), BF),
        psend=((A, Ck, Hn), BF), precv=((A, Ck, Hn), BF), zsend=((A, Ck, Hn), BF), zrecv=((A, Ck, Hn), BF),
        gat=((2 * A, Ck, Hn), BF), dpb=((B, Hn), BF), gb=((B, Hn), F32),
        meta=((W, Bg, 128), F32), xbw=((W, 2 * Bg, D // 2), BF), hgw=((W, 2 * Bg, Hn), BF),
        bfw=((W, 2 * Bg, Fn // 2), BF), gw=((W, 2 * Bg, Hn // 2), BF), kw=((W, S, B), F32),
        ur=((W, Bg, Hn), F32), uz=((W, 2 * Bg, Hn), BF), nw=((W, 8, 128), F32),
        xbn=((N, brow, D), F32), ad=((N, S + 8, R), F32), hbn=((N, Bg, Hn), F32), gzr=((N, Bg, Hn + Mn), F32),
        kn=((N, S, B), F32), agr=((N, S, R), F32), uzn=((N, B, Hn + Mn), BF), hbx=((N, B, Hn), BF), dhr=((N, B, Hn), BF),
        nn=((N, 8, 128), F32),
    )
    sems = [("lsem", 5), ("x_s", 7), ("x_r", 7)]
    sems += [(name + end, W) for name in WIDE_EX for end in ("_s", "_r")]
    sems += [(name + end, N) for name in NARROW_EX for end in ("_s", "_r")]
    sems += [(name + end, A) for name in ("p", "z", "f") for end in ("_s", "_r")]
    sems += [("g_s", 2 * A), ("g_r", 2 * A)]
    names = [*args, *outs, *scratch] + [n for n, _ in sems]
    scal, g1, g2, agrad = pl.pallas_call(
        lambda *refs: step_kernel(W, N, names, *refs),
        out_shape=[jax.ShapeDtypeStruct(s, t) for s, t, _ in outs.values()],
        in_specs=[spec for _, spec in args.values()],
        out_specs=[spec for _, _, spec in outs.values()],
        scratch_shapes=[pltpu.VMEM(s, t) for s, t in scratch.values()] + [pltpu.SemaphoreType.DMA((k,)) for _, k in sems],
        compiler_params=pltpu.CompilerParams(collective_id=0, has_side_effects=True, vmem_limit_bytes=56 * 2**20),
        name="gradients",
    )(*[v for v, _ in args.values()])
    loss_sum, weight_total, norm_sq = scal[0, 0], scal[0, 1], scal[0, 2]
    clip = jnp.minimum(1.0, 0.1 / jnp.sqrt(norm_sq))
    w1_mn, w1_sn, w1_new = adamw(w1_master, clip * g1, w1_moment, w1_second, 0.03, 0.01)
    w2_mn, w2_sn, w2_new = adamw(w2_master, clip * g2, w2_moment, w2_second, 0.03, 0.01)
    al_mn, al_sn, al_new = adamw(alpha, clip * agrad.T, alpha_moment, alpha_second, 0.2, 0.0)
    return (
        loss_sum, weight_total, norm_sq,
        w1_mn, w1_sn, w1_new, w1_new.astype(BF),
        w2_mn, w2_sn, w2_new, w2_new.astype(BF),
        al_mn, al_sn, al_new,
    )


def solution(mesh):
    both = P(("wide", "narrow"))
    both2 = P(("wide", "narrow"), None)
    col = P(None, "narrow")
    return jax.shard_map(
        on_device,
        mesh=mesh,
        in_specs=(both2, both, both2, P("wide"), P("wide"), P("wide"), P(), P("wide", None), P(), P(), P())
        + (col,) * 6 + (both2,) * 3,
        out_specs=(P(), P(), P()) + (col,) * 8 + (both2,) * 3,
        check_vma=False,
    )
```

```python
import math
from types import SimpleNamespace

import jax
import jax.numpy as jnp
from jax import lax
from jax.experimental import pallas as pl
from jax.experimental.pallas import tpu as pltpu
from jax.sharding import PartitionSpec as P

STEP_NUM = 10
HIGH = lax.Precision.HIGHEST
MESH = pl.DeviceIdType.MESH
GC = math.sqrt(2.0 / math.pi)
F32 = jnp.float32
BF = jnp.bfloat16


def gelu_pair(pre):
    square = pre * pre
    t = jnp.tanh(pre * (GC + (GC * 0.044715) * square))
    half = 0.5 * (1.0 + t)
    slope = half + 0.5 * pre * (1.0 - t * t) * (GC + (3 * GC * 0.044715) * square)
    return pre * half, slope


def dot(left, right, dims=((1,), (0,)), precision=None):
    return lax.dot_general(left, right, (dims, ((), ())), precision=precision, preferred_element_type=F32)


NT = ((1,), (1,))
TN = ((0,), (0,))


class Exchange:
    def __init__(self, axis, size, me, send, recv):
        self.axis, self.size, self.me, self.send, self.recv = axis, size, me, send, recv

    def copy(self, src, dst, p, slot):
        return pltpu.make_async_remote_copy(
            src_ref=src, dst_ref=dst, send_sem=self.send.at[p], recv_sem=self.recv.at[slot],
            device_id={self.axis: p}, device_id_type=MESH)

    def loop(self, body):
        def step(k, carry):
            body(lax.rem(self.me + k, self.size))
            return carry

        lax.fori_loop(1, self.size, step, 0)

    def gather(self, buf):
        self.loop(lambda p: self.copy(buf.at[self.me], buf.at[self.me], p, self.me).start())

    def scatter(self, src, buf):
        self.loop(lambda p: self.copy(src.at[p], buf.at[self.me], p, self.me).start())

    def wait(self, buf):
        self.loop(lambda p: self.copy(buf.at[p], buf.at[p], p, p).wait_recv())

    def drain(self, buf):
        self.loop(lambda p: self.copy(buf.at[p], buf.at[p], p, p).wait_send())


WIDE_EX = ("meta", "xbw", "hgw", "bfw", "gw", "kw", "ur", "uz", "nw")
NARROW_EX = ("xbn", "ad", "hbn", "gzr", "kn", "agr", "uzn", "hbx", "dhr", "nn")


def step_kernel(W, N, resident, names, *refs):
    r = SimpleNamespace(**dict(zip(names, refs)))
    wi, ni = lax.axis_index("wide"), lax.axis_index("narrow")
    A = W // 2
    a, b = wi // 2, lax.rem(wi, 2)
    pair = wi + 1 - 2 * b
    n1 = ni + 1 - 2 * lax.rem(ni, 2)
    n2 = lax.rem(ni + 2, N)
    n3 = lax.rem(n1 + 2, N)
    xg, hid, gd, xT, dpre = r.xg, r.hid, r.gd, r.xT, r.dpre
    w1b, w2b, om = r.w1b, r.w2b, r.om
    _, R, D = xg.shape
    Bg, S = r.targets.shape
    brow = r.batch_x.shape[0]
    Hn, Fn = w1b.shape[1], w2b.shape[1]
    H, F, M = w2b.shape[0], r.omega.shape[0], r.omega.shape[1]
    Mn = M // N
    B = W * Bg
    half = D // 2
    Ck = half // A
    scale = math.sqrt(2.0 / M)
    lsem = r.lsem
    ex = SimpleNamespace()
    for name in WIDE_EX:
        vars(ex)[name] = Exchange("wide", W, wi, getattr(r, name + "_s"), getattr(r, name + "_r"))
    for name in NARROW_EX:
        vars(ex)[name] = Exchange("narrow", N, ni, getattr(r, name + "_s"), getattr(r, name + "_r"))

    own_f = pl.ds(pl.multiple_of(ni * Fn, Fn), Fn)
    own_m = pl.ds(pl.multiple_of(ni * Mn, Mn), Mn)
    loads = [
        pltpu.make_async_copy(r.w1, r.w1f, lsem.at[0]),
        pltpu.make_async_copy(r.data_x, xg.at[ni], lsem.at[1]),
        pltpu.make_async_copy(r.w2, r.w2f, lsem.at[2]),
        pltpu.make_async_copy(r.omega.at[own_f], om, lsem.at[3]),
        pltpu.make_async_copy(r.prior_wt.at[:, own_m], r.pwt, lsem.at[4]),
    ]
    for load in loads:
        load.start()

    barrier = pltpu.get_barrier_semaphore()

    def greet(axis, size, me):
        def step(k, carry):
            pl.semaphore_signal(barrier, inc=1, device_id={axis: lax.rem(me + k, size)}, device_id_type=MESH)
            return carry

        lax.fori_loop(1, size, step, 0)

    greet("narrow", N, ni)
    greet("wide", W, wi)

    r.xbn[ni] = r.batch_x[...].astype(F32)
    lane = lax.broadcasted_iota(jnp.int32, (1, 128), 1)
    for k in range(Bg):
        prec_k = r.ptable[r.pindex[k]]
        r.meta[wi, k : k + 1, :] = jnp.where(
            lane == 0, r.bgroup[k].astype(F32),
            jnp.where(lane == 1, r.bindex[k].astype(F32), jnp.where(lane == 2, prec_k, 0.0)))
    r.meta[wi, :, S : 2 * S] = r.targets[...]
    r.ad[ni, 0:S, :] = r.alphat_own[...]
    r.ad[ni, S : S + 8, :] = jnp.broadcast_to(r.dgroup[...].astype(F32), (8, R))

    pl.semaphore_wait(barrier, W - 1 + N - 1)

    def xcopy(src, dst, k, p):
        return pltpu.make_async_remote_copy(
            src_ref=src, dst_ref=dst, send_sem=r.x_s.at[k], recv_sem=r.x_r.at[k],
            device_id={"narrow": p}, device_id_type=MESH)

    cut = R * 5 // 16 // 16 * 16
    cuts = (0, cut, 2 * cut, R)

    def piece(k, src=None, slot=None):
        rows = pl.ds(cuts[k], cuts[k + 1] - cuts[k])
        slot = ni if slot is None else slot
        src = xg.at[slot, rows] if src is None else src.at[rows]
        return src, xg.at[slot, rows]

    def x_side():
        return xcopy(r.data_x, xg.at[ni], 0, n1)

    def x_over(k):
        return xcopy(*piece(k, r.data_x), 1 + k, n2)

    def x_pass(k):
        return xcopy(*piece(k, slot=n2), 4 + k, n1)

    ex.xbn.gather(r.xbn)
    x_over(0).start()
    ex.meta.gather(r.meta)
    ex.ad.gather(r.ad)

    loads[0].wait()

    def cast1(k, carry):
        rows = pl.ds(pl.multiple_of(k * 128, 128), 128)
        w1b[rows, :] = r.w1f[rows, :].astype(BF)
        return carry

    lax.fori_loop(0, D // 128, cast1, 0)
    ex.xbn.wait(r.xbn)
    for n in range(N):
        r.xbg[n * brow : (n + 1) * brow, :] = r.xbn[n]
    xbg = r.xbg[...]
    hb, gb = gelu_pair(dot(xbg.astype(BF), w1b[...]))
    hb = hb.astype(BF).astype(F32)
    r.hbn[ni] = hb
    ex.hbn.gather(r.hbn)
    x_over(1).start()
    x_side().start()
    r.hgw[wi] = jnp.concatenate([hb, gb], axis=0).astype(BF)
    ex.hgw.gather(r.hgw)
    r.xbw[wi] = jnp.concatenate([xbg[:, : D // 2], xbg[:, D // 2 :]], axis=0).astype(BF)
    ex.xbw.gather(r.xbw)
    loads[2].wait()

    def cast2(k, carry):
        rows = pl.ds(pl.multiple_of(k * 128, 128), 128)
        w2b[rows, :] = r.w2f[rows, :].astype(BF)
        return carry

    lax.fori_loop(0, H // 128, cast2, 0)

    def block(q):
        base = q * R
        r.pre[...] = dot(xg[q], w1b[...])

        def part(k, carry):
            src = pl.ds(pl.multiple_of(k * 32, 32), 32)
            dst = pl.ds(pl.multiple_of(base + k * 32, 32), 32)
            out, slope = gelu_pair(r.pre[src, :])
            hid[dst, :] = out.astype(BF)
            gd[dst, :] = slope
            return carry

        lax.fori_loop(0, R // 32, part, 0)

    def turn(q):
        xT[:, pl.ds(pl.multiple_of(q * R, R), R)] = xg[q].T

    loads[3].wait()
    ex.hbn.wait(r.hbn)
    hid_g = jnp.concatenate([r.hbn[n] for n in range(N)], axis=1).astype(BF)
    bfeat = dot(hid_g, w2b[...]).astype(BF)
    gpart = dot(bfeat, w2b[...], NT)
    zpart = dot(bfeat, om[...])
    for n in range(N):
        r.gzs[n, :, :Hn] = gpart[:, n * Hn : (n + 1) * Hn]
        r.gzs[n, :, Hn:] = zpart[:, n * Mn : (n + 1) * Mn]
    ex.gzr.scatter(r.gzs, r.gzr)
    x_over(2).start()
    later = []
    if resident:
        pairs = ((r.w1_m, r.m1), (r.w1_v, r.v1), (r.w2_m, r.m2), (r.w2_v, r.v2))
        later = [pltpu.make_async_copy(src, dst, lsem.at[5 + k]) for k, (src, dst) in enumerate(pairs)]
    for load in later:
        load.start()
    for k in range(2):
        xcopy(*piece(k, slot=n2), 1 + k, n2).wait_recv()
        x_pass(k).start()
    r.gzr[ni] = r.gzs[ni]
    bf32 = bfeat.astype(F32)
    r.bfw[wi] = jnp.concatenate([bf32[:, : Fn // 2], bf32[:, Fn // 2 :]], axis=0).astype(BF)
    ex.bfw.gather(r.bfw)
    loads[1].wait()
    block(ni)
    ex.gzr.wait(r.gzr)
    gz = jnp.sum(r.gzr[...], axis=0)
    r.gw[wi] = jnp.concatenate([gz[:, : Hn // 2], gz[:, Hn // 2 : Hn]], axis=0).astype(BF)
    ex.gw.gather(r.gw)
    own_b = pl.ds(pl.multiple_of(wi * Bg, Bg), Bg)
    angle = gz[:, Hn:] + r.phase[:, own_m]
    r.cz[...] = jnp.zeros_like(r.cz)
    r.cz[own_b, :] = scale * jnp.cos(angle)
    r.sz[...] = scale * jnp.sin(angle)
    loads[4].wait()
    r.prior[...] = dot(r.pwt[...], r.cz[...], NT, HIGH)

    xcopy(r.data_x, xg.at[n1], 0, n1).wait_recv()
    block(n1)
    turn(ni)
    turn(n1)
    ex.meta.wait(r.meta)
    ex.ad.wait(r.ad)
    meta = r.meta[...].reshape(B, 128)
    r.metat[...] = meta.T
    alphat = jnp.concatenate([r.ad[n, 0:S, :] for n in range(N)], axis=1)
    r.alphat[...] = alphat
    group = jnp.concatenate([r.ad[n, S : S + 1, :] for n in range(N)], axis=1)
    pmask = (0.5 + (meta[:, 0:1] == group).astype(F32)) / F
    r.pmask[...] = pmask
    col = lax.broadcasted_iota(jnp.int32, (1, N * R), 1) + wi * (N * R)
    first = (ni == 0).astype(F32)
    r.amat[...] = jnp.where(meta[:, 1:2] == col.astype(F32), first / meta[:, 2:3], 0.0)
    xcopy(*piece(2, slot=n2), 3, n2).wait_recv()
    x_pass(2).start()
    block(n2)
    for k in range(3):
        xcopy(*piece(k, slot=n3), 4 + k, n1).wait_recv()
    block(n3)

    ex.gw.wait(r.gw)
    gw = r.gw[...].astype(F32)
    gmat = jnp.concatenate([gw[:, :Bg].reshape(B, Hn // 2), gw[:, Bg:].reshape(B, Hn // 2)], axis=1).astype(BF)
    r.gmat[...] = gmat
    amat = r.pmask[...] * dot(gmat, hid[...], NT) + r.amat[...]
    r.amat[...] = amat
    r.kn[ni] = dot(r.alphat[...], amat, NT, HIGH) + r.prior[...]
    ex.kn.gather(r.kn)
    turn(n2)
    turn(n3)
    ex.kn.wait(r.kn)
    r.kw[wi] = jnp.sum(r.kn[...], axis=0)
    ex.kw.gather(r.kw)
    ex.hgw.wait(r.hgw)
    hg = r.hgw[...].astype(F32)
    r.hbx[ni] = hg[:, :Bg].reshape(B, Hn).astype(BF)
    r.gb[...] = hg[:, Bg:].reshape(B, Hn)
    ex.hbx.gather(r.hbx)
    ex.xbw.wait(r.xbw)
    xbw = r.xbw[...].astype(F32)
    r.xbt[...] = jnp.concatenate([xbw[:, :Bg].reshape(B, D // 2), xbw[:, Bg:].reshape(B, D // 2)], axis=1).T.astype(BF)
    ex.kw.wait(r.kw)
    prec = r.metat[2:3, :]
    resid = r.metat[S : 2 * S, :] - jnp.sum(r.kw[...], axis=0)
    total = jnp.sum(prec, axis=1, keepdims=True)
    loss = 0.5 * jnp.sum(jnp.sum(prec * (resid * resid), axis=1, keepdims=True), axis=0, keepdims=True)
    grt = prec * resid / total

    ds = (-r.pmask[...] * dot(grt, r.alphat[...], TN, HIGH)).astype(BF)
    r.us[...] = dot(ds, hid[...]).reshape(W, Bg, Hn)
    ex.ur.scatter(r.us, r.ur)
    for q in range(N):
        rows = slice(q * R, (q + 1) * R)
        dpre[rows, :] = (dot(ds[:, rows], r.gmat[...], TN) * gd[rows, :]).astype(BF)

    def wcopy(src, dst, kind, k, slot, p):
        return pltpu.make_async_remote_copy(
            src_ref=src, dst_ref=dst, send_sem=getattr(r, kind + "_s").at[k], recv_sem=getattr(r, kind + "_r").at[slot],
            device_id={"wide": p}, device_id_type=MESH)

    psend, precv, zsend, zrecv, gat = r.psend, r.precv, r.zsend, r.zrecv, r.gat

    def grad_rows(row):
        return dot(xT[pl.ds(pl.multiple_of(row, Ck), Ck), :], dpre[...])

    def target(step):
        off = lax.rem(A // 2 + step - 1, max(A - 1, 1)) + 1
        return lax.rem(a + off + lax.rem(a, 2) * (A - 2 * off), A)

    def pair_chunk(ap):
        psend[ap] = grad_rows((1 - b) * half + ap * Ck).astype(BF)
        wcopy(psend.at[ap], precv.at[ap], "p", ap, ap, pair).start()

    def pair_send(step, carry):
        pair_chunk(target(step))
        return carry

    def z_sum(ap):
        v = grad_rows(b * half + ap * Ck)
        wcopy(psend.at[ap], precv.at[ap], "p", ap, ap, pair).wait_recv()
        return v + precv[ap].astype(F32)

    def z_send(step, carry):
        ap = target(step)
        zsend[ap] = z_sum(ap).astype(BF)
        wcopy(zsend.at[ap], zrecv.at[a], "z", ap, a, 2 * ap + b).start()
        return carry

    lax.fori_loop(0, min(1, A - 1), pair_send, 0)

    agt = -dot(grt, r.amat[...], precision=HIGH)
    for n in range(N):
        r.ags[n] = agt[:, n * R : (n + 1) * R]
    ex.agr.scatter(r.ags, r.agr)
    r.agr[ni] = r.ags[ni]
    r.gp[...] = dot(grt, r.pwt[...], TN, HIGH)
    dz = r.sz[...] * r.gp[own_b, :]
    ex.ur.wait(r.ur)
    r.ur[wi] = r.us[wi]
    uown = jnp.sum(r.ur[...], axis=0)
    r.uz[wi] = jnp.concatenate([uown, dz], axis=0).astype(BF)
    ex.uz.gather(r.uz)
    lax.fori_loop(min(1, A - 1), A - 1, pair_send, 0)
    pair_chunk(a)

    lax.fori_loop(0, min(1, A - 1), z_send, 0)

    ex.bfw.wait(r.bfw)
    ex.uz.wait(r.uz)
    uz = r.uz[...].astype(F32)
    r.uzn[ni] = jnp.concatenate([uz[:, :Bg].reshape(B, Hn), uz[:, Bg:].reshape(B, Mn)], axis=1).astype(BF)
    ex.uzn.gather(r.uzn)

    lax.fori_loop(min(1, A - 1), A - 1, z_send, 0)
    fin = z_sum(a)

    ex.uzn.wait(r.uzn)
    acc = jnp.zeros((B, Fn), F32)
    for n in range(N):
        acc = acc + dot(r.uzn[n, :, :Hn], w2b[n * Hn : (n + 1) * Hn, :])
        acc = acc + dot(r.uzn[n, :, Hn:], om[:, n * Mn : (n + 1) * Mn], NT)
    bfw = r.bfw[...].astype(F32)
    bfall = jnp.concatenate([bfw[:, :Bg].reshape(B, Fn // 2), bfw[:, Bg:].reshape(B, Fn // 2)], axis=1)
    r.db[...] = jnp.concatenate([acc, bfall], axis=0).astype(BF)
    for n in range(N):
        r.dhs[n] = dot(r.db[:B, :], w2b[n * Hn : (n + 1) * Hn, :], NT).astype(BF)
    ex.dhr.scatter(r.dhs, r.dhr)
    r.dhr[ni] = r.dhs[ni]

    def z_gain(k, total_rows):
        ap = lax.rem(a + k, A)
        wcopy(zsend.at[ap], zrecv.at[ap], "z", ap, ap, 2 * ap + b).wait_recv()
        return total_rows + zrecv[ap].astype(F32)

    fin = lax.fori_loop(1, A, z_gain, fin)
    mine = b * A + a


    def shard(slot):
        return pl.ds(pl.multiple_of(slot * Ck, Ck), Ck)

    gat[shard(mine), :] = fin.astype(BF)

    def fcopy(ap, side):
        rows = shard(side * A + ap)
        return wcopy(gat.at[rows], gat.at[rows], "f", ap, ap, pair)

    def gcopy(ap, way):
        rows = shard(b * A + ap)
        k = ap if way > 0 else A + ap
        return wcopy(gat.at[rows], gat.at[rows], "g", k, k, 2 * (a + way) + b)

    fcopy(a, b).start()

    @pl.when(a + 1 < A)
    def _():
        gcopy(a, 1).start()

    @pl.when(a > 0)
    def _():
        gcopy(a, -1).start()

    def g_pass(step, carry):
        below, above = a - 1 - step, a + 1 + step

        @pl.when(below >= 0)
        def _():
            gcopy(below, 1).wait_recv()

            @pl.when(a + 1 < A)
            def _():
                gcopy(below, 1).start()

            fcopy(below, b).start()

        @pl.when(above < A)
        def _():
            gcopy(above, -1).wait_recv()

            @pl.when(a > 0)
            def _():
                gcopy(above, -1).start()

            fcopy(above, b).start()

        return carry

    def two(v):
        return jnp.sum(jnp.sum(v * v, axis=1, keepdims=True), axis=0, keepdims=True)

    square = jnp.zeros((1, 1), F32)
    for n in range(N):
        if n == 0:
            ex.hbx.wait(r.hbx)
        hu = jnp.concatenate([r.hbx[n], r.uzn[n, :, :Hn]], axis=0)
        g2 = dot(hu, r.db[...], TN)
        r.g2[n * Hn : (n + 1) * Hn, :] = g2
        square = square + two(g2)

    ex.agr.wait(r.agr)
    agt = jnp.sum(r.agr[...], axis=0)
    r.agrad[...] = agt
    ex.dhr.wait(r.dhr)
    r.dpb[...] = (jnp.sum(r.dhr[...].astype(F32), axis=0) * r.gb[...]).astype(BF)

    square = square * (1.0 / W) + two(fin + dot(r.xbt[shard(mine), :], r.dpb[...])) + two(agt)
    r.nn[ni] = jnp.broadcast_to(square, (8, 128))
    ex.nn.gather(r.nn)
    lax.fori_loop(0, min(1, A - 1), g_pass, 0)
    ex.nn.wait(r.nn)
    r.nw[wi] = jnp.sum(r.nn[...], axis=0)
    ex.nw.gather(r.nw)
    lax.fori_loop(min(1, A - 1), A - 1, g_pass, 0)

    ex.nw.wait(r.nw)
    norm = jnp.sum(r.nw[...], axis=0)
    lanes = lax.broadcasted_iota(jnp.int32, (8, 128), 1)
    r.scal[...] = jnp.where(lanes == 0, loss, jnp.where(lanes == 1, total, norm))

    def g_last(k, carry):
        ap = lax.rem(a + k, A)
        fcopy(ap, 1 - b).wait_recv()
        return carry

    lax.fori_loop(0, A, g_last, 0)

    for name in WIDE_EX:
        vars(ex)[name].drain(getattr(r, name))
    for name in NARROW_EX:
        vars(ex)[name].drain(getattr(r, name))
    x_side().wait_send()
    for k in range(3):
        x_over(k).wait_send()
        x_pass(k).wait_send()

    def left(k, carry):
        wcopy(psend.at[k], precv.at[k], "p", k, k, pair).wait_send()
        fcopy(k, b).wait_send()

        @pl.when((k <= a) & (a + 1 < A))
        def _():
            gcopy(k, 1).wait_send()

        @pl.when((k >= a) & (a > 0))
        def _():
            gcopy(k, -1).wait_send()

        return carry

    def left_z(k, carry):
        ap = lax.rem(a + k, A)
        wcopy(zsend.at[ap], zrecv.at[a], "z", ap, a, 2 * ap + b).wait_send()
        return carry

    lax.fori_loop(0, A, left, 0)
    lax.fori_loop(1, A, left_z, 0)
    for load in later:
        load.wait()


CORR1 = 1.0 - 0.9**STEP_NUM
CORR2 = 1.0 - 0.999**STEP_NUM


def adamw(weight, grad, moment, second, rate, decay):
    moment_new = 0.9 * moment + 0.1 * grad
    second_new = 0.999 * second + 0.001 * grad * grad
    step = moment_new / (jnp.sqrt(second_new) * (1.0 / math.sqrt(CORR2)) + 1e-08)
    new = weight * (1.0 - rate * decay) - (rate / CORR1) * step
    return moment_new, second_new, new


def update_kernel(resident, slots, C, names, *refs):
    r = SimpleNamespace(**dict(zip(names, refs)))
    if not resident:
        pairs = ((r.w1, r.w1f), (r.w1_m, r.m1), (r.w1_v, r.v1), (r.w2, r.w2f), (r.w2_m, r.m2), (r.w2_v, r.v2))
        loads = [pltpu.make_async_copy(src, dst, r.lsem.at[k]) for k, (src, dst) in enumerate(pairs)]
        for load in loads:
            load.start()
        for load in loads:
            load.wait()
    small = [pltpu.make_async_copy(src, r.asl.at[k], r.asem.at[k]) for k, src in enumerate((r.at, r.atm, r.atv))]
    for load in small:
        load.start()
    norm = r.scal[0:1, 2:3]
    clip = jnp.minimum(1.0, 0.1 / jnp.sqrt(norm))
    ring = (r.sm, r.sv, r.sn, r.sc)

    def copies(outs, slot, rows):
        return [pltpu.make_async_copy(buf.at[slot], out.at[rows], r.osem.at[slot, k]) for k, (buf, out) in enumerate(zip(ring, outs))]

    def chunk(grad, state, outs, k, ahead):
        w, m, v = state
        slot = lax.rem(k + ahead, slots)
        base = pl.multiple_of(k * C, C)
        rows = pl.ds(base, C)

        def drain():
            for copy in copies(outs, slot, rows):
                copy.wait()

        if ahead:
            drain()
        else:
            pl.when(k >= slots)(drain)

        def part(j, carry):
            src = pl.ds(pl.multiple_of(base + j * 16, 16), 16)
            dst = pl.ds(pl.multiple_of(j * 16, 16), 16)
            mn, vn, wn = adamw(w[src, :], clip * grad[src, :], m[src, :], v[src, :], 0.03, 0.01)
            r.sm[slot, dst, :] = mn
            r.sv[slot, dst, :] = vn
            r.sn[slot, dst, :] = wn
            r.sc[slot, dst, :] = wn.astype(BF)
            return carry

        lax.fori_loop(0, C // 16, part, 0, unroll=True)
        for copy in copies(outs, slot, rows):
            copy.start()

    outs1 = (r.m1o, r.v1o, r.n1o, r.c1o)
    outs2 = (r.m2o, r.v2o, r.n2o, r.c2o)
    count1, count2 = r.w1f.shape[0] // C, r.w2f.shape[0] // C

    def step2(k, carry):
        chunk(r.g2, (r.w2f, r.m2, r.v2), outs2, k, 0)
        return carry

    def step1(k, carry):
        chunk(r.gs, (r.w1f, r.m1, r.v1), outs1, k, count2)
        return carry

    lax.fori_loop(0, count2, step2, 0)
    r.gs[...] = r.gat[...].astype(F32) + dot(r.xbt[...], r.dpb[...])
    lax.fori_loop(0, count1, step1, 0)
    for load in small:
        load.wait()
    am, av, an = adamw(r.asl[0], clip * r.agrad[...], r.asl[1], r.asl[2], 0.2, 0.0)
    for k, v in enumerate((am, av, an)):
        r.ast[k] = v
    last = [pltpu.make_async_copy(r.ast.at[k], dst, r.asem.at[k]) for k, dst in enumerate((r.amo, r.avo, r.ano))]
    for copy in last:
        copy.start()
    for k in range(slots):
        for copy in copies(outs1, k, pl.ds(0, C)):
            copy.wait()
    for copy in last:
        copy.wait()


def on_device(
    data_x, data_group, batch_x, batch_group, batch_index, prec_index, prec_table, targets,
    omega, phase, prior_w, w1_master, w1_moment, w1_second, w2_master, w2_moment, w2_second,
    alpha, alpha_moment, alpha_second,
):
    W, N = lax.axis_size("wide"), lax.axis_size("narrow")
    A = W // 2
    R, D = data_x.shape
    brow, Bg, S = batch_x.shape[0], targets.shape[0], targets.shape[1]
    F, M = omega.shape
    Hn, Fn, Mn, H = w1_master.shape[1], w2_master.shape[1], M // N, w2_master.shape[0]
    B, Ck = W * Bg, D // 2 // A
    hbm, vmem, smem = (pl.BlockSpec(memory_space=m) for m in (pl.ANY, pltpu.VMEM, pltpu.SMEM))
    resident = B <= 128
    args = dict(
        data_x=(data_x, hbm), dgroup=(data_group.reshape(1, R), vmem), batch_x=(batch_x, vmem),
        bgroup=(batch_group, smem), bindex=(batch_index, smem), pindex=(prec_index, smem),
        ptable=(prec_table, smem), targets=(targets, vmem), omega=(omega, hbm),
        phase=(phase.reshape(1, M), vmem), prior_wt=(prior_w.T, hbm), w1=(w1_master, hbm),
        w2=(w2_master, hbm), alphat_own=(alpha.T, vmem),
    )
    state = dict(
        w1=(w1_master, hbm), w1_m=(w1_moment, hbm), w1_v=(w1_second, hbm),
        w2=(w2_master, hbm), w2_m=(w2_moment, hbm), w2_v=(w2_second, hbm),
    )
    outs = dict(
        scal=((8, 128), F32), agrad=((S, R), F32), gat=((D, Hn), BF), xbt=((D, B), BF), dpb=((B, Hn), BF),
        g2=((H, Fn), F32),
    )
    held = dict(
        w1f=((D, Hn), F32), m1=((D, Hn), F32), v1=((D, Hn), F32), w2f=((H, Fn), F32), m2=((H, Fn), F32), v2=((H, Fn), F32),
    )
    scratch = dict(
        xg=((N, R, D), BF), xT=((D, N * R), BF), hid=((N * R, Hn), BF), gd=((N * R, Hn), F32),
        dpre=((N * R, Hn), BF), pre=((R, Hn), F32), w1b=((D, Hn), BF),
        w2b=((H, Fn), BF), om=((Fn, M), BF), pwt=((S, Mn), F32),
        xbg=((Bg, D), F32), gzs=((N, Bg, Hn + Mn), F32), us=((W, Bg, Hn), F32), ags=((N, S, R), F32),
        dhs=((N, B, Hn), BF), cz=((B, Mn), F32), sz=((Bg, Mn), F32), prior=((S, B), F32), gp=((B, Mn), F32),
        metat=((128, B), F32), alphat=((S, N * R), F32), pmask=((B, N * R), F32), amat=((B, N * R), F32),
        gmat=((B, Hn), BF), db=((2 * B, Fn), BF),
        psend=((A, Ck, Hn), BF), precv=((A, Ck, Hn), BF), zsend=((A, Ck, Hn), BF), zrecv=((A, Ck, Hn), BF),
        gb=((B, Hn), F32),
        meta=((W, Bg, 128), F32), xbw=((W, 2 * Bg, D // 2), BF), hgw=((W, 2 * Bg, Hn), BF),
        bfw=((W, 2 * Bg, Fn // 2), BF), gw=((W, 2 * Bg, Hn // 2), BF), kw=((W, S, B), F32),
        ur=((W, Bg, Hn), F32), uz=((W, 2 * Bg, Hn), BF), nw=((W, 8, 128), F32),
        xbn=((N, brow, D), F32), ad=((N, S + 8, R), F32), hbn=((N, Bg, Hn), F32), gzr=((N, Bg, Hn + Mn), F32),
        kn=((N, S, B), F32), agr=((N, S, R), F32), uzn=((N, B, Hn + Mn), BF), hbx=((N, B, Hn), BF), dhr=((N, B, Hn), BF),
        nn=((N, 8, 128), F32),
    )
    if resident:
        args.update(state)
        outs.update(held)
    else:
        scratch.update(w1f=held["w1f"], w2f=held["w2f"])
    sems = [("lsem", 9), ("x_s", 7), ("x_r", 7)]
    sems += [(name + end, W) for name in WIDE_EX for end in ("_s", "_r")]
    sems += [(name + end, N) for name in NARROW_EX for end in ("_s", "_r")]
    sems += [(name + end, A) for name in ("p", "z", "f") for end in ("_s", "_r")]
    sems += [("g_s", 2 * A), ("g_r", 2 * A)]
    names = [*args, *outs, *scratch] + [n for n, _ in sems]
    grads = pl.pallas_call(
        lambda *refs: step_kernel(W, N, resident, names, *refs),
        out_shape=[(pltpu.VMEM if resident else jax.ShapeDtypeStruct)(s, t) for s, t in outs.values()],
        in_specs=[spec for _, spec in args.values()],
        out_specs=[vmem] * len(outs),
        scratch_shapes=[pltpu.VMEM(s, t) for s, t in scratch.values()] + [pltpu.SemaphoreType.DMA((k,)) for _, k in sems],
        compiler_params=pltpu.CompilerParams(collective_id=0, has_side_effects=True, vmem_limit_bytes=(60 if not resident else 39) * 2**20),
        name="gradients",
    )(*[v for v, _ in args.values()])

    args2 = {k: (v, vmem) for k, v in zip(outs, grads)}
    args2.update(at=(alpha.T, hbm), atm=(alpha_moment.T, hbm), atv=(alpha_second.T, hbm))
    C, slots = 256, 3
    outs2 = dict(amo=((S, R), F32, hbm), avo=((S, R), F32, hbm), ano=((S, R), F32, hbm))
    for k, shape in (("1", (D, Hn)), ("2", (H, Fn))):
        outs2.update({"m" + k + "o": (shape, F32, hbm), "v" + k + "o": (shape, F32, hbm)})
        outs2.update({"n" + k + "o": (shape, F32, hbm), "c" + k + "o": (shape, BF, hbm)})
    scratch2 = dict(
        gs=pltpu.VMEM((D, Hn), F32), sm=pltpu.VMEM((slots, C, Hn), F32), sv=pltpu.VMEM((slots, C, Hn), F32),
        sn=pltpu.VMEM((slots, C, Hn), F32), sc=pltpu.VMEM((slots, C, Hn), BF), osem=pltpu.SemaphoreType.DMA((slots, 4)),
        asl=pltpu.VMEM((3, S, R), F32), ast=pltpu.VMEM((3, S, R), F32), asem=pltpu.SemaphoreType.DMA((3,)),
    )
    if not resident:
        args2.update(state)
        scratch2.update({k: pltpu.VMEM(s, t) for k, (s, t) in held.items()}, lsem=pltpu.SemaphoreType.DMA((6,)))
    names2 = [*args2, *outs2, *scratch2]
    new = pl.pallas_call(
        lambda *refs: update_kernel(resident, slots, C, names2, *refs),
        out_shape=[jax.ShapeDtypeStruct(s, t) for s, t, _ in outs2.values()],
        in_specs=[spec for _, spec in args2.values()],
        out_specs=[spec for _, _, spec in outs2.values()],
        scratch_shapes=list(scratch2.values()),
        compiler_params=pltpu.CompilerParams(vmem_limit_bytes=(36 if not resident else 10) * 2**20),
        name="adamw",
    )(*[v for v, _ in args2.values()])
    new = dict(zip(outs2, new))
    scal = grads[0]
    return (
        scal[0, 0], scal[0, 1], scal[0, 2],
        new["m1o"], new["v1o"], new["n1o"], new["c1o"],
        new["m2o"], new["v2o"], new["n2o"], new["c2o"],
        new["amo"].T, new["avo"].T, new["ano"].T,
    )


def solution(mesh):
    both = P(("wide", "narrow"))
    both2 = P(("wide", "narrow"), None)
    col = P(None, "narrow")
    return jax.shard_map(
        on_device,
        mesh=mesh,
        in_specs=(both2, both, both2, P("wide"), P("wide"), P("wide"), P(), P("wide", None), P(), P(), P())
        + (col,) * 6 + (both2,) * 3,
        out_specs=(P(), P(), P()) + (col,) * 8 + (both2,) * 3,
        check_vma=False,
    )
```

```python
import math
from types import SimpleNamespace

import jax
import jax.numpy as jnp
from jax import lax
from jax.experimental import pallas as pl
from jax.experimental.pallas import tpu as pltpu
from jax.sharding import PartitionSpec as P

STEP_NUM = 10
HIGH = lax.Precision.HIGHEST
MESH = pl.DeviceIdType.MESH
GC = math.sqrt(2.0 / math.pi)
F32 = jnp.float32
BF = jnp.bfloat16


def gelu_pair(pre):
    square = pre * pre
    t = jnp.tanh(pre * (GC + (GC * 0.044715) * square))
    half = 0.5 * (1.0 + t)
    slope = half + 0.5 * pre * (1.0 - t * t) * (GC + (3 * GC * 0.044715) * square)
    return pre * half, slope


def dot(left, right, dims=((1,), (0,)), precision=None):
    return lax.dot_general(left, right, (dims, ((), ())), precision=precision, preferred_element_type=F32)


NT = ((1,), (1,))
TN = ((0,), (0,))


class Exchange:
    def __init__(self, size, me, where, sems, k):
        self.size, self.me, self.where, self.sems, self.k = size, me, where, sems, k

    def copy(self, src, dst, p):
        return pltpu.make_async_remote_copy(
            src_ref=src, dst_ref=dst, send_sem=self.sems.at[self.k], recv_sem=self.sems.at[self.k + 1],
            device_id=self.where(p), device_id_type=MESH)

    def loop(self, body):
        def step(k, carry):
            body(lax.rem(self.me + k, self.size))
            return carry

        lax.fori_loop(1, self.size, step, 0)

    def greet(self, barrier):
        self.loop(lambda p: pl.semaphore_signal(barrier, inc=1, device_id=self.where(p), device_id_type=MESH))

    def gather(self, buf):
        self.loop(lambda p: self.copy(buf.at[self.me], buf.at[self.me], p).start())

    def scatter(self, src, buf):
        self.loop(lambda p: self.copy(src.at[p], buf.at[self.me], p).start())

    def all(self, buf):
        others = buf.at[pl.ds(0, self.size - 1)]
        return self.copy(others, others, lax.rem(self.me + 1, self.size))

    def wait(self, buf):
        self.all(buf).wait_recv()

    def drain(self, buf):
        self.all(buf).wait_send()


WIDE_EX = ("meta", "xbw", "hgw", "bfw", "gw", "ur", "uz")
NARROW_EX = ("xbn", "hbn", "ger", "zer", "agr", "uzn", "hbx", "dhr")
CHIP_EX = ("kw", "nw")


def step_kernel(W, N, resident, names, *refs):
    r = SimpleNamespace(**dict(zip(names, refs)))
    wi, ni = lax.axis_index("wide"), lax.axis_index("narrow")
    A = W // 2
    a, b = wi // 2, lax.rem(wi, 2)
    pair = wi + 1 - 2 * b
    n1 = ni + 1 - 2 * lax.rem(ni, 2)
    n2 = lax.rem(ni + 2, N)
    n3 = lax.rem(n1 + 2, N)
    xg, hid, gd, xT, dpre = r.xg, r.hid, r.gd, r.xT, r.dpre
    w1b, w2b, om = r.w1b, r.w2b, r.om
    _, R, D = xg.shape
    Bg, S = r.targets.shape
    brow = r.batch_x.shape[0]
    Hn, Fn = w1b.shape[1], w2b.shape[1]
    H, F, M = w2b.shape[0], r.omega.shape[0], r.omega.shape[1]
    Mn = M // N
    B = W * Bg
    half = D // 2
    Ck = half // A
    scale = math.sqrt(2.0 / M)
    lsem = r.lsem
    core, side = lax.rem(ni, 2), ni // 2
    groups = (
        (WIDE_EX, W, wi, lambda p: {"wide": p}),
        (NARROW_EX, N, ni, lambda p: {"narrow": p}),
        (CHIP_EX, W * N // 2, wi * (N // 2) + side, lambda p: {"wide": p // (N // 2), "narrow": lax.rem(p, N // 2) * 2 + core}),
    )
    ex, live = SimpleNamespace(), []
    for group, size, me, where in groups:
        for name in group:
            vars(ex)[name] = Exchange(size, me, where, r.es, 2 * len(live))
            live.append(name)

    own_f = pl.ds(pl.multiple_of(ni * Fn, Fn), Fn)
    own_m = pl.ds(pl.multiple_of(ni * Mn, Mn), Mn)
    loads = [
        pltpu.make_async_copy(r.w1, r.w1f, lsem.at[0]),
        pltpu.make_async_copy(r.data_x, xg.at[ni], lsem.at[1]),
        pltpu.make_async_copy(r.w2, r.w2f, lsem.at[2]),
        pltpu.make_async_copy(r.omega.at[own_f], om, lsem.at[3]),
        pltpu.make_async_copy(r.prior_wt.at[:, own_m], r.pwt, lsem.at[4]),
        pltpu.make_async_copy(r.phase.at[:, own_m], r.ph, lsem.at[9]),
    ]
    small = [
        pltpu.make_async_copy(r.batch_x, r.xbs, lsem.at[10]),
        pltpu.make_async_copy(r.targets, r.tgs, lsem.at[11]),
        pltpu.make_async_copy(r.dgroup, r.dgs, lsem.at[12]),
        pltpu.make_async_copy(r.alphat_own, r.als, lsem.at[13]),
    ]
    for load in small[:1] + loads[:1] + small[1:] + loads[1:]:
        load.start()

    barrier = pltpu.get_barrier_semaphore()

    ex.kw.greet(barrier)
    ex.xbn.greet(barrier)
    small[0].wait()
    r.xbn[ni] = r.xbs[...].astype(F32)
    lane = lax.broadcasted_iota(jnp.int32, (1, 128), 1)
    for k in range(Bg):
        prec_k = r.ptable[r.pindex[k]]
        r.meta[wi, k : k + 1, :] = jnp.where(
            lane == 0, r.bgroup[k].astype(F32),
            jnp.where(lane == 1, r.bindex[k].astype(F32), jnp.where(lane == 2, prec_k, 0.0)))
    for load in small[1:]:
        load.wait()
    r.meta[wi, :, S : 2 * S] = r.tgs[...]
    r.ad[ni, 0:S, :] = r.als[...]
    r.ad[ni, S : S + 8, :] = jnp.broadcast_to(r.dgs[...].astype(F32), (8, R))

    pl.semaphore_wait(barrier, W * N // 2 - 1 + N - 1)

    def xcopy(src, dst, k, p):
        return pltpu.make_async_remote_copy(
            src_ref=src, dst_ref=dst, send_sem=r.x_s.at[k], recv_sem=r.x_r.at[k],
            device_id={"narrow": p}, device_id_type=MESH)

    cuts = (0, R * 4 // 16, R * 11 // 16, R)

    def piece(k, src=None, slot=None):
        rows = pl.ds(cuts[k], cuts[k + 1] - cuts[k])
        slot = ni if slot is None else slot
        src = xg.at[slot, rows] if src is None else src.at[rows]
        return src, xg.at[slot, rows]

    def x_side():
        return xcopy(r.data_x, xg.at[ni], 0, n1)

    def x_over(k):
        return xcopy(*piece(k, r.data_x), 1 + k, n2)

    def x_pass(k):
        return xcopy(*piece(k, slot=n2), 4 + k, n1)

    ex.xbn.gather(r.xbn)
    x_over(0).start()
    ex.meta.gather(r.meta)

    def ad_copy(slot, k, p):
        return xcopy(r.ad.at[slot], r.ad.at[slot], 7 + k, p)

    ad_copy(ni, 0, n1).start()

    loads[0].wait()

    def cast1(k, carry):
        rows = pl.ds(pl.multiple_of(k * 128, 128), 128)
        w1b[rows, :] = r.w1f[rows, :].astype(BF)
        return carry

    lax.fori_loop(0, D // 128, cast1, 0)
    ex.xbn.wait(r.xbn)
    for n in range(N):
        r.xbg[n * brow : (n + 1) * brow, :] = r.xbn[n]
    xbg = r.xbg[...]
    hb, gb = gelu_pair(dot(xbg.astype(BF), w1b[...]))
    hb = hb.astype(BF).astype(F32)
    r.hbn[ni] = jnp.concatenate([hb[:, : Hn // 2], hb[:, Hn // 2 :]], axis=0).astype(BF)
    ex.hbn.gather(r.hbn)
    x_over(1).start()
    x_side().start()
    ad_copy(ni, 1, n2).start()
    r.hgw[wi] = jnp.concatenate([hb, gb], axis=0).astype(BF)
    ex.hgw.gather(r.hgw)
    r.xbw[wi] = jnp.concatenate([xbg[:, : D // 2], xbg[:, D // 2 :]], axis=0).astype(BF)
    ex.xbw.gather(r.xbw)
    loads[2].wait()

    def cast2(k, carry):
        rows = pl.ds(pl.multiple_of(k * 128, 128), 128)
        w2b[rows, :] = r.w2f[rows, :].astype(BF)
        return carry

    lax.fori_loop(0, H // 128, cast2, 0)

    def block(q):
        base = q * R
        r.pre[...] = dot(xg[q], w1b[...])

        def part(k, carry):
            src = pl.ds(pl.multiple_of(k * 32, 32), 32)
            dst = pl.ds(pl.multiple_of(base + k * 32, 32), 32)
            out, slope = gelu_pair(r.pre[src, :])
            hid[dst, :] = out.astype(BF)
            gd[dst, :] = slope
            return carry

        lax.fori_loop(0, R // 32, part, 0)

    def turn(q):
        xT[:, pl.ds(pl.multiple_of(q * R, R), R)] = xg[q].T

    ex.hbn.wait(r.hbn)
    hbn = [r.hbn[n].astype(F32) for n in range(N)]
    hid_g = jnp.concatenate([h[k * Bg : (k + 1) * Bg] for h in hbn for k in range(2)], axis=1).astype(BF)
    bfeat = dot(hid_g, w2b[...]).astype(BF)
    r.bfs[...] = bfeat.astype(F32)
    gpart = dot(bfeat, w2b[...], NT)
    for n in range(N):
        r.ges[n] = gpart[:, n * Hn : (n + 1) * Hn]
    ex.ger.scatter(r.ges, r.ger)
    r.ger[ni] = r.ges[ni]
    loads[3].wait()
    zpart = dot(r.bfs[...].astype(BF), om[...])
    for n in range(N):
        r.zes[n] = zpart[:, n * Mn : (n + 1) * Mn]
    ex.zer.scatter(r.zes, r.zer)
    r.zer[ni] = r.zes[ni]
    x_over(2).start()
    later = []
    if resident:
        pairs = ((r.w1_m, r.m1), (r.w1_v, r.v1), (r.w2_m, r.m2), (r.w2_v, r.v2))
        later = [pltpu.make_async_copy(src, dst, lsem.at[5 + k]) for k, (src, dst) in enumerate(pairs)]
    for load in later:
        load.start()
    bf32 = r.bfs[...]
    r.bfw[wi] = jnp.concatenate([bf32[:, : Fn // 2], bf32[:, Fn // 2 :]], axis=0).astype(BF)
    ex.bfw.gather(r.bfw)
    loads[1].wait()
    block(ni)
    ex.ger.wait(r.ger)
    gz = jnp.sum(r.ger[...], axis=0)
    r.gw[wi] = jnp.concatenate([gz[:, : Hn // 2], gz[:, Hn // 2 : Hn]], axis=0).astype(BF)
    ex.gw.gather(r.gw)
    for k in range(2):
        xcopy(*piece(k, slot=n2), 1 + k, n2).wait_recv()
        x_pass(k).start()
    ad_copy(n2, 1, n2).wait_recv()
    ad_copy(n2, 2, n1).start()
    ex.zer.wait(r.zer)
    own_b = pl.ds(pl.multiple_of(wi * Bg, Bg), Bg)
    loads[5].wait()
    angle = jnp.sum(r.zer[...], axis=0) + r.ph[...]
    r.cz[...] = jnp.zeros_like(r.cz)
    r.cz[own_b, :] = scale * jnp.cos(angle)
    r.sz[...] = scale * jnp.sin(angle)
    loads[4].wait()
    r.prior[...] = dot(r.pwt[...], r.cz[...], NT, HIGH)

    xcopy(r.data_x, xg.at[n1], 0, n1).wait_recv()
    block(n1)
    turn(ni)
    turn(n1)
    ex.meta.wait(r.meta)
    ad_copy(n1, 0, n1).wait_recv()
    ad_copy(n3, 2, n1).wait_recv()
    meta = r.meta[...].reshape(B, 128)
    r.metat[...] = meta.T
    alphat = jnp.concatenate([r.ad[n, 0:S, :] for n in range(N)], axis=1)
    r.alphat[...] = alphat
    group = jnp.concatenate([r.ad[n, S : S + 1, :] for n in range(N)], axis=1)
    pmask = (0.5 + (meta[:, 0:1] == group).astype(F32)) / F
    r.pmask[...] = pmask
    col = lax.broadcasted_iota(jnp.int32, (1, N * R), 1) + wi * (N * R)
    first = (ni == 0).astype(F32)
    r.amat[...] = jnp.where(meta[:, 1:2] == col.astype(F32), first / meta[:, 2:3], 0.0)
    xcopy(*piece(2, slot=n2), 3, n2).wait_recv()
    x_pass(2).start()
    block(n2)
    for k in range(3):
        xcopy(*piece(k, slot=n3), 4 + k, n1).wait_recv()
    block(n3)

    ex.gw.wait(r.gw)
    gw = r.gw[...].astype(F32)
    gmat = jnp.concatenate([gw[:, :Bg].reshape(B, Hn // 2), gw[:, Bg:].reshape(B, Hn // 2)], axis=1).astype(BF)
    r.gmat[...] = gmat
    amat = r.pmask[...] * dot(gmat, hid[...], NT) + r.amat[...]
    r.amat[...] = amat
    r.kn[core] = dot(r.alphat[...], amat, NT, HIGH) + r.prior[...]

    def core_copy(buf, k):
        return xcopy(buf.at[core], buf.at[core], 10 + k, n1)

    def core_sum(buf, k):
        xcopy(buf.at[1 - core], buf.at[1 - core], 10 + k, n1).wait_recv()
        return buf[0] + buf[1]

    core_copy(r.kn, 0).start()
    turn(n2)
    turn(n3)
    chip = wi * (N // 2) + side
    r.kw[chip] = core_sum(r.kn, 0)
    ex.kw.gather(r.kw)
    ex.hgw.wait(r.hgw)
    hg = r.hgw[...].astype(F32)
    r.hbx[ni] = hg[:, :Bg].reshape(B, Hn).astype(BF)
    r.gb[...] = hg[:, Bg:].reshape(B, Hn)
    ex.hbx.gather(r.hbx)
    ex.xbw.wait(r.xbw)
    xbw = r.xbw[...].astype(F32)
    r.xbt[...] = jnp.concatenate([xbw[:, :Bg].reshape(B, D // 2), xbw[:, Bg:].reshape(B, D // 2)], axis=1).T.astype(BF)
    ex.kw.wait(r.kw)
    prec = r.metat[2:3, :]
    resid = r.metat[S : 2 * S, :] - jnp.sum(r.kw[...], axis=0)
    total = jnp.sum(prec, axis=1, keepdims=True)
    loss = 0.5 * jnp.sum(jnp.sum(prec * (resid * resid), axis=1, keepdims=True), axis=0, keepdims=True)
    grt = prec * resid / total

    ds = (-r.pmask[...] * dot(grt, r.alphat[...], TN, HIGH)).astype(BF)
    r.us[...] = dot(ds, hid[...]).reshape(W, Bg, Hn)
    ex.ur.scatter(r.us, r.ur)
    for q in range(N):
        rows = slice(q * R, (q + 1) * R)
        dpre[rows, :] = (dot(ds[:, rows], r.gmat[...], TN) * gd[rows, :]).astype(BF)

    def wcopy(src, dst, kind, k, slot, p):
        return pltpu.make_async_remote_copy(
            src_ref=src, dst_ref=dst, send_sem=getattr(r, kind + "_s").at[k], recv_sem=getattr(r, kind + "_r").at[slot],
            device_id={"wide": p}, device_id_type=MESH)

    psend, precv, zsend, zrecv, gat = r.psend, r.precv, r.zsend, r.zrecv, r.gat

    def grad_rows(row):
        return dot(xT[pl.ds(pl.multiple_of(row, Ck), Ck), :], dpre[...])

    def target(step):
        off = lax.rem(A // 2 + step - 1, max(A - 1, 1)) + 1
        return lax.rem(a + off + lax.rem(a, 2) * (A - 2 * off), A)

    Q = max(1, min(4, Ck // 16))
    Cq = Ck // Q

    def pcopy(ap, q):
        rows = pl.ds(pl.multiple_of(ap * Ck + q * Cq, Cq), Cq)
        return wcopy(psend.at[rows], precv.at[rows], "p", 0, ap * Q + q, pair)

    def pair_chunk(ap):
        psend[pl.ds(pl.multiple_of(ap * Ck, Ck), Ck), :] = grad_rows((1 - b) * half + ap * Ck).astype(BF)
        for q in range(Q):
            pcopy(ap, q).start()

    def pair_send(step, carry):
        pair_chunk(target(step))
        return carry

    def zcopy(ap, q):
        rows = pl.ds(q * Cq, Cq)
        return wcopy(zsend.at[ap, rows], zrecv.at[a, rows], "z", 0, 0, 2 * ap + b)

    def z_part(ap, q):
        pcopy(ap, q).wait_recv()
        rows = pl.ds(pl.multiple_of(ap * Ck + q * Cq, Cq), Cq)
        return r.zf[q * Cq : (q + 1) * Cq, :] + precv[rows, :].astype(F32)

    def z_send(step, carry):
        ap = target(step)
        r.zf[...] = grad_rows(b * half + ap * Ck)
        for q in range(Q):
            zsend[ap, q * Cq : (q + 1) * Cq, :] = z_part(ap, q).astype(BF)
            zcopy(ap, q).start()
        return carry

    lax.fori_loop(0, min(2, A - 1), pair_send, 0)

    agt = -dot(grt, r.amat[...], precision=HIGH)
    for n in range(N):
        r.ags[n] = agt[:, n * R : (n + 1) * R]
    ex.agr.scatter(r.ags, r.agr)
    r.agr[ni] = r.ags[ni]
    r.gp[...] = dot(grt, r.pwt[...], TN, HIGH)
    dz = r.sz[...] * r.gp[own_b, :]
    ex.ur.wait(r.ur)
    r.ur[wi] = r.us[wi]
    uown = jnp.sum(r.ur[...], axis=0)
    r.uz[wi] = jnp.concatenate([uown, dz], axis=0).astype(BF)
    ex.uz.gather(r.uz)
    lax.fori_loop(min(2, A - 1), A - 1, pair_send, 0)
    pair_chunk(a)

    lax.fori_loop(0, min(2, A - 1), z_send, 0)

    ex.bfw.wait(r.bfw)
    ex.uz.wait(r.uz)
    uz = r.uz[...].astype(F32)
    r.uzn[ni] = jnp.concatenate([uz[:, :Bg].reshape(B, Hn), uz[:, Bg:].reshape(B, Mn)], axis=1).astype(BF)
    ex.uzn.gather(r.uzn)

    lax.fori_loop(min(2, A - 1), A - 1, z_send, 0)
    r.zf[...] = grad_rows(b * half + a * Ck)
    for q in range(Q):
        r.zf[q * Cq : (q + 1) * Cq, :] = z_part(a, q)

    if A > 1:
        others = pl.ds(0, A - 1)
        wcopy(zsend.at[others], zrecv.at[others], "z", 0, 0, pair).wait_recv()

    def z_gain(k, carry):
        r.zf[...] = r.zf[...] + zrecv[lax.rem(a + k, A)].astype(F32)
        return carry

    lax.fori_loop(1, A, z_gain, 0)
    mine = b * A + a

    def shard(slot, q=0, count=Ck):
        return pl.ds(pl.multiple_of(slot * Ck + q * Cq, Cq), count)

    gat[shard(mine), :] = r.zf[...].astype(BF)

    def fcopy(ap, q):
        rows = shard(b * A + ap, q, Cq)
        return wcopy(gat.at[rows], gat.at[rows], "f", 0, 0, pair)

    def gcopy(ap, q, way):
        rows = shard(b * A + ap, q, Cq)
        k = ap * Q + q if way > 0 else (A + ap) * Q + q
        return wcopy(gat.at[rows], gat.at[rows], "g", 0 if way > 0 else 1, k, 2 * (a + way) + b)

    for q in range(Q):

        @pl.when(a + 1 < A)
        def _():
            gcopy(a, q, 1).start()

        @pl.when(a > 0)
        def _():
            gcopy(a, q, -1).start()

        fcopy(a, q).start()

    def g_pass(step, carry):
        below, above = a - 1 - step // Q, a + 1 + step // Q
        q = lax.rem(step, Q)

        @pl.when(below >= 0)
        def _():
            gcopy(below, q, 1).wait_recv()

            @pl.when(a + 1 < A)
            def _():
                gcopy(below, q, 1).start()

            fcopy(below, q).start()

        @pl.when(above < A)
        def _():
            gcopy(above, q, -1).wait_recv()

            @pl.when(a > 0)
            def _():
                gcopy(above, q, -1).start()

            fcopy(above, q).start()

        return carry

    steps = (A - 1) * Q
    third = min(Q, steps)
    ex.uzn.wait(r.uzn)
    acc = jnp.zeros((B, Fn), F32)
    for n in range(N):
        acc = acc + dot(r.uzn[n, :, :Hn], w2b[n * Hn : (n + 1) * Hn, :])
        acc = acc + dot(r.uzn[n, :, Hn:], om[:, n * Mn : (n + 1) * Mn], NT)
    bfw = r.bfw[...].astype(F32)
    bfall = jnp.concatenate([bfw[:, :Bg].reshape(B, Fn // 2), bfw[:, Bg:].reshape(B, Fn // 2)], axis=1)
    r.db[...] = jnp.concatenate([acc, bfall], axis=0).astype(BF)
    for n in range(N):
        r.dhs[n] = dot(r.db[:B, :], w2b[n * Hn : (n + 1) * Hn, :], NT).astype(BF)
    ex.dhr.scatter(r.dhs, r.dhr)
    r.dhr[ni] = r.dhs[ni]

    lax.fori_loop(0, third, g_pass, 0)

    def two(v):
        return jnp.sum(jnp.sum(v * v, axis=1, keepdims=True), axis=0, keepdims=True)

    square = jnp.zeros((1, 1), F32)
    for n in range(N):
        if n == 0:
            ex.hbx.wait(r.hbx)
        hu = jnp.concatenate([r.hbx[n], r.uzn[n, :, :Hn]], axis=0)
        g2 = dot(hu, r.db[...], TN)
        r.g2[n * Hn : (n + 1) * Hn, :] = g2
        square = square + two(g2)

    ex.agr.wait(r.agr)
    agt = jnp.sum(r.agr[...], axis=0)
    r.agrad[...] = agt
    ex.dhr.wait(r.dhr)
    r.dpb[...] = (jnp.sum(r.dhr[...].astype(F32), axis=0) * r.gb[...]).astype(BF)

    square = square * (1.0 / W) + two(r.zf[...] + dot(r.xbt[shard(mine), :], r.dpb[...])) + two(agt)
    r.nn[core] = jnp.broadcast_to(square, (8, 128))
    core_copy(r.nn, 1).start()
    lax.fori_loop(third, min(2 * third, steps), g_pass, 0)
    r.nw[chip] = core_sum(r.nn, 1)
    ex.nw.gather(r.nw)
    lax.fori_loop(min(2 * third, steps), steps, g_pass, 0)
    ex.nw.wait(r.nw)
    norm = jnp.sum(r.nw[...], axis=0)
    lanes = lax.broadcasted_iota(jnp.int32, (8, 128), 1)
    r.scal[...] = jnp.where(lanes == 0, loss, jnp.where(lanes == 1, total, norm))

    theirs = pl.ds(pl.multiple_of((1 - b) * half, half), half)
    ours = pl.ds(pl.multiple_of(b * half, half), half)
    wcopy(gat.at[theirs], gat.at[theirs], "f", 0, 0, pair).wait_recv()

    for name in live:
        vars(ex)[name].drain(getattr(r, name))
    x_side().wait_send()
    for k in range(3):
        x_over(k).wait_send()
        x_pass(k).wait_send()
    for slot, k, p in ((ni, 0, n1), (ni, 1, n2), (n2, 2, n1)):
        ad_copy(slot, k, p).wait_send()
    core_copy(r.kn, 0).wait_send()
    core_copy(r.nn, 1).wait_send()
    wcopy(psend, precv, "p", 0, 0, pair).wait_send()
    wcopy(gat.at[ours], gat.at[ours], "f", 0, 0, pair).wait_send()
    if A > 1:
        wcopy(zsend.at[others], zrecv.at[others], "z", 0, 0, pair).wait_send()
    for k in range(A):
        up, down = (pl.ds(0, n * Ck) for n in (k + 1, A - k))

        @pl.when((a == k) & (a + 1 < A))
        def _():
            wcopy(gat.at[up], gat.at[up], "g", 0, 0, pair).wait_send()

        @pl.when((a == k) & (a > 0))
        def _():
            wcopy(gat.at[down], gat.at[down], "g", 1, 0, pair).wait_send()

    for load in later:
        load.wait()


CORR1 = 1.0 - 0.9**STEP_NUM
CORR2 = 1.0 - 0.999**STEP_NUM


def adamw(weight, grad, moment, second, rate, decay):
    moment_new = 0.9 * moment + 0.1 * grad
    second_new = 0.999 * second + 0.001 * grad * grad
    step = moment_new / (jnp.sqrt(second_new) * (1.0 / math.sqrt(CORR2)) + 1e-08)
    new = weight * (1.0 - rate * decay) - (rate / CORR1) * step
    return moment_new, second_new, new


def update_kernel(resident, slots, C, names, *refs):
    r = SimpleNamespace(**dict(zip(names, refs)))
    if not resident:
        pairs = ((r.w1, r.w1f), (r.w1_m, r.m1), (r.w1_v, r.v1), (r.w2, r.w2f), (r.w2_m, r.m2), (r.w2_v, r.v2))
        loads = [pltpu.make_async_copy(src, dst, r.lsem.at[k]) for k, (src, dst) in enumerate(pairs)]
        for load in loads:
            load.start()
        for load in loads:
            load.wait()
    small = [pltpu.make_async_copy(src, r.asl.at[k], r.asem.at[k]) for k, src in enumerate((r.at, r.atm, r.atv))]
    for load in small:
        load.start()
    norm = r.scal[0:1, 2:3]
    clip = jnp.minimum(1.0, 0.1 / jnp.sqrt(norm))
    ring = (r.sm, r.sv, r.sn, r.sc)

    def copies(outs, slot, rows):
        return [pltpu.make_async_copy(buf.at[slot], out.at[rows], r.osem.at[slot, k]) for k, (buf, out) in enumerate(zip(ring, outs))]

    def chunk(grad, state, outs, k, ahead):
        w, m, v = state
        slot = lax.rem(k + ahead, slots)
        base = pl.multiple_of(k * C, C)
        rows = pl.ds(base, C)

        def drain():
            for copy in copies(outs, slot, rows):
                copy.wait()

        if ahead:
            drain()
        else:
            pl.when(k >= slots)(drain)

        def part(j, carry):
            src = pl.ds(pl.multiple_of(base + j * 16, 16), 16)
            dst = pl.ds(pl.multiple_of(j * 16, 16), 16)
            mn, vn, wn = adamw(w[src, :], clip * grad[src, :], m[src, :], v[src, :], 0.03, 0.01)
            r.sm[slot, dst, :] = mn
            r.sv[slot, dst, :] = vn
            r.sn[slot, dst, :] = wn
            r.sc[slot, dst, :] = wn.astype(BF)
            return carry

        lax.fori_loop(0, C // 16, part, 0, unroll=True)
        for copy in copies(outs, slot, rows):
            copy.start()

    outs1 = (r.m1o, r.v1o, r.n1o, r.c1o)
    outs2 = (r.m2o, r.v2o, r.n2o, r.c2o)
    count1, count2 = r.w1f.shape[0] // C, r.w2f.shape[0] // C

    def step2(k, carry):
        chunk(r.g2, (r.w2f, r.m2, r.v2), outs2, k, 0)
        return carry

    def step1(k, carry):
        chunk(r.gs, (r.w1f, r.m1, r.v1), outs1, k, count2)
        return carry

    lax.fori_loop(0, count2, step2, 0)
    r.gs[...] = r.gat[...].astype(F32) + dot(r.xbt[...], r.dpb[...])
    lax.fori_loop(0, count1, step1, 0)
    for load in small:
        load.wait()
    am, av, an = adamw(r.asl[0], clip * r.agrad[...], r.asl[1], r.asl[2], 0.2, 0.0)
    for k, v in enumerate((am, av, an)):
        r.ast[k] = v
    last = [pltpu.make_async_copy(r.ast.at[k], dst, r.asem.at[k]) for k, dst in enumerate((r.amo, r.avo, r.ano))]
    for copy in last:
        copy.start()
    for k in range(slots):
        for copy in copies(outs1, k, pl.ds(0, C)):
            copy.wait()
    for copy in last:
        copy.wait()


def on_device(
    data_x, data_group, batch_x, batch_group, batch_index, prec_index, prec_table, targets,
    omega, phase, prior_w, w1_master, w1_moment, w1_second, w2_master, w2_moment, w2_second,
    alpha, alpha_moment, alpha_second,
):
    W, N = lax.axis_size("wide"), lax.axis_size("narrow")
    A = W // 2
    R, D = data_x.shape
    brow, Bg, S = batch_x.shape[0], targets.shape[0], targets.shape[1]
    F, M = omega.shape
    Hn, Fn, Mn, H = w1_master.shape[1], w2_master.shape[1], M // N, w2_master.shape[0]
    B, Ck = W * Bg, D // 2 // A
    hbm, vmem, smem = (pl.BlockSpec(memory_space=m) for m in (pl.ANY, pltpu.VMEM, pltpu.SMEM))
    resident = B <= 128
    args = dict(
        data_x=(data_x, hbm), dgroup=(data_group.reshape(1, R), hbm), batch_x=(batch_x, hbm),
        bgroup=(batch_group, smem), bindex=(batch_index, smem), pindex=(prec_index, smem),
        ptable=(prec_table, smem), targets=(targets, hbm), omega=(omega, hbm),
        phase=(phase.reshape(1, M), hbm), prior_wt=(prior_w.T, hbm), w1=(w1_master, hbm),
        w2=(w2_master, hbm), alphat_own=(alpha.T, hbm),
    )
    state = dict(
        w1=(w1_master, hbm), w1_m=(w1_moment, hbm), w1_v=(w1_second, hbm),
        w2=(w2_master, hbm), w2_m=(w2_moment, hbm), w2_v=(w2_second, hbm),
    )
    outs = dict(
        scal=((8, 128), F32), agrad=((S, R), F32), gat=((D, Hn), BF), xbt=((D, B), BF), dpb=((B, Hn), BF),
        g2=((H, Fn), F32),
    )
    held = dict(
        w1f=((D, Hn), F32), m1=((D, Hn), F32), v1=((D, Hn), F32), w2f=((H, Fn), F32), m2=((H, Fn), F32), v2=((H, Fn), F32),
    )
    scratch = dict(
        xg=((N, R, D), BF), xT=((D, N * R), BF), hid=((N * R, Hn), BF), gd=((N * R, Hn), F32),
        dpre=((N * R, Hn), BF), pre=((R, Hn), F32), w1b=((D, Hn), BF),
        w2b=((H, Fn), BF), om=((Fn, M), BF), pwt=((S, Mn), F32),
        xbg=((Bg, D), F32), xbs=((brow, D), BF), tgs=((Bg, S), F32), dgs=((1, R), jnp.int32), als=((S, R), F32), ph=((1, Mn), F32), ges=((N, Bg, Hn), F32), zes=((N, Bg, Mn), F32), bfs=((Bg, Fn), F32), zf=((Ck, Hn), F32), us=((W, Bg, Hn), F32), ags=((N, S, R), F32),
        dhs=((N, B, Hn), BF), cz=((B, Mn), F32), sz=((Bg, Mn), F32), prior=((S, B), F32), gp=((B, Mn), F32),
        metat=((128, B), F32), alphat=((S, N * R), F32), pmask=((B, N * R), F32), amat=((B, N * R), F32),
        gmat=((B, Hn), BF), db=((2 * B, Fn), BF),
        psend=((A * Ck, Hn), BF), precv=((A * Ck, Hn), BF), zsend=((A, Ck, Hn), BF), zrecv=((A, Ck, Hn), BF),
        gb=((B, Hn), F32),
        meta=((W, Bg, 128), F32), xbw=((W, 2 * Bg, D // 2), BF), hgw=((W, 2 * Bg, Hn), BF),
        bfw=((W, 2 * Bg, Fn // 2), BF), gw=((W, 2 * Bg, Hn // 2), BF), kw=((W * N // 2, S, B), F32),
        ur=((W, Bg, Hn), F32), uz=((W, 2 * Bg, Hn), BF), nw=((W * N // 2, 8, 128), F32),
        xbn=((N, brow, D), F32), ad=((N, S + 8, R), F32), hbn=((N, 2 * Bg, Hn // 2), BF), ger=((N, Bg, Hn), F32), zer=((N, Bg, Mn), F32),
        kn=((2, S, B), F32), agr=((N, S, R), F32), uzn=((N, B, Hn + Mn), BF), hbx=((N, B, Hn), BF), dhr=((N, B, Hn), BF),
        nn=((2, 8, 128), F32),
    )
    if resident:
        args.update(state)
        outs.update(held)
    else:
        scratch.update(w1f=held["w1f"], w2f=held["w2f"])
    Q = max(1, min(4, Ck // 16))
    count = 2 * len(WIDE_EX + NARROW_EX + CHIP_EX)
    sems = [("lsem", 14), ("x_s", 12), ("x_r", 12), ("es", count), ("p_s", 1), ("p_r", A * Q), ("z_s", 1), ("z_r", 1)]
    sems += [("f_s", 1), ("f_r", 1), ("g_s", 2), ("g_r", 2 * A * Q)]
    names = [*args, *outs, *scratch] + [n for n, _ in sems]
    grads = pl.pallas_call(
        lambda *refs: step_kernel(W, N, resident, names, *refs),
        out_shape=[(pltpu.VMEM if resident else jax.ShapeDtypeStruct)(s, t) for s, t in outs.values()],
        in_specs=[spec for _, spec in args.values()],
        out_specs=[vmem] * len(outs),
        scratch_shapes=[pltpu.VMEM(s, t) for s, t in scratch.values()] + [pltpu.SemaphoreType.DMA((k,)) for _, k in sems],
        compiler_params=pltpu.CompilerParams(collective_id=0, has_side_effects=True, vmem_limit_bytes=(62 if not resident else 39) * 2**20),
        name="gradients",
    )(*[v for v, _ in args.values()])

    args2 = {k: (v, vmem) for k, v in zip(outs, grads)}
    args2.update(at=(alpha.T, hbm), atm=(alpha_moment.T, hbm), atv=(alpha_second.T, hbm))
    C, slots = 256, 3
    outs2 = dict(amo=((S, R), F32, hbm), avo=((S, R), F32, hbm), ano=((S, R), F32, hbm))
    for k, shape in (("1", (D, Hn)), ("2", (H, Fn))):
        outs2.update({"m" + k + "o": (shape, F32, hbm), "v" + k + "o": (shape, F32, hbm)})
        outs2.update({"n" + k + "o": (shape, F32, hbm), "c" + k + "o": (shape, BF, hbm)})
    scratch2 = dict(
        gs=pltpu.VMEM((D, Hn), F32), sm=pltpu.VMEM((slots, C, Hn), F32), sv=pltpu.VMEM((slots, C, Hn), F32),
        sn=pltpu.VMEM((slots, C, Hn), F32), sc=pltpu.VMEM((slots, C, Hn), BF), osem=pltpu.SemaphoreType.DMA((slots, 4)),
        asl=pltpu.VMEM((3, S, R), F32), ast=pltpu.VMEM((3, S, R), F32), asem=pltpu.SemaphoreType.DMA((3,)),
    )
    if not resident:
        args2.update(state)
        scratch2.update({k: pltpu.VMEM(s, t) for k, (s, t) in held.items()}, lsem=pltpu.SemaphoreType.DMA((6,)))
    names2 = [*args2, *outs2, *scratch2]
    new = pl.pallas_call(
        lambda *refs: update_kernel(resident, slots, C, names2, *refs),
        out_shape=[jax.ShapeDtypeStruct(s, t) for s, t, _ in outs2.values()],
        in_specs=[spec for _, spec in args2.values()],
        out_specs=[spec for _, _, spec in outs2.values()],
        scratch_shapes=list(scratch2.values()),
        compiler_params=pltpu.CompilerParams(vmem_limit_bytes=(36 if not resident else 10) * 2**20),
        name="adamw",
    )(*[v for v, _ in args2.values()])
    new = dict(zip(outs2, new))
    scal = grads[0]
    return (
        scal[0, 0], scal[0, 1], scal[0, 2],
        new["m1o"], new["v1o"], new["n1o"], new["c1o"],
        new["m2o"], new["v2o"], new["n2o"], new["c2o"],
        new["amo"].T, new["avo"].T, new["ano"].T,
    )


def solution(mesh):
    both = P(("wide", "narrow"))
    both2 = P(("wide", "narrow"), None)
    col = P(None, "narrow")
    return jax.shard_map(
        on_device,
        mesh=mesh,
        in_specs=(both2, both, both2, P("wide"), P("wide"), P("wide"), P(), P("wide", None), P(), P(), P())
        + (col,) * 6 + (both2,) * 3,
        out_specs=(P(), P(), P()) + (col,) * 8 + (both2,) * 3,
        check_vma=False,
    )
```

```python
import math
from types import SimpleNamespace

import jax
import jax.numpy as jnp
from jax import lax
from jax.experimental import pallas as pl
from jax.experimental.pallas import tpu as pltpu
from jax.sharding import PartitionSpec as P

STEP_NUM = 10
HIGH = lax.Precision.HIGHEST
MESH = pl.DeviceIdType.MESH
GC = math.sqrt(2.0 / math.pi)
F32 = jnp.float32
BF = jnp.bfloat16


def gelu_pair(pre):
    square = pre * pre
    t = jnp.tanh(pre * (GC + (GC * 0.044715) * square))
    half = 0.5 * (1.0 + t)
    slope = half + 0.5 * pre * (1.0 - t * t) * (GC + (3 * GC * 0.044715) * square)
    return pre * half, slope


def dot(left, right, dims=((1,), (0,)), precision=None):
    return lax.dot_general(left, right, (dims, ((), ())), precision=precision, preferred_element_type=F32)


NT = ((1,), (1,))
TN = ((0,), (0,))


class Exchange:
    def __init__(self, size, me, where, sems, k):
        self.size, self.me, self.where, self.sems, self.k = size, me, where, sems, k

    def copy(self, src, dst, p):
        return pltpu.make_async_remote_copy(
            src_ref=src, dst_ref=dst, send_sem=self.sems.at[self.k], recv_sem=self.sems.at[self.k + 1],
            device_id=self.where(p), device_id_type=MESH)

    def loop(self, body):
        def step(k, carry):
            body(lax.rem(self.me + k, self.size))
            return carry

        lax.fori_loop(1, self.size, step, 0)

    def greet(self, barrier):
        self.loop(lambda p: pl.semaphore_signal(barrier, inc=1, device_id=self.where(p), device_id_type=MESH))

    def gather(self, buf):
        self.loop(lambda p: self.copy(buf.at[self.me], buf.at[self.me], p).start())

    def scatter(self, src, buf):
        self.loop(lambda p: self.copy(src.at[p], buf.at[self.me], p).start())

    def all(self, buf):
        others = buf.at[pl.ds(0, self.size - 1)]
        return self.copy(others, others, lax.rem(self.me + 1, self.size))

    def wait(self, buf):
        self.all(buf).wait_recv()

    def drain(self, buf):
        self.all(buf).wait_send()


WIDE_EX = ("meta", "xbw", "hgw", "bfw", "gw", "szw", "ur", "uz")
NARROW_EX = ("xbn", "hbn", "ger", "zer", "agr", "hbx", "dhr")
CHIP_EX = ("kw", "nw")


def step_kernel(W, N, resident, names, *refs):
    r = SimpleNamespace(**dict(zip(names, refs)))
    wi, ni = lax.axis_index("wide"), lax.axis_index("narrow")
    A = W // 2
    a, b = wi // 2, lax.rem(wi, 2)
    pair = wi + 1 - 2 * b
    n1 = ni + 1 - 2 * lax.rem(ni, 2)
    n2 = lax.rem(ni + 2, N)
    n3 = lax.rem(n1 + 2, N)
    xg, hid, gd, xT, dpre = r.xg, r.hid, r.gd, r.xT, r.dpre
    w1b, w2b, om = r.w1b, r.w2b, r.om
    _, R, D = xg.shape
    Bg, S = r.targets.shape
    brow = r.batch_x.shape[0]
    Hn, Fn = w1b.shape[1], w2b.shape[1]
    H, F, M = w2b.shape[0], r.omega.shape[0], r.omega.shape[1]
    Mn = M // N
    B = W * Bg
    half = D // 2
    Ck = half // A
    scale = math.sqrt(2.0 / M)
    lsem = r.lsem
    core, side = lax.rem(ni, 2), ni // 2
    groups = (
        (WIDE_EX, W, wi, lambda p: {"wide": p}),
        (NARROW_EX, N, ni, lambda p: {"narrow": p}),
        (CHIP_EX, W * N // 2, wi * (N // 2) + side, lambda p: {"wide": p // (N // 2), "narrow": lax.rem(p, N // 2) * 2 + core}),
    )
    ex, live = SimpleNamespace(), []
    for group, size, me, where in groups:
        for name in group:
            vars(ex)[name] = Exchange(size, me, where, r.es, 2 * len(live))
            live.append(name)

    own_f = pl.ds(pl.multiple_of(ni * Fn, Fn), Fn)
    own_m = pl.ds(pl.multiple_of(ni * Mn, Mn), Mn)
    loads = [
        pltpu.make_async_copy(r.w1, r.w1f, lsem.at[0]),
        pltpu.make_async_copy(r.data_x, xg.at[ni], lsem.at[1]),
        pltpu.make_async_copy(r.w2, r.w2f, lsem.at[2]),
        pltpu.make_async_copy(r.omega.at[own_f], om, lsem.at[3]),
        pltpu.make_async_copy(r.prior_wt.at[:, own_m], r.pwt, lsem.at[4]),
        pltpu.make_async_copy(r.phase.at[:, own_m], r.ph, lsem.at[9]),
    ]
    small = [
        pltpu.make_async_copy(r.batch_x, r.xbs, lsem.at[10]),
        pltpu.make_async_copy(r.targets, r.tgs, lsem.at[11]),
        pltpu.make_async_copy(r.dgroup, r.dgs, lsem.at[12]),
        pltpu.make_async_copy(r.alphat_own, r.als, lsem.at[13]),
    ]
    for load in small[:1] + loads[:1] + small[1:] + loads[1:]:
        load.start()

    barrier = pltpu.get_barrier_semaphore()

    ex.kw.greet(barrier)
    ex.xbn.greet(barrier)
    small[0].wait()
    r.xbn[ni] = r.xbs[...].astype(F32)
    lane = lax.broadcasted_iota(jnp.int32, (1, 128), 1)
    for k in range(Bg):
        prec_k = r.ptable[r.pindex[k]]
        r.meta[wi, k : k + 1, :] = jnp.where(
            lane == 0, r.bgroup[k].astype(F32),
            jnp.where(lane == 1, r.bindex[k].astype(F32), jnp.where(lane == 2, prec_k, 0.0)))
    for load in small[1:]:
        load.wait()
    r.meta[wi, :, S : 2 * S] = r.tgs[...]
    r.ad[ni, 0:S, :] = r.als[...]
    r.ad[ni, S : S + 8, :] = jnp.broadcast_to(r.dgs[...].astype(F32), (8, R))

    pl.semaphore_wait(barrier, W * N // 2 - 1 + N - 1)

    def xcopy(src, dst, k, p):
        return pltpu.make_async_remote_copy(
            src_ref=src, dst_ref=dst, send_sem=r.x_s.at[k], recv_sem=r.x_r.at[k],
            device_id={"narrow": p}, device_id_type=MESH)

    cuts = (0, R * 4 // 16, R * 10 // 16, R)
    P = len(cuts) - 1

    def piece(k, src=None, slot=None):
        rows = pl.ds(cuts[k], cuts[k + 1] - cuts[k])
        slot = ni if slot is None else slot
        src = xg.at[slot, rows] if src is None else src.at[rows]
        return src, xg.at[slot, rows]

    def x_side():
        return xcopy(r.data_x, xg.at[ni], 0, n1)

    def x_over(k):
        return xcopy(*piece(k, r.data_x), 1 + k, n2)

    def x_pass(k):
        return xcopy(*piece(k, slot=n2), 1 + P + k, n1)

    ex.xbn.gather(r.xbn)
    x_over(0).start()
    ex.meta.gather(r.meta)

    def ad_copy(slot, k, p):
        return xcopy(r.ad.at[slot], r.ad.at[slot], 9 + k, p)

    ad_copy(ni, 1, n2).start()
    ad_copy(ni, 0, n1).start()

    loads[0].wait()

    def cast1(k, carry):
        rows = pl.ds(pl.multiple_of(k * 128, 128), 128)
        w1b[rows, :] = r.w1f[rows, :].astype(BF)
        return carry

    lax.fori_loop(0, D // 128, cast1, 0)
    ex.xbn.wait(r.xbn)
    for n in range(N):
        r.xbg[n * brow : (n + 1) * brow, :] = r.xbn[n]
    xbg = r.xbg[...]
    hb, gb = gelu_pair(dot(xbg.astype(BF), w1b[...]))
    hb = hb.astype(BF).astype(F32)
    r.hbn[ni] = jnp.concatenate([hb[:, : Hn // 2], hb[:, Hn // 2 :]], axis=0).astype(BF)
    ex.hbn.gather(r.hbn)
    x_over(1).start()
    x_side().start()
    r.hgw[wi] = jnp.concatenate([hb, gb], axis=0).astype(BF)
    ex.hgw.gather(r.hgw)
    r.xbw[wi] = jnp.concatenate([xbg[:, : D // 2], xbg[:, D // 2 :]], axis=0).astype(BF)
    ex.xbw.gather(r.xbw)
    loads[2].wait()

    def cast2(k, carry):
        rows = pl.ds(pl.multiple_of(k * 128, 128), 128)
        w2b[rows, :] = r.w2f[rows, :].astype(BF)
        return carry

    lax.fori_loop(0, H // 128, cast2, 0)

    def block(q, first=0, last=P):
        base = q * R + cuts[first]
        size = cuts[last] - cuts[first]
        r.pre[:size, :] = dot(xg[q, cuts[first] : cuts[last], :], w1b[...])
        step = math.gcd(size, 32)

        def part(k, carry):
            src = pl.ds(pl.multiple_of(k * step, step), step)
            dst = pl.ds(pl.multiple_of(base + k * step, step), step)
            out, slope = gelu_pair(r.pre[src, :])
            hid[dst, :] = out.astype(BF)
            gd[dst, :] = slope
            return carry

        lax.fori_loop(0, size // step, part, 0)

    def turn(q):
        xT[:, pl.ds(pl.multiple_of(q * R, R), R)] = xg[q].T

    ex.hbn.wait(r.hbn)
    hbn = [r.hbn[n].astype(F32) for n in range(N)]
    hid_g = jnp.concatenate([h[k * Bg : (k + 1) * Bg] for h in hbn for k in range(2)], axis=1).astype(BF)
    bfeat = dot(hid_g, w2b[...]).astype(BF)
    r.bfs[...] = bfeat.astype(F32)
    gpart = dot(bfeat, w2b[...], NT)
    for n in range(N):
        r.ges[n] = gpart[:, n * Hn : (n + 1) * Hn]
    ex.ger.scatter(r.ges, r.ger)
    r.ger[ni] = r.ges[ni]
    loads[3].wait()
    zpart = dot(r.bfs[...].astype(BF), om[...])
    for n in range(N):
        r.zes[n] = zpart[:, n * Mn : (n + 1) * Mn]
    ex.zer.scatter(r.zes, r.zer)
    r.zer[ni] = r.zes[ni]
    x_over(2).start()
    later = []
    if resident:
        pairs = ((r.w1_m, r.m1), (r.w1_v, r.v1), (r.w2_m, r.m2), (r.w2_v, r.v2))
        later = [pltpu.make_async_copy(src, dst, lsem.at[5 + k]) for k, (src, dst) in enumerate(pairs)]
    for load in later:
        load.start()
    bf32 = r.bfs[...]
    r.bfw[wi] = jnp.concatenate([bf32[:, : Fn // 2], bf32[:, Fn // 2 :]], axis=0).astype(BF)
    ex.bfw.gather(r.bfw)
    loads[1].wait()
    block(ni)
    ex.ger.wait(r.ger)
    gz = jnp.sum(r.ger[...], axis=0)
    r.gw[wi] = jnp.concatenate([gz[:, : Hn // 2], gz[:, Hn // 2 : Hn]], axis=0).astype(BF)
    ex.gw.gather(r.gw)
    for k in range(2):
        xcopy(*piece(k, slot=n2), 1 + k, n2).wait_recv()
        x_pass(k).start()
    ad_copy(n2, 1, n2).wait_recv()
    ad_copy(n2, 2, n1).start()
    ex.zer.wait(r.zer)
    own_b = pl.ds(pl.multiple_of(wi * Bg, Bg), Bg)
    loads[5].wait()
    angle = jnp.sum(r.zer[...], axis=0) + r.ph[...]
    r.cz[...] = jnp.zeros_like(r.cz)
    r.cz[own_b, :] = scale * jnp.cos(angle)
    sz = scale * jnp.sin(angle)
    r.szw[wi] = jnp.concatenate([sz[:, : Mn // 2], sz[:, Mn // 2 :]], axis=0).astype(BF)
    ex.szw.gather(r.szw)
    loads[4].wait()
    r.prior[...] = dot(r.pwt[...], r.cz[...], NT, HIGH)

    def x_last(k):
        xcopy(*piece(k, slot=n3), 1 + P + k, n1).wait_recv()

    xcopy(r.data_x, xg.at[n1], 0, n1).wait_recv()
    block(n1)
    block(n2, 0, 2)
    x_last(0)
    x_last(1)
    block(n3, 0, 2)
    ex.meta.wait(r.meta)
    meta = r.meta[...].reshape(B, 128)
    r.metat[...] = meta.T
    ad_copy(n1, 0, n1).wait_recv()
    ad_copy(n3, 2, n1).wait_recv()
    alphat = jnp.concatenate([r.ad[n, 0:S, :] for n in range(N)], axis=1)
    r.alphat[...] = alphat
    group = jnp.concatenate([r.ad[n, S : S + 1, :] for n in range(N)], axis=1)
    pmask = (0.5 + (meta[:, 0:1] == group).astype(F32)) / F
    r.pmask[...] = pmask
    col = lax.broadcasted_iota(jnp.int32, (1, N * R), 1) + wi * (N * R)
    first = (ni == 0).astype(F32)
    r.amat[...] = jnp.where(meta[:, 1:2] == col.astype(F32), first / meta[:, 2:3], 0.0)
    turn(ni)
    turn(n1)
    xcopy(*piece(2, slot=n2), 3, n2).wait_recv()
    x_pass(2).start()
    block(n2, 2, 3)
    x_last(2)
    block(n3, 2, 3)

    ex.gw.wait(r.gw)
    gw = r.gw[...].astype(F32)
    gmat = jnp.concatenate([gw[:, :Bg].reshape(B, Hn // 2), gw[:, Bg:].reshape(B, Hn // 2)], axis=1).astype(BF)
    r.gmat[...] = gmat
    amat = r.pmask[...] * dot(gmat, hid[...], NT) + r.amat[...]
    r.amat[...] = amat
    kal = dot(r.alphat[...], amat, NT, HIGH) + r.prior[...]
    fold = max(1, min(S // 8, 128 // B))
    r.kn[core] = jnp.concatenate([kal[k * (S // fold) : (k + 1) * (S // fold)] for k in range(fold)], axis=1)

    def core_copy(buf, k):
        return xcopy(buf.at[core], buf.at[core], 12 + k, n1)

    def core_sum(buf, k):
        xcopy(buf.at[1 - core], buf.at[1 - core], 12 + k, n1).wait_recv()
        return buf[0] + buf[1]

    core_copy(r.kn, 0).start()
    chip = wi * (N // 2) + side
    r.kw[chip] = core_sum(r.kn, 0)
    ex.kw.gather(r.kw)
    turn(n2)
    turn(n3)
    ex.hgw.wait(r.hgw)
    hg = r.hgw[...].astype(F32)
    r.hbx[ni] = hg[:, :Bg].reshape(B, Hn).astype(BF)
    r.gb[...] = hg[:, Bg:].reshape(B, Hn)
    ex.hbx.gather(r.hbx)
    ex.xbw.wait(r.xbw)
    xbw = r.xbw[...].astype(F32)
    r.xbt[...] = jnp.concatenate([xbw[:, :Bg].reshape(B, D // 2), xbw[:, Bg:].reshape(B, D // 2)], axis=1).T.astype(BF)
    ex.kw.wait(r.kw)
    prec = r.metat[2:3, :]
    kal = jnp.sum(r.kw[...], axis=0)
    resid = r.metat[S : 2 * S, :] - jnp.concatenate([kal[:, k * B : (k + 1) * B] for k in range(fold)], axis=0)
    total = jnp.sum(prec, axis=1, keepdims=True)
    loss = 0.5 * jnp.sum(jnp.sum(prec * (resid * resid), axis=1, keepdims=True), axis=0, keepdims=True)
    grt = prec * resid / total

    ds = (-r.pmask[...] * dot(grt, r.alphat[...], TN, HIGH)).astype(BF)
    upart = dot(ds, hid[...]).reshape(W, Bg, Hn)
    r.us[...] = jnp.concatenate([upart[:, :, : Hn // 2], upart[:, :, Hn // 2 :]], axis=1).astype(BF)
    ex.ur.scatter(r.us, r.ur)
    for q in range(N):
        rows = slice(q * R, (q + 1) * R)
        dpre[rows, :] = (dot(ds[:, rows], r.gmat[...], TN) * gd[rows, :]).astype(BF)

    def wcopy(src, dst, kind, k, slot, p):
        return pltpu.make_async_remote_copy(
            src_ref=src, dst_ref=dst, send_sem=getattr(r, kind + "_s").at[k], recv_sem=getattr(r, kind + "_r").at[slot],
            device_id={"wide": p}, device_id_type=MESH)

    psend, precv, zsend, zrecv, gat = r.psend, r.precv, r.zsend, r.zrecv, r.gat

    NH = 2 if Ck % 32 == 0 else 1
    Hk = Ck // NH
    Q = 2 if Hk % 32 == 0 else 1
    Cq = Hk // Q

    def grad_rows(row):
        return dot(xT[pl.ds(pl.multiple_of(row, Hk), Hk), :], dpre[...])

    def target(step):
        low = a // (A // 2)
        m = a + low * (A - 1 - 2 * a)
        single = A - 1 - 2 * m
        late = (step // single + A - 1) // A
        e = step - single
        t = (1 - late) * (A - 1 - step) + late * (m + (1 - lax.rem(e + 2 * A, 2) * 2) * (m - (e + 2 * A) // 2 + A))
        return t + low * (A - 1 - 2 * t)

    def pcopy(ap, h, q):
        rows = pl.ds(pl.multiple_of(ap * Ck + h * Hk + q * Cq, Cq), Cq)
        return wcopy(psend.at[rows], precv.at[rows], "p", 0, ap * NH * Q + h * Q + q, pair)

    def pair_chunk(h, ap):
        base = ap * Ck + h * Hk
        psend[pl.ds(pl.multiple_of(base, Hk), Hk), :] = grad_rows((1 - b) * half + base).astype(BF)
        for q in range(Q):
            pcopy(ap, h, q).start()

    def pair_sends(h, first, last):
        def send(step, carry):
            pair_chunk(h, target(step))
            return carry

        lax.fori_loop(min(first, A - 1), min(last, A - 1), send, 0)
        if last >= A:
            pair_chunk(h, a)

    def zcopy(ap, h, q):
        rows = pl.ds(h * Hk + q * Cq, Cq)
        return wcopy(zsend.at[ap, rows], zrecv.at[a, rows], "z", 0, h, 2 * ap + b)

    def z_part(ap, h, q):
        pcopy(ap, h, q).wait_recv()
        rows = pl.ds(pl.multiple_of(ap * Ck + h * Hk + q * Cq, Cq), Cq)
        return r.zt[q * Cq : (q + 1) * Cq, :] + precv[rows, :].astype(F32)

    def z_sends(h, first, last):
        def send(step, carry):
            ap = target(step)
            r.zt[...] = grad_rows(b * half + ap * Ck + h * Hk)
            for q in range(Q):
                zsend[ap, h * Hk + q * Cq : h * Hk + (q + 1) * Cq, :] = z_part(ap, h, q).astype(BF)
                zcopy(ap, h, q).start()
            return carry

        lax.fori_loop(min(first, A - 1), min(last, A - 1), send, 0)

    def z_own(h):
        r.zt[...] = grad_rows(b * half + a * Ck + h * Hk)
        for q in range(Q):
            r.zf[h * Hk + q * Cq : h * Hk + (q + 1) * Cq, :] = z_part(a, h, q)

    pair_sends(0, 0, 2)

    agt = -dot(grt, r.amat[...], precision=HIGH)
    for n in range(N):
        r.ags[n] = agt[:, n * R : (n + 1) * R]
    ex.agr.scatter(r.ags, r.agr)
    r.agr[ni] = r.ags[ni]
    ex.szw.wait(r.szw)

    def unfold(buf):
        v = buf[...].astype(F32)
        return jnp.concatenate([v[:, :Bg].reshape(B, -1), v[:, Bg:].reshape(B, -1)], axis=1)

    r.uzn[ni, :, Hn:] = (unfold(r.szw) * dot(grt, r.pwt[...], TN, HIGH)).astype(BF)
    ex.ur.wait(r.ur)
    r.ur[wi] = r.us[wi]
    r.uz[wi] = jnp.sum(r.ur[...].astype(F32), axis=0).astype(BF)
    ex.uz.gather(r.uz)
    pair_sends(0, 2, A)
    z_sends(0, 0, 1)
    for h in range(1, NH):
        pair_sends(h, 0, A)
    z_sends(0, 1, 2)
    ex.bfw.wait(r.bfw)
    ex.uz.wait(r.uz)
    r.uzn[ni, :, :Hn] = unfold(r.uz).astype(BF)

    def u_copy(slot, k, p):
        return xcopy(r.uzn.at[slot], r.uzn.at[slot], 14 + k, p)

    u_copy(ni, 1, n2).start()
    u_copy(ni, 0, n1).start()
    z_sends(0, 2, A)
    z_own(0)

    others = pl.ds(0, A - 1)
    mine = b * A + a

    def shard(slot, h=0, q=0, count=Ck):
        return pl.ds(pl.multiple_of(slot * Ck + h * Hk + q * Cq, min(count, Cq)), count)

    def fcopy(ap, h, q):
        rows = shard(b * A + ap, h, q, Cq)
        return wcopy(gat.at[rows], gat.at[rows], "f", 0, 0, pair)

    def gcopy(ap, h, q, way):
        rows = shard(b * A + ap, h, q, Cq)
        k = ap if way > 0 else A + ap
        return wcopy(gat.at[rows], gat.at[rows], "g", 0 if way > 0 else 1, (k * NH + h) * Q + q, 2 * (a + way) + b)

    def straight(h):
        return h > 0

    def gdirect(ap, h, q):
        rows = shard(mine, h, q, Cq)
        k = a + (1 - (ap - a + A) // (A + 1)) * A
        return wcopy(gat.at[rows], gat.at[rows], "g", 2, (k * NH + h) * Q + q, 2 * ap + b)

    def z_done(h):
        rows = slice(h * Hk, (h + 1) * Hk)
        part = pl.ds(h * Hk, Hk)
        wcopy(zsend.at[others, part], zrecv.at[others, part], "z", 0, h, pair).wait_recv()

        def gain(k, carry):
            r.zf[rows, :] = r.zf[rows, :] + zrecv[lax.rem(a + k, A), rows, :].astype(F32)
            return carry

        lax.fori_loop(1, A, gain, 0)
        gat[shard(mine, h, 0, Hk), :] = r.zf[rows, :].astype(BF)
        for q in range(Q):
            fcopy(a, h, q).start()
        if straight(h):

            def send(step, carry):
                for q in range(Q):
                    gdirect(target(step), h, q).start()
                return carry

            lax.fori_loop(0, A - 1, send, 0)
        else:
            for q in range(Q):

                @pl.when(a + 1 < A)
                def _():
                    gcopy(a, h, q, 1).start()

                @pl.when(a > 0)
                def _():
                    gcopy(a, h, q, -1).start()

    def g_pass(h, first, last):
        def step(k, carry):
            below, above = a - 1 - k // Q, a + 1 + k // Q
            q = lax.rem(k, Q)

            @pl.when(below >= 0)
            def _():
                gcopy(below, h, q, 1).wait_recv()

                if not straight(h):

                    @pl.when(a + 1 < A)
                    def _():
                        gcopy(below, h, q, 1).start()

                fcopy(below, h, q).start()

            @pl.when(above < A)
            def _():
                gcopy(above, h, q, -1).wait_recv()

                if not straight(h):

                    @pl.when(a > 0)
                    def _():
                        gcopy(above, h, q, -1).start()

                fcopy(above, h, q).start()

            return carry

        lax.fori_loop(min(first, A - 1) * Q, min(last, A - 1) * Q, step, 0)

    if NH > 1:
        z_sends(1, 0, 1)
    z_done(0)
    u_copy(n2, 1, n2).wait_recv()
    u_copy(n2, 2, n1).start()
    if NH > 1:
        z_sends(1, 1, A)
        z_own(1)
    g_pass(0, 0, 1)
    u_copy(n1, 0, n1).wait_recv()
    u_copy(n3, 2, n1).wait_recv()
    acc = jnp.zeros((B, Fn), F32)
    for n in range(N):
        acc = acc + dot(r.uzn[n, :, :Hn], w2b[n * Hn : (n + 1) * Hn, :])
        acc = acc + dot(r.uzn[n, :, Hn:], om[:, n * Mn : (n + 1) * Mn], NT)
    r.db[...] = jnp.concatenate([acc, unfold(r.bfw)], axis=0).astype(BF)
    for n in range(N):
        r.dhs[n] = dot(r.db[:B, :], w2b[n * Hn : (n + 1) * Hn, :], NT).astype(BF)
    ex.dhr.scatter(r.dhs, r.dhr)
    r.dhr[ni] = r.dhs[ni]
    if NH > 1:
        z_done(1)
    g_pass(0, 1, 2)

    def two(v):
        return jnp.sum(jnp.sum(v * v, axis=1, keepdims=True), axis=0, keepdims=True)

    square = jnp.zeros((1, 1), F32)
    for n in range(N):
        if n == 0:
            ex.hbx.wait(r.hbx)
        hu = jnp.concatenate([r.hbx[n], r.uzn[n, :, :Hn]], axis=0)
        g2 = dot(hu, r.db[...], TN)
        r.g2[n * Hn : (n + 1) * Hn, :] = g2
        square = square + two(g2)

    ex.agr.wait(r.agr)
    agt = jnp.sum(r.agr[...], axis=0)
    r.agrad[...] = agt
    ex.dhr.wait(r.dhr)
    r.dpb[...] = (jnp.sum(r.dhr[...].astype(F32), axis=0) * r.gb[...]).astype(BF)

    square = square * (1.0 / W) + two(r.zf[...] + dot(r.xbt[shard(mine), :], r.dpb[...])) + two(agt)
    r.nn[core] = jnp.broadcast_to(square, (8, 128))
    core_copy(r.nn, 1).start()
    g_pass(0, 2, A)
    r.nw[chip] = core_sum(r.nn, 1)
    ex.nw.gather(r.nw)
    if NH > 1:
        g_pass(1, 0, A)
    ex.nw.wait(r.nw)
    norm = jnp.sum(r.nw[...], axis=0)
    lanes = lax.broadcasted_iota(jnp.int32, (8, 128), 1)
    r.scal[...] = jnp.where(lanes == 0, loss, jnp.where(lanes == 1, total, norm))

    theirs = pl.ds(pl.multiple_of((1 - b) * half, half), half)
    ours = pl.ds(pl.multiple_of(b * half, half), half)
    wcopy(gat.at[theirs], gat.at[theirs], "f", 0, 0, pair).wait_recv()

    for name in live:
        vars(ex)[name].drain(getattr(r, name))
    x_side().wait_send()
    for k in range(P):
        x_over(k).wait_send()
        x_pass(k).wait_send()
    for slot, k, p in ((ni, 0, n1), (ni, 1, n2), (n2, 2, n1)):
        ad_copy(slot, k, p).wait_send()
        u_copy(slot, k, p).wait_send()
    core_copy(r.kn, 0).wait_send()
    core_copy(r.nn, 1).wait_send()
    wcopy(psend, precv, "p", 0, 0, pair).wait_send()
    wcopy(gat.at[ours], gat.at[ours], "f", 0, 0, pair).wait_send()
    wcopy(zsend.at[others], zrecv.at[others], "z", 0, 0, pair).wait_send()
    if NH > 1:
        direct = pl.ds(0, (A - 1) * Hk)
        wcopy(gat.at[direct], gat.at[direct], "g", 2, 0, pair).wait_send()
    for k in range(A):
        up, down = (pl.ds(0, n * Hk) for n in (k + 1, A - k))

        @pl.when((a == k) & (a + 1 < A))
        def _():
            wcopy(gat.at[up], gat.at[up], "g", 0, 0, pair).wait_send()

        @pl.when((a == k) & (a > 0))
        def _():
            wcopy(gat.at[down], gat.at[down], "g", 1, 0, pair).wait_send()

    for load in later:
        load.wait()


CORR1 = 1.0 - 0.9**STEP_NUM
CORR2 = 1.0 - 0.999**STEP_NUM


def adamw(weight, grad, moment, second, rate, decay):
    moment_new = 0.9 * moment + 0.1 * grad
    second_new = 0.999 * second + 0.001 * grad * grad
    step = moment_new / (jnp.sqrt(second_new) * (1.0 / math.sqrt(CORR2)) + 1e-08)
    new = weight * (1.0 - rate * decay) - (rate / CORR1) * step
    return moment_new, second_new, new


def update_kernel(resident, slots, C, names, *refs):
    r = SimpleNamespace(**dict(zip(names, refs)))
    if not resident:
        pairs = ((r.w1, r.w1f), (r.w1_m, r.m1), (r.w1_v, r.v1), (r.w2, r.w2f), (r.w2_m, r.m2), (r.w2_v, r.v2))
        loads = [pltpu.make_async_copy(src, dst, r.lsem.at[k]) for k, (src, dst) in enumerate(pairs)]
        for load in loads:
            load.start()
        for load in loads:
            load.wait()
    small = [pltpu.make_async_copy(src, r.asl.at[k], r.asem.at[k]) for k, src in enumerate((r.at, r.atm, r.atv))]
    for load in small:
        load.start()
    norm = r.scal[0:1, 2:3]
    clip = jnp.minimum(1.0, 0.1 / jnp.sqrt(norm))
    ring = (r.sm, r.sv, r.sn, r.sc)

    def copies(outs, slot, rows):
        return [pltpu.make_async_copy(buf.at[slot], out.at[rows], r.osem.at[slot, k]) for k, (buf, out) in enumerate(zip(ring, outs))]

    def chunk(grad, state, outs, k, ahead):
        w, m, v = state
        slot = lax.rem(k + ahead, slots)
        base = pl.multiple_of(k * C, C)
        rows = pl.ds(base, C)

        def drain():
            for copy in copies(outs, slot, rows):
                copy.wait()

        if ahead:
            drain()
        else:
            pl.when(k >= slots)(drain)

        def part(j, carry):
            src = pl.ds(pl.multiple_of(base + j * 16, 16), 16)
            dst = pl.ds(pl.multiple_of(j * 16, 16), 16)
            mn, vn, wn = adamw(w[src, :], clip * grad[src, :], m[src, :], v[src, :], 0.03, 0.01)
            r.sm[slot, dst, :] = mn
            r.sv[slot, dst, :] = vn
            r.sn[slot, dst, :] = wn
            r.sc[slot, dst, :] = wn.astype(BF)
            return carry

        lax.fori_loop(0, C // 16, part, 0, unroll=True)
        for copy in copies(outs, slot, rows):
            copy.start()

    outs1 = (r.m1o, r.v1o, r.n1o, r.c1o)
    outs2 = (r.m2o, r.v2o, r.n2o, r.c2o)
    count1, count2 = r.w1f.shape[0] // C, r.w2f.shape[0] // C

    def step2(k, carry):
        chunk(r.g2, (r.w2f, r.m2, r.v2), outs2, k, 0)
        return carry

    def step1(k, carry):
        chunk(r.gs, (r.w1f, r.m1, r.v1), outs1, k, count2)
        return carry

    lax.fori_loop(0, count2, step2, 0)
    r.gs[...] = r.gat[...].astype(F32) + dot(r.xbt[...], r.dpb[...])
    lax.fori_loop(0, count1, step1, 0)
    for load in small:
        load.wait()
    am, av, an = adamw(r.asl[0], clip * r.agrad[...], r.asl[1], r.asl[2], 0.2, 0.0)
    for k, v in enumerate((am, av, an)):
        r.ast[k] = v
    last = [pltpu.make_async_copy(r.ast.at[k], dst, r.asem.at[k]) for k, dst in enumerate((r.amo, r.avo, r.ano))]
    for copy in last:
        copy.start()
    for k in range(slots):
        for copy in copies(outs1, k, pl.ds(0, C)):
            copy.wait()
    for copy in last:
        copy.wait()


def on_device(
    data_x, data_group, batch_x, batch_group, batch_index, prec_index, prec_table, targets,
    omega, phase, prior_w, w1_master, w1_moment, w1_second, w2_master, w2_moment, w2_second,
    alpha, alpha_moment, alpha_second,
):
    W, N = lax.axis_size("wide"), lax.axis_size("narrow")
    A = W // 2
    R, D = data_x.shape
    brow, Bg, S = batch_x.shape[0], targets.shape[0], targets.shape[1]
    F, M = omega.shape
    Hn, Fn, Mn, H = w1_master.shape[1], w2_master.shape[1], M // N, w2_master.shape[0]
    B, Ck = W * Bg, D // 2 // A
    hbm, vmem, smem = (pl.BlockSpec(memory_space=m) for m in (pl.ANY, pltpu.VMEM, pltpu.SMEM))
    resident = B <= 128
    fold = max(1, min(S // 8, 128 // B))
    args = dict(
        data_x=(data_x, hbm), dgroup=(data_group.reshape(1, R), hbm), batch_x=(batch_x, hbm),
        bgroup=(batch_group, smem), bindex=(batch_index, smem), pindex=(prec_index, smem),
        ptable=(prec_table, smem), targets=(targets, hbm), omega=(omega, hbm),
        phase=(phase.reshape(1, M), hbm), prior_wt=(prior_w.T, hbm), w1=(w1_master, hbm),
        w2=(w2_master, hbm), alphat_own=(alpha.T, hbm),
    )
    state = dict(
        w1=(w1_master, hbm), w1_m=(w1_moment, hbm), w1_v=(w1_second, hbm),
        w2=(w2_master, hbm), w2_m=(w2_moment, hbm), w2_v=(w2_second, hbm),
    )
    outs = dict(
        scal=((8, 128), F32), agrad=((S, R), F32), gat=((D, Hn), BF), xbt=((D, B), BF), dpb=((B, Hn), BF),
        g2=((H, Fn), F32),
    )
    held = dict(
        w1f=((D, Hn), F32), m1=((D, Hn), F32), v1=((D, Hn), F32), w2f=((H, Fn), F32), m2=((H, Fn), F32), v2=((H, Fn), F32),
    )
    scratch = dict(
        xg=((N, R, D), BF), xT=((D, N * R), BF), hid=((N * R, Hn), BF), gd=((N * R, Hn), F32),
        dpre=((N * R, Hn), BF), pre=((R, Hn), F32), w1b=((D, Hn), BF),
        w2b=((H, Fn), BF), om=((Fn, M), BF), pwt=((S, Mn), F32),
        xbg=((Bg, D), F32), xbs=((brow, D), BF), tgs=((Bg, S), F32), dgs=((1, R), jnp.int32), als=((S, R), F32), ph=((1, Mn), F32), ges=((N, Bg, Hn), F32), zes=((N, Bg, Mn), F32), bfs=((Bg, Fn), F32), zf=((Ck, Hn), F32), zt=((Ck // (2 if Ck % 32 == 0 else 1), Hn), F32), us=((W, 2 * Bg, Hn // 2), BF), ags=((N, S, R), F32),
        dhs=((N, B, Hn), BF), cz=((B, Mn), F32), prior=((S, B), F32),
        metat=((128, B), F32), alphat=((S, N * R), F32), pmask=((B, N * R), F32), amat=((B, N * R), F32),
        gmat=((B, Hn), BF), db=((2 * B, Fn), BF),
        psend=((A * Ck, Hn), BF), precv=((A * Ck, Hn), BF), zsend=((A, Ck, Hn), BF), zrecv=((A + 1, Ck, Hn), BF),
        gb=((B, Hn), F32),
        meta=((W, Bg, 128), F32), xbw=((W, 2 * Bg, D // 2), BF), hgw=((W, 2 * Bg, Hn), BF),
        bfw=((W, 2 * Bg, Fn // 2), BF), gw=((W, 2 * Bg, Hn // 2), BF), kw=((W * N // 2, S // fold, fold * B), F32),
        ur=((W, 2 * Bg, Hn // 2), BF), uz=((W, 2 * Bg, Hn // 2), BF), szw=((W, 2 * Bg, Mn // 2), BF), nw=((W * N // 2, 8, 128), F32),
        xbn=((N, brow, D), F32), ad=((N, S + 8, R), F32), hbn=((N, 2 * Bg, Hn // 2), BF), ger=((N, Bg, Hn), F32), zer=((N, Bg, Mn), F32),
        kn=((2, S // fold, fold * B), F32), agr=((N, S, R), F32), uzn=((N, B, Hn + Mn), BF), hbx=((N, B, Hn), BF), dhr=((N, B, Hn), BF),
        nn=((2, 8, 128), F32),
    )
    if resident:
        args.update(state)
        outs.update(held)
    else:
        scratch.update(w1f=held["w1f"], w2f=held["w2f"])
    pieces = A * math.gcd(Ck // 16, 4)
    count = 2 * len(WIDE_EX + NARROW_EX + CHIP_EX)
    sems = [("lsem", 14), ("x_s", 17), ("x_r", 17), ("es", count), ("p_s", 1), ("p_r", pieces), ("z_s", 1), ("z_r", pieces + pieces // A)]
    sems += [("f_s", 1), ("f_r", 1), ("g_s", 3), ("g_r", 2 * pieces)]
    names = [*args, *outs, *scratch] + [n for n, _ in sems]
    grads = pl.pallas_call(
        lambda *refs: step_kernel(W, N, resident, names, *refs),
        out_shape=[(pltpu.VMEM if resident else jax.ShapeDtypeStruct)(s, t) for s, t in outs.values()],
        in_specs=[spec for _, spec in args.values()],
        out_specs=[vmem] * len(outs),
        scratch_shapes=[pltpu.VMEM(s, t) for s, t in scratch.values()] + [pltpu.SemaphoreType.DMA((k,)) for _, k in sems],
        compiler_params=pltpu.CompilerParams(collective_id=0, has_side_effects=True, vmem_limit_bytes=(62 if not resident else 39) * 2**20),
        name="gradients",
    )(*[v for v, _ in args.values()])

    args2 = {k: (v, vmem) for k, v in zip(outs, grads)}
    args2.update(at=(alpha.T, hbm), atm=(alpha_moment.T, hbm), atv=(alpha_second.T, hbm))
    C, slots = 256, 3
    outs2 = dict(amo=((S, R), F32, hbm), avo=((S, R), F32, hbm), ano=((S, R), F32, hbm))
    for k, shape in (("1", (D, Hn)), ("2", (H, Fn))):
        outs2.update({"m" + k + "o": (shape, F32, hbm), "v" + k + "o": (shape, F32, hbm)})
        outs2.update({"n" + k + "o": (shape, F32, hbm), "c" + k + "o": (shape, BF, hbm)})
    scratch2 = dict(
        gs=pltpu.VMEM((D, Hn), F32), sm=pltpu.VMEM((slots, C, Hn), F32), sv=pltpu.VMEM((slots, C, Hn), F32),
        sn=pltpu.VMEM((slots, C, Hn), F32), sc=pltpu.VMEM((slots, C, Hn), BF), osem=pltpu.SemaphoreType.DMA((slots, 4)),
        asl=pltpu.VMEM((3, S, R), F32), ast=pltpu.VMEM((3, S, R), F32), asem=pltpu.SemaphoreType.DMA((3,)),
    )
    if not resident:
        args2.update(state)
        scratch2.update({k: pltpu.VMEM(s, t) for k, (s, t) in held.items()}, lsem=pltpu.SemaphoreType.DMA((6,)))
    names2 = [*args2, *outs2, *scratch2]
    new = pl.pallas_call(
        lambda *refs: update_kernel(resident, slots, C, names2, *refs),
        out_shape=[jax.ShapeDtypeStruct(s, t) for s, t, _ in outs2.values()],
        in_specs=[spec for _, spec in args2.values()],
        out_specs=[spec for _, _, spec in outs2.values()],
        scratch_shapes=list(scratch2.values()),
        compiler_params=pltpu.CompilerParams(vmem_limit_bytes=(36 if not resident else 10) * 2**20),
        name="adamw",
    )(*[v for v, _ in args2.values()])
    new = dict(zip(outs2, new))
    scal = grads[0]
    return (
        scal[0, 0], scal[0, 1], scal[0, 2],
        new["m1o"], new["v1o"], new["n1o"], new["c1o"],
        new["m2o"], new["v2o"], new["n2o"], new["c2o"],
        new["amo"].T, new["avo"].T, new["ano"].T,
    )


def solution(mesh):
    both = P(("wide", "narrow"))
    both2 = P(("wide", "narrow"), None)
    col = P(None, "narrow")
    return jax.shard_map(
        on_device,
        mesh=mesh,
        in_specs=(both2, both, both2, P("wide"), P("wide"), P("wide"), P(), P("wide", None), P(), P(), P())
        + (col,) * 6 + (both2,) * 3,
        out_specs=(P(), P(), P()) + (col,) * 8 + (both2,) * 3,
        check_vma=False,
    )
```

```python
import math
from types import SimpleNamespace

import jax
import jax.numpy as jnp
from jax import lax
from jax.experimental import pallas as pl
from jax.experimental.pallas import tpu as pltpu
from jax.sharding import PartitionSpec as P

STEP_NUM = 10
HIGH = lax.Precision.HIGHEST
MESH = pl.DeviceIdType.MESH
GC = math.sqrt(2.0 / math.pi)
F32 = jnp.float32
BF = jnp.bfloat16


def gelu_pair(pre):
    square = pre * pre
    t = jnp.tanh(pre * (GC + (GC * 0.044715) * square))
    half = 0.5 * (1.0 + t)
    slope = half + 0.5 * pre * (1.0 - t * t) * (GC + (3 * GC * 0.044715) * square)
    return pre * half, slope


def dot(left, right, dims=((1,), (0,)), precision=None):
    return lax.dot_general(left, right, (dims, ((), ())), precision=precision, preferred_element_type=F32)


NT = ((1,), (1,))
TN = ((0,), (0,))


class Exchange:
    def __init__(self, size, me, where, sems, k):
        self.size, self.me, self.where, self.sems, self.k = size, me, where, sems, k

    def copy(self, src, dst, p):
        return pltpu.make_async_remote_copy(
            src_ref=src, dst_ref=dst, send_sem=self.sems.at[self.k], recv_sem=self.sems.at[self.k + 1],
            device_id=self.where(p), device_id_type=MESH)

    def loop(self, body):
        def step(k, carry):
            body(lax.rem(self.me + k, self.size))
            return carry

        lax.fori_loop(1, self.size, step, 0)

    def greet(self, barrier):
        self.loop(lambda p: pl.semaphore_signal(barrier, inc=1, device_id=self.where(p), device_id_type=MESH))

    def gather(self, buf):
        self.loop(lambda p: self.copy(buf.at[self.me], buf.at[self.me], p).start())

    def scatter(self, src, buf):
        self.loop(lambda p: self.copy(src.at[p], buf.at[self.me], p).start())

    def all(self, buf):
        others = buf.at[pl.ds(0, self.size - 1)]
        return self.copy(others, others, lax.rem(self.me + 1, self.size))

    def wait(self, buf):
        self.all(buf).wait_recv()

    def drain(self, buf):
        self.all(buf).wait_send()


WIDE_EX = ("meta", "xbw", "hgw", "bfw", "gw", "szw", "ur", "uz")
NARROW_EX = ("xbn", "hbn", "ger", "zer", "agr", "hbx", "dhr")
CHIP_EX = ("kw", "nw")


def step_kernel(W, N, resident, names, *refs):
    r = SimpleNamespace(**dict(zip(names, refs)))
    wi, ni = lax.axis_index("wide"), lax.axis_index("narrow")
    A = W // 2
    a, b = wi // 2, lax.rem(wi, 2)
    pair = wi + 1 - 2 * b
    n1 = ni + 1 - 2 * lax.rem(ni, 2)
    n2 = lax.rem(ni + 2, N)
    n3 = lax.rem(n1 + 2, N)
    xg, hid, gd, xT, dpre = r.xg, r.hid, r.gd, r.xT, r.dpre
    w1b, w2b, om = r.w1b, r.w2b, r.om
    _, R, D = xg.shape
    Bg, S = r.targets.shape
    brow = r.batch_x.shape[0]
    Hn, Fn = w1b.shape[1], w2b.shape[1]
    H, F, M = w2b.shape[0], r.omega.shape[0], r.omega.shape[1]
    Mn = M // N
    B = W * Bg
    half = D // 2
    Ck = half // A
    scale = math.sqrt(2.0 / M)
    lsem = r.lsem
    core, side = lax.rem(ni, 2), ni // 2
    groups = (
        (WIDE_EX, W, wi, lambda p: {"wide": p}),
        (NARROW_EX, N, ni, lambda p: {"narrow": p}),
        (CHIP_EX, W * N // 2, wi * (N // 2) + side, lambda p: {"wide": p // (N // 2), "narrow": lax.rem(p, N // 2) * 2 + core}),
    )
    ex, live = SimpleNamespace(), []
    for group, size, me, where in groups:
        for name in group:
            vars(ex)[name] = Exchange(size, me, where, r.es, 2 * len(live))
            live.append(name)

    own_f = pl.ds(pl.multiple_of(ni * Fn, Fn), Fn)
    own_m = pl.ds(pl.multiple_of(ni * Mn, Mn), Mn)
    loads = [
        pltpu.make_async_copy(r.w1, r.w1f, lsem.at[0]),
        pltpu.make_async_copy(r.data_x, xg.at[ni], lsem.at[1]),
        pltpu.make_async_copy(r.w2, r.w2f, lsem.at[2]),
        pltpu.make_async_copy(r.omega.at[own_f], om, lsem.at[3]),
        pltpu.make_async_copy(r.prior_wt.at[:, own_m], r.pwt, lsem.at[4]),
        pltpu.make_async_copy(r.phase.at[:, own_m], r.ph, lsem.at[9]),
    ]
    small = [
        pltpu.make_async_copy(r.batch_x, r.xbs, lsem.at[10]),
        pltpu.make_async_copy(r.targets, r.tgs, lsem.at[11]),
        pltpu.make_async_copy(r.dgroup, r.dgs, lsem.at[12]),
        pltpu.make_async_copy(r.alphat_own, r.als, lsem.at[13]),
        pltpu.make_async_copy(r.bgroup, r.sm_g, lsem.at[14]),
        pltpu.make_async_copy(r.bindex, r.sm_i, lsem.at[15]),
        pltpu.make_async_copy(r.pindex, r.sm_p, lsem.at[16]),
        pltpu.make_async_copy(r.ptable, r.sm_t, lsem.at[17]),
    ]
    for load in small[:1] + loads[:1]:
        load.start()
    barrier = pltpu.get_barrier_semaphore()
    ex.kw.greet(barrier)
    ex.xbn.greet(barrier)
    for load in small[1:] + loads[1:]:
        load.start()
    pl.semaphore_wait(barrier, W * N // 2 - 1 + N - 1)

    def xcopy(src, dst, k, p):
        return pltpu.make_async_remote_copy(
            src_ref=src, dst_ref=dst, send_sem=r.x_s.at[k], recv_sem=r.x_r.at[k],
            device_id={"narrow": p}, device_id_type=MESH)

    cuts = (0, R * 4 // 16, R * 8 // 16, R * 10 // 16, R)
    P = len(cuts) - 1

    def piece(k, src=None, slot=None):
        rows = pl.ds(cuts[k], cuts[k + 1] - cuts[k])
        slot = ni if slot is None else slot
        src = xg.at[slot, rows] if src is None else src.at[rows]
        return src, xg.at[slot, rows]

    def x_side():
        return xcopy(r.data_x, xg.at[ni], 0, n1)

    def x_over(k):
        return xcopy(*piece(k, r.data_x), 1 + k, n2)

    def x_pass(k):
        return xcopy(*piece(k, slot=n2), 1 + P + k, n1)

    small[0].wait()
    r.xbn[ni] = r.xbs[...].astype(F32)
    ex.xbn.gather(r.xbn)
    x_over(0).start()
    for load in small[1:]:
        load.wait()
    r.ad[ni, 0:S, :] = r.als[...]
    r.ad[ni, S : S + 8, :] = jnp.broadcast_to(r.dgs[...].astype(F32), (8, R))

    def ad_copy(slot, k, p):
        return xcopy(r.ad.at[slot], r.ad.at[slot], 9 + k, p)

    ad_copy(ni, 1, n2).start()
    ad_copy(ni, 0, n1).start()
    lane = lax.broadcasted_iota(jnp.int32, (1, 128), 1)
    for k in range(Bg):
        prec_k = r.sm_t[r.sm_p[k]]
        r.meta[wi, k : k + 1, :] = jnp.where(
            lane == 0, r.sm_g[k].astype(F32), jnp.where(lane == 1, r.sm_i[k].astype(F32), jnp.where(lane == 2, prec_k, 0.0)))
    r.meta[wi, :, S : 2 * S] = r.tgs[...]
    ex.meta.gather(r.meta)

    loads[0].wait()

    def cast1(k, carry):
        rows = pl.ds(pl.multiple_of(k * 128, 128), 128)
        w1b[rows, :] = r.w1f[rows, :].astype(BF)
        return carry

    lax.fori_loop(0, D // 128, cast1, 0)
    ex.xbn.wait(r.xbn)
    for n in range(N):
        r.xbg[n * brow : (n + 1) * brow, :] = r.xbn[n]
    xbg = r.xbg[...]
    hb, gb = gelu_pair(dot(xbg.astype(BF), w1b[...]))
    hb = hb.astype(BF).astype(F32)
    r.hbn[ni] = jnp.concatenate([hb[:, : Hn // 2], hb[:, Hn // 2 :]], axis=0).astype(BF)
    ex.hbn.gather(r.hbn)
    x_over(1).start()
    x_over(2).start()
    x_side().start()
    r.hgw[wi] = jnp.concatenate([hb, gb], axis=0).astype(BF)
    ex.hgw.gather(r.hgw)
    r.xbw[wi] = jnp.concatenate([xbg[:, : D // 2], xbg[:, D // 2 :]], axis=0).astype(BF)
    ex.xbw.gather(r.xbw)
    loads[2].wait()

    def cast2(k, carry):
        rows = pl.ds(pl.multiple_of(k * 128, 128), 128)
        w2b[rows, :] = r.w2f[rows, :].astype(BF)
        return carry

    lax.fori_loop(0, H // 128, cast2, 0)

    def block(q, first=0, last=P):
        base = q * R + cuts[first]
        size = cuts[last] - cuts[first]
        r.pre[:size, :] = dot(xg[q, cuts[first] : cuts[last], :], w1b[...])
        step = math.gcd(size, 32)

        def part(k, carry):
            src = pl.ds(pl.multiple_of(k * step, step), step)
            dst = pl.ds(pl.multiple_of(base + k * step, step), step)
            out, slope = gelu_pair(r.pre[src, :])
            hid[dst, :] = out.astype(BF)
            gd[dst, :] = slope
            return carry

        lax.fori_loop(0, size // step, part, 0)

    def turn(q):
        xT[:, pl.ds(pl.multiple_of(q * R, R), R)] = xg[q].T

    ex.hbn.wait(r.hbn)
    hbn = [r.hbn[n].astype(F32) for n in range(N)]
    hid_g = jnp.concatenate([h[k * Bg : (k + 1) * Bg] for h in hbn for k in range(2)], axis=1).astype(BF)
    bfeat = dot(hid_g, w2b[...]).astype(BF)
    r.bfs[...] = bfeat.astype(F32)
    gpart = dot(bfeat, w2b[...], NT)
    for n in range(N):
        g = gpart[:, n * Hn : (n + 1) * Hn]
        r.ges[n] = jnp.concatenate([g[:, : Hn // 2], g[:, Hn // 2 :]], axis=0).astype(BF)
    ex.ger.scatter(r.ges, r.ger)
    r.ger[ni] = r.ges[ni]
    loads[3].wait()
    zpart = dot(r.bfs[...].astype(BF), om[...])
    for n in range(N):
        r.zes[n] = zpart[:, n * Mn : (n + 1) * Mn]
    ex.zer.scatter(r.zes, r.zer)
    r.zer[ni] = r.zes[ni]
    x_over(3).start()
    later = []
    if resident:
        pairs = ((r.w1_m, r.m1), (r.w1_v, r.v1), (r.w2_m, r.m2), (r.w2_v, r.v2))
        later = [pltpu.make_async_copy(src, dst, lsem.at[5 + k]) for k, (src, dst) in enumerate(pairs)]
    for load in later:
        load.start()
    bf32 = r.bfs[...]
    r.bfw[wi] = jnp.concatenate([bf32[:, : Fn // 2], bf32[:, Fn // 2 :]], axis=0).astype(BF)
    ex.bfw.gather(r.bfw)
    loads[1].wait()
    block(ni)
    xcopy(r.data_x, xg.at[n1], 0, n1).wait_recv()
    block(n1)
    turn(ni)
    turn(n1)
    ex.ger.wait(r.ger)
    r.gw[wi] = jnp.sum(r.ger[...].astype(F32), axis=0).astype(BF)
    ex.gw.gather(r.gw)
    for k in range(3):
        xcopy(*piece(k, slot=n2), 1 + k, n2).wait_recv()
        x_pass(k).start()
    ad_copy(n2, 1, n2).wait_recv()
    ad_copy(n2, 2, n1).start()
    ex.zer.wait(r.zer)
    own_b = pl.ds(pl.multiple_of(wi * Bg, Bg), Bg)
    loads[5].wait()
    angle = jnp.sum(r.zer[...], axis=0) + r.ph[...]
    r.cz[...] = jnp.zeros_like(r.cz)
    r.cz[own_b, :] = scale * jnp.cos(angle)
    sz = scale * jnp.sin(angle)
    r.szw[wi] = jnp.concatenate([sz[:, : Mn // 2], sz[:, Mn // 2 :]], axis=0).astype(BF)
    ex.szw.gather(r.szw)
    loads[4].wait()
    r.prior[...] = dot(r.pwt[...], r.cz[...], NT, HIGH)

    def x_last(k):
        xcopy(*piece(k, slot=n3), 1 + P + k, n1).wait_recv()

    block(n2, 0, 2)
    x_last(0)
    x_last(1)
    block(n3, 0, 2)
    ex.meta.wait(r.meta)
    meta = r.meta[...].reshape(B, 128)
    r.metat[...] = meta.T
    ad_copy(n1, 0, n1).wait_recv()
    ad_copy(n3, 2, n1).wait_recv()
    alphat = jnp.concatenate([r.ad[n, 0:S, :] for n in range(N)], axis=1)
    r.alphat[...] = alphat
    group = jnp.concatenate([r.ad[n, S : S + 1, :] for n in range(N)], axis=1)
    pmask = (0.5 + (meta[:, 0:1] == group).astype(F32)) / F
    r.pmask[...] = pmask
    col = lax.broadcasted_iota(jnp.int32, (1, N * R), 1) + wi * (N * R)
    first = (ni == 0).astype(F32)
    r.amat[...] = jnp.where(meta[:, 1:2] == col.astype(F32), first / meta[:, 2:3], 0.0)
    ex.gw.wait(r.gw)
    gw = r.gw[...].astype(F32)
    r.gmat[...] = jnp.concatenate([gw[:, :Bg].reshape(B, Hn // 2), gw[:, Bg:].reshape(B, Hn // 2)], axis=1).astype(BF)

    def columns(q, first=0, last=P):
        size = cuts[last] - cuts[first]
        return pl.ds(pl.multiple_of(q * R + cuts[first], size), size)

    def kernel_block(cols):
        r.amat[:, cols] = r.pmask[:, cols] * dot(r.gmat[...], hid[cols, :], NT) + r.amat[:, cols]

    def kalpha(cols):
        return dot(r.alphat[:, cols], r.amat[:, cols], NT, HIGH)

    for q in (ni, n1):
        kernel_block(columns(q))
    for q in (n2, n3):
        kernel_block(columns(q, 0, 2))
    xcopy(*piece(3, slot=n2), 4, n2).wait_recv()
    x_pass(3).start()
    block(n2, 2, 4)
    kernel_block(columns(n2, 2, 4))
    kal = r.prior[...] + (kalpha(columns(ni)) + kalpha(columns(n1))) + (kalpha(columns(n2)) + kalpha(columns(n3, 0, 2)))
    r.prior[...] = kal
    x_last(2)
    x_last(3)
    block(n3, 2, 4)

    kernel_block(columns(n3, 2, 4))
    kal = r.prior[...] + kalpha(columns(n3, 2, 4))
    fold = max(1, min(S // 8, 128 // B))
    r.kn[core] = jnp.concatenate([kal[k * (S // fold) : (k + 1) * (S // fold)] for k in range(fold)], axis=1)

    def core_copy(buf, k):
        return xcopy(buf.at[core], buf.at[core], 12 + k, n1)

    def core_sum(buf, k):
        xcopy(buf.at[1 - core], buf.at[1 - core], 12 + k, n1).wait_recv()
        return buf[0] + buf[1]

    core_copy(r.kn, 0).start()
    chip = wi * (N // 2) + side
    r.kw[chip] = core_sum(r.kn, 0)
    ex.kw.gather(r.kw)
    turn(n2)
    turn(n3)
    ex.hgw.wait(r.hgw)
    hg = r.hgw[...].astype(F32)
    r.hbx[ni] = hg[:, :Bg].reshape(B, Hn).astype(BF)
    r.gb[...] = hg[:, Bg:].reshape(B, Hn)
    ex.hbx.gather(r.hbx)
    ex.xbw.wait(r.xbw)
    xbw = r.xbw[...].astype(F32)
    r.xbt[...] = jnp.concatenate([xbw[:, :Bg].reshape(B, D // 2), xbw[:, Bg:].reshape(B, D // 2)], axis=1).T.astype(BF)
    prec = r.metat[2:3, :]
    total = jnp.sum(prec, axis=1, keepdims=True)
    ex.kw.wait(r.kw)
    kal = jnp.sum(r.kw[...], axis=0)
    resid = r.metat[S : 2 * S, :] - jnp.concatenate([kal[:, k * B : (k + 1) * B] for k in range(fold)], axis=0)
    grt = prec * resid / total

    ds = (-r.pmask[...] * dot(grt, r.alphat[...], TN, HIGH)).astype(BF)
    upart = dot(ds, hid[...]).reshape(W, Bg, Hn)
    r.us[...] = jnp.concatenate([upart[:, :, : Hn // 2], upart[:, :, Hn // 2 :]], axis=1).astype(BF)
    ex.ur.scatter(r.us, r.ur)
    for q in range(N):
        rows = slice(q * R, (q + 1) * R)
        dpre[rows, :] = (dot(ds[:, rows], r.gmat[...], TN) * gd[rows, :]).astype(BF)

    def wcopy(src, dst, kind, k, slot, p):
        return pltpu.make_async_remote_copy(
            src_ref=src, dst_ref=dst, send_sem=getattr(r, kind + "_s").at[k], recv_sem=getattr(r, kind + "_r").at[slot],
            device_id={"wide": p}, device_id_type=MESH)

    psend, precv, zsend, zrecv, gat = r.psend, r.precv, r.zsend, r.zrecv, r.gat

    NH = 2 if Ck % 32 == 0 else 1
    Hk = Ck // NH
    Q = 2 if Hk % 32 == 0 else 1
    Cq = Hk // Q

    def grad_rows(row):
        return dot(xT[pl.ds(pl.multiple_of(row, Hk), Hk), :], dpre[...])

    def target(step):
        low = a // (A // 2)
        m = a + low * (A - 1 - 2 * a)
        single = A - 1 - 2 * m
        late = (step // single + A - 1) // A
        e = step - single
        t = (1 - late) * (A - 1 - step) + late * (m + (1 - lax.rem(e + 2 * A, 2) * 2) * (m - (e + 2 * A) // 2 + A))
        return t + low * (A - 1 - 2 * t)

    def pcopy(ap, h, q):
        rows = pl.ds(pl.multiple_of(ap * Ck + h * Hk + q * Cq, Cq), Cq)
        return wcopy(psend.at[rows], precv.at[rows], "p", 0, ap * NH * Q + h * Q + q, pair)

    def pair_chunk(h, ap):
        base = ap * Ck + h * Hk
        psend[pl.ds(pl.multiple_of(base, Hk), Hk), :] = grad_rows((1 - b) * half + base).astype(BF)
        for q in range(Q):
            pcopy(ap, h, q).start()

    def pair_sends(h, first, last):
        def send(step, carry):
            pair_chunk(h, target(step))
            return carry

        lax.fori_loop(min(first, A - 1), min(last, A - 1), send, 0)
        if last >= A:
            pair_chunk(h, a)

    def zcopy(ap, h, q):
        rows = pl.ds(h * Hk + q * Cq, Cq)
        return wcopy(zsend.at[ap, rows], zrecv.at[a, rows], "z", 0, h, 2 * ap + b)

    def z_part(ap, h, q):
        pcopy(ap, h, q).wait_recv()
        rows = pl.ds(pl.multiple_of(ap * Ck + h * Hk + q * Cq, Cq), Cq)
        return r.zt[q * Cq : (q + 1) * Cq, :] + precv[rows, :].astype(F32)

    def z_sends(h, first, last):
        def send(step, carry):
            ap = target(step)
            r.zt[...] = grad_rows(b * half + ap * Ck + h * Hk)
            for q in range(Q):
                zsend[ap, h * Hk + q * Cq : h * Hk + (q + 1) * Cq, :] = z_part(ap, h, q).astype(BF)
                zcopy(ap, h, q).start()
            return carry

        lax.fori_loop(min(first, A - 1), min(last, A - 1), send, 0)

    def z_own(h):
        r.zt[...] = grad_rows(b * half + a * Ck + h * Hk)
        for q in range(Q):
            r.zf[h * Hk + q * Cq : h * Hk + (q + 1) * Cq, :] = z_part(a, h, q)

    pair_sends(0, 0, 2)

    loss = 0.5 * jnp.sum(jnp.sum(prec * (resid * resid), axis=1, keepdims=True), axis=0, keepdims=True)
    agt = -dot(grt, r.amat[...], precision=HIGH)
    for n in range(N):
        r.ags[n] = agt[:, n * R : (n + 1) * R]
    ex.agr.scatter(r.ags, r.agr)
    r.agr[ni] = r.ags[ni]
    ex.szw.wait(r.szw)

    def unfold(buf):
        v = buf[...].astype(F32)
        return jnp.concatenate([v[:, :Bg].reshape(B, -1), v[:, Bg:].reshape(B, -1)], axis=1)

    r.dzn[ni] = (unfold(r.szw) * dot(grt, r.pwt[...], TN, HIGH)).astype(BF)

    def dz_copy(slot, k, p):
        return xcopy(r.dzn.at[slot], r.dzn.at[slot], 17 + k, p)

    dz_copy(ni, 1, n2).start()
    dz_copy(ni, 0, n1).start()
    ex.ur.wait(r.ur)
    r.ur[wi] = r.us[wi]
    r.uz[wi] = jnp.sum(r.ur[...].astype(F32), axis=0).astype(BF)
    ex.uz.gather(r.uz)
    pair_sends(0, 2, A)
    z_sends(0, 0, 1)
    for h in range(1, NH):
        pair_sends(h, 0, A)
    z_sends(0, 1, 2)
    ex.bfw.wait(r.bfw)
    ex.uz.wait(r.uz)
    r.uzn[ni] = unfold(r.uz).astype(BF)

    def u_copy(slot, k, p):
        return xcopy(r.uzn.at[slot], r.uzn.at[slot], 14 + k, p)

    u_copy(ni, 1, n2).start()
    u_copy(ni, 0, n1).start()
    dz_copy(n2, 1, n2).wait_recv()
    dz_copy(n2, 2, n1).start()
    z_sends(0, 2, A)
    z_own(0)

    others = pl.ds(0, A - 1)
    mine = b * A + a

    def shard(slot, h=0, q=0, count=Ck):
        return pl.ds(pl.multiple_of(slot * Ck + h * Hk + q * Cq, min(count, Cq)), count)

    def fcopy(ap, h, q):
        rows = shard(b * A + ap, h, q, Cq)
        return wcopy(gat.at[rows], gat.at[rows], "f", 0, 0, pair)

    def gcopy(ap, h, q, way):
        rows = shard(b * A + ap, h, q, Cq)
        return wcopy(gat.at[rows], gat.at[rows], "g", 0 if way > 0 else 1, (ap * NH + h) * Q + q, 2 * (a + way) + b)

    def straight(h):
        return h > 0

    def gdirect(ap, h, q):
        rows = shard(mine, h, q, Cq)
        return wcopy(gat.at[rows], gat.at[rows], "g", 2, (a * NH + h) * Q + q, 2 * ap + b)

    def z_done(h):
        rows = slice(h * Hk, (h + 1) * Hk)
        part = pl.ds(h * Hk, Hk)
        wcopy(zsend.at[others, part], zrecv.at[others, part], "z", 0, h, pair).wait_recv()

        def gain(k, carry):
            r.zf[rows, :] = r.zf[rows, :] + zrecv[lax.rem(a + k, A), rows, :].astype(F32)
            return carry

        lax.fori_loop(1, A, gain, 0)
        gat[shard(mine, h, 0, Hk), :] = r.zf[rows, :].astype(BF)
        for q in range(Q):
            fcopy(a, h, q).start()
        if straight(h):

            def send(step, carry):
                for q in range(Q):
                    gdirect(target(step), h, q).start()
                return carry

            lax.fori_loop(0, A - 1, send, 0)
        else:
            for q in range(Q):

                @pl.when(a + 1 < A)
                def _():
                    gcopy(a, h, q, 1).start()

                @pl.when(a > 0)
                def _():
                    gcopy(a, h, q, -1).start()

    def g_pass(h, first, last):
        def step(k, carry):
            below, above = a - 1 - k // Q, a + 1 + k // Q
            q = lax.rem(k, Q)

            @pl.when(below >= 0)
            def _():
                gcopy(below, h, q, 1).wait_recv()

                if not straight(h):

                    @pl.when(a + 1 < A)
                    def _():
                        gcopy(below, h, q, 1).start()

                fcopy(below, h, q).start()

            @pl.when(above < A)
            def _():
                gcopy(above, h, q, -1).wait_recv()

                if not straight(h):

                    @pl.when(a > 0)
                    def _():
                        gcopy(above, h, q, -1).start()

                fcopy(above, h, q).start()

            return carry

        lax.fori_loop(min(first, A - 1) * Q, min(last, A - 1) * Q, step, 0)

    if NH > 1:
        z_sends(1, 0, 1)
    u_copy(n2, 1, n2).wait_recv()
    u_copy(n2, 2, n1).start()
    z_done(0)
    if NH > 1:
        z_sends(1, 1, A)
        z_own(1)
    u_copy(n1, 0, n1).wait_recv()
    u_copy(n3, 2, n1).wait_recv()
    dz_copy(n1, 0, n1).wait_recv()
    dz_copy(n3, 2, n1).wait_recv()
    acc = jnp.zeros((B, Fn), F32)
    for n in range(N):
        acc = acc + dot(r.uzn[n], w2b[n * Hn : (n + 1) * Hn, :])
        acc = acc + dot(r.dzn[n], om[:, n * Mn : (n + 1) * Mn], NT)
    r.db[...] = jnp.concatenate([acc, unfold(r.bfw)], axis=0).astype(BF)
    for n in range(N):
        r.dhs[n] = dot(r.db[:B, :], w2b[n * Hn : (n + 1) * Hn, :], NT).astype(BF)
    ex.dhr.scatter(r.dhs, r.dhr)
    r.dhr[ni] = r.dhs[ni]
    g_pass(0, 0, 1)
    if NH > 1:
        z_done(1)
    g_pass(0, 1, 2)

    def two(v):
        return jnp.sum(jnp.sum(v * v, axis=1, keepdims=True), axis=0, keepdims=True)

    square = jnp.zeros((1, 1), F32)
    for n in range(N):
        if n == 0:
            ex.hbx.wait(r.hbx)
        hu = jnp.concatenate([r.hbx[n], r.uzn[n]], axis=0)
        g2 = dot(hu, r.db[...], TN)
        r.g2[n * Hn : (n + 1) * Hn, :] = g2
        square = square + two(g2)

    ex.agr.wait(r.agr)
    agt = jnp.sum(r.agr[...], axis=0)
    r.agrad[...] = agt
    ex.dhr.wait(r.dhr)
    r.dpb[...] = (jnp.sum(r.dhr[...].astype(F32), axis=0) * r.gb[...]).astype(BF)

    square = square * (1.0 / W) + two(r.zf[...] + dot(r.xbt[shard(mine), :], r.dpb[...])) + two(agt)
    r.nn[core] = jnp.broadcast_to(square, (8, 128))
    core_copy(r.nn, 1).start()
    if NH > 1:
        g_pass(1, 0, 1)
    g_pass(0, 2, A)
    r.nw[chip] = core_sum(r.nn, 1)
    ex.nw.gather(r.nw)
    if NH > 1:
        g_pass(1, 1, A)
    ex.nw.wait(r.nw)
    norm = jnp.sum(r.nw[...], axis=0)
    lanes = lax.broadcasted_iota(jnp.int32, (8, 128), 1)
    r.scal[...] = jnp.where(lanes == 0, loss, jnp.where(lanes == 1, total, norm))

    theirs = pl.ds(pl.multiple_of((1 - b) * half, half), half)
    ours = pl.ds(pl.multiple_of(b * half, half), half)
    wcopy(gat.at[theirs], gat.at[theirs], "f", 0, 0, pair).wait_recv()

    for name in live:
        vars(ex)[name].drain(getattr(r, name))
    x_side().wait_send()
    for k in range(P):
        x_over(k).wait_send()
        x_pass(k).wait_send()
    for slot, k, p in ((ni, 0, n1), (ni, 1, n2), (n2, 2, n1)):
        ad_copy(slot, k, p).wait_send()
        u_copy(slot, k, p).wait_send()
        dz_copy(slot, k, p).wait_send()
    core_copy(r.kn, 0).wait_send()
    core_copy(r.nn, 1).wait_send()
    wcopy(psend, precv, "p", 0, 0, pair).wait_send()
    wcopy(gat.at[ours], gat.at[ours], "f", 0, 0, pair).wait_send()
    wcopy(zsend.at[others], zrecv.at[others], "z", 0, 0, pair).wait_send()
    if NH > 1:
        direct = pl.ds(0, (A - 1) * Hk)
        wcopy(gat.at[direct], gat.at[direct], "g", 2, 0, pair).wait_send()
    for k in range(A):
        up, down = (pl.ds(0, n * Hk) for n in (k + 1, A - k))

        @pl.when((a == k) & (a + 1 < A))
        def _():
            wcopy(gat.at[up], gat.at[up], "g", 0, 0, pair).wait_send()

        @pl.when((a == k) & (a > 0))
        def _():
            wcopy(gat.at[down], gat.at[down], "g", 1, 0, pair).wait_send()

    for load in later:
        load.wait()


CORR1 = 1.0 - 0.9**STEP_NUM
CORR2 = 1.0 - 0.999**STEP_NUM


def adamw(weight, grad, moment, second, rate, decay):
    moment_new = 0.9 * moment + 0.1 * grad
    second_new = 0.999 * second + 0.001 * grad * grad
    step = moment_new / (jnp.sqrt(second_new) * (1.0 / math.sqrt(CORR2)) + 1e-08)
    new = weight * (1.0 - rate * decay) - (rate / CORR1) * step
    return moment_new, second_new, new


def update_kernel(resident, slots, C, names, *refs):
    r = SimpleNamespace(**dict(zip(names, refs)))
    if not resident:
        pairs = ((r.w1, r.w1f), (r.w1_m, r.m1), (r.w1_v, r.v1), (r.w2, r.w2f), (r.w2_m, r.m2), (r.w2_v, r.v2))
        loads = [pltpu.make_async_copy(src, dst, r.lsem.at[k]) for k, (src, dst) in enumerate(pairs)]
        for load in loads:
            load.start()
        for load in loads:
            load.wait()
    for k in range(3):
        r.s3[k] = r.scal[0:1, k : k + 1]
    last = [pltpu.make_async_copy(r.s3.at[k], dst, r.asem.at[3 + k]) for k, dst in enumerate((r.loss, r.total, r.normsq))]
    for copy in last:
        copy.start()
    small = [pltpu.make_async_copy(src, r.asl.at[k], r.asem.at[k]) for k, src in enumerate((r.at, r.atm, r.atv))]
    for load in small:
        load.start()
    norm = r.scal[0:1, 2:3]
    clip = jnp.minimum(1.0, 0.1 / jnp.sqrt(norm))
    ring = (r.sm, r.sv, r.sn, r.sc)

    def copies(outs, slot, rows):
        return [pltpu.make_async_copy(buf.at[slot], out.at[rows], r.osem.at[slot, k]) for k, (buf, out) in enumerate(zip(ring, outs))]

    def chunk(grad, state, outs, k, ahead):
        w, m, v = state
        slot = lax.rem(k + ahead, slots)
        base = pl.multiple_of(k * C, C)
        rows = pl.ds(base, C)

        def drain():
            for copy in copies(outs, slot, rows):
                copy.wait()

        if ahead:
            drain()
        else:
            pl.when(k >= slots)(drain)

        def part(j, carry):
            src = pl.ds(pl.multiple_of(base + j * 16, 16), 16)
            dst = pl.ds(pl.multiple_of(j * 16, 16), 16)
            mn, vn, wn = adamw(w[src, :], clip * grad[src, :], m[src, :], v[src, :], 0.03, 0.01)
            r.sm[slot, dst, :] = mn
            r.sv[slot, dst, :] = vn
            r.sn[slot, dst, :] = wn
            r.sc[slot, dst, :] = wn.astype(BF)
            return carry

        lax.fori_loop(0, C // 16, part, 0, unroll=True)
        for copy in copies(outs, slot, rows):
            copy.start()

    outs1 = (r.m1o, r.v1o, r.n1o, r.c1o)
    outs2 = (r.m2o, r.v2o, r.n2o, r.c2o)
    count1, count2 = r.w1f.shape[0] // C, r.w2f.shape[0] // C

    def step2(k, carry):
        chunk(r.g2, (r.w2f, r.m2, r.v2), outs2, k, 0)
        return carry

    def step1(k, carry):
        chunk(r.gs, (r.w1f, r.m1, r.v1), outs1, k, count2)
        return carry

    lax.fori_loop(0, count2, step2, 0)
    r.gs[...] = r.gat[...].astype(F32) + dot(r.xbt[...], r.dpb[...])
    lax.fori_loop(0, count1, step1, 0)
    for load in small:
        load.wait()
    am, av, an = adamw(r.asl[0], clip * r.agrad[...], r.asl[1], r.asl[2], 0.2, 0.0)
    for k, v in enumerate((am, av, an)):
        r.ast[k] = v
    alphas = [pltpu.make_async_copy(r.ast.at[k], dst, r.asem.at[k]) for k, dst in enumerate((r.amo, r.avo, r.ano))]
    for copy in alphas:
        copy.start()
    for k in range(slots):
        for copy in copies(outs1, k, pl.ds(0, C)):
            copy.wait()
    for copy in last + alphas:
        copy.wait()


def on_device(
    data_x, data_group, batch_x, batch_group, batch_index, prec_index, prec_table, targets,
    omega, phase, prior_w, w1_master, w1_moment, w1_second, w2_master, w2_moment, w2_second,
    alpha, alpha_moment, alpha_second,
):
    W, N = lax.axis_size("wide"), lax.axis_size("narrow")
    A = W // 2
    R, D = data_x.shape
    brow, Bg, S = batch_x.shape[0], targets.shape[0], targets.shape[1]
    F, M = omega.shape
    Hn, Fn, Mn, H = w1_master.shape[1], w2_master.shape[1], M // N, w2_master.shape[0]
    B, Ck = W * Bg, D // 2 // A
    hbm, vmem = (pl.BlockSpec(memory_space=m) for m in (pl.ANY, pltpu.VMEM))
    resident = B <= 128
    fold = max(1, min(S // 8, 128 // B))
    args = dict(
        data_x=(data_x, hbm), dgroup=(data_group.reshape(1, R), hbm), batch_x=(batch_x, hbm),
        bgroup=(batch_group, hbm), bindex=(batch_index, hbm), pindex=(prec_index, hbm),
        ptable=(prec_table, hbm), targets=(targets, hbm), omega=(omega, hbm),
        phase=(phase.reshape(1, M), hbm), prior_wt=(prior_w.T, hbm), w1=(w1_master, hbm),
        w2=(w2_master, hbm), alphat_own=(alpha.T, hbm),
    )
    state = dict(
        w1=(w1_master, hbm), w1_m=(w1_moment, hbm), w1_v=(w1_second, hbm),
        w2=(w2_master, hbm), w2_m=(w2_moment, hbm), w2_v=(w2_second, hbm),
    )
    outs = dict(
        scal=((8, 128), F32), agrad=((S, R), F32), gat=((D, Hn), BF), xbt=((D, B), BF), dpb=((B, Hn), BF),
        g2=((H, Fn), F32),
    )
    held = dict(
        w1f=((D, Hn), F32), m1=((D, Hn), F32), v1=((D, Hn), F32), w2f=((H, Fn), F32), m2=((H, Fn), F32), v2=((H, Fn), F32),
    )
    scratch = dict(
        xg=((N, R, D), BF), xT=((D, N * R), BF), hid=((N * R, Hn), BF), gd=((N * R, Hn), F32),
        dpre=((N * R, Hn), BF), pre=((R, Hn), F32), w1b=((D, Hn), BF),
        w2b=((H, Fn), BF), om=((Fn, M), BF), pwt=((S, Mn), F32),
        xbg=((Bg, D), F32), xbs=((brow, D), BF), tgs=((Bg, S), F32), dgs=((1, R), jnp.int32), als=((S, R), F32), ph=((1, Mn), F32), ges=((N, 2 * Bg, Hn // 2), BF), zes=((N, Bg, Mn), F32), bfs=((Bg, Fn), F32), zf=((Ck, Hn), F32), zt=((Ck // (2 if Ck % 32 == 0 else 1), Hn), F32), us=((W, 2 * Bg, Hn // 2), BF), ags=((N, S, R), F32),
        dhs=((N, B, Hn), BF), cz=((B, Mn), F32), prior=((S, B), F32),
        metat=((128, B), F32), alphat=((S, N * R), F32), pmask=((B, N * R), F32), amat=((B, N * R), F32),
        gmat=((B, Hn), BF), db=((2 * B, Fn), BF),
        psend=((A * Ck, Hn), BF), precv=((A * Ck, Hn), BF), zsend=((A, Ck, Hn), BF), zrecv=((A + 1, Ck, Hn), BF),
        gb=((B, Hn), F32),
        meta=((W, Bg, 128), F32), xbw=((W, 2 * Bg, D // 2), BF), hgw=((W, 2 * Bg, Hn), BF),
        bfw=((W, 2 * Bg, Fn // 2), BF), gw=((W, 2 * Bg, Hn // 2), BF), kw=((W * N // 2, S // fold, fold * B), F32),
        ur=((W, 2 * Bg, Hn // 2), BF), uz=((W, 2 * Bg, Hn // 2), BF), szw=((W, 2 * Bg, Mn // 2), BF), nw=((W * N // 2, 8, 128), F32),
        xbn=((N, brow, D), F32), ad=((N, S + 8, R), F32), hbn=((N, 2 * Bg, Hn // 2), BF), ger=((N, 2 * Bg, Hn // 2), BF), zer=((N, Bg, Mn), F32),
        kn=((2, S // fold, fold * B), F32), agr=((N, S, R), F32), uzn=((N, B, Hn), BF), dzn=((N, B, Mn), BF), hbx=((N, B, Hn), BF), dhr=((N, B, Hn), BF),
        nn=((2, 8, 128), F32),
    )
    if resident:
        args.update(state)
        outs.update(held)
    else:
        scratch.update(w1f=held["w1f"], w2f=held["w2f"])
    pieces = A * math.gcd(Ck // 16, 4)
    count = 2 * len(WIDE_EX + NARROW_EX + CHIP_EX)
    sems = [("lsem", 18), ("x_s", 20), ("x_r", 20), ("es", count), ("p_s", 1), ("p_r", pieces), ("z_s", 1), ("z_r", pieces + pieces // A)]
    sems += [("f_s", 1), ("f_r", 1), ("g_s", 3), ("g_r", pieces)]
    smem = dict(sm_g=(Bg, jnp.int32), sm_i=(Bg, jnp.int32), sm_p=(Bg, jnp.int32), sm_t=(prec_table.shape[0], F32))
    names = [*args, *outs, *scratch, *smem] + [n for n, _ in sems]
    grads = pl.pallas_call(
        lambda *refs: step_kernel(W, N, resident, names, *refs),
        out_shape=[(pltpu.VMEM if resident else jax.ShapeDtypeStruct)(s, t) for s, t in outs.values()],
        in_specs=[spec for _, spec in args.values()],
        out_specs=[vmem] * len(outs),
        scratch_shapes=[pltpu.VMEM(s, t) for s, t in scratch.values()]
        + [pltpu.SMEM((k,), t) for k, t in smem.values()]
        + [pltpu.SemaphoreType.DMA((k,)) for _, k in sems],
        compiler_params=pltpu.CompilerParams(collective_id=0, has_side_effects=True, vmem_limit_bytes=(62 if not resident else 39) * 2**20),
        name="gradients",
    )(*[v for v, _ in args.values()])

    args2 = {k: (v, vmem) for k, v in zip(outs, grads)}
    args2.update(at=(alpha.T, hbm), atm=(alpha_moment.T, hbm), atv=(alpha_second.T, hbm))
    C, slots = 256, 4
    outs2 = dict(amo=((S, R), F32, hbm), avo=((S, R), F32, hbm), ano=((S, R), F32, hbm))
    outs2.update(loss=((1, 1), F32, hbm), total=((1, 1), F32, hbm), normsq=((1, 1), F32, hbm))
    for k, shape in (("1", (D, Hn)), ("2", (H, Fn))):
        outs2.update({"m" + k + "o": (shape, F32, hbm), "v" + k + "o": (shape, F32, hbm)})
        outs2.update({"n" + k + "o": (shape, F32, hbm), "c" + k + "o": (shape, BF, hbm)})
    scratch2 = dict(
        gs=pltpu.VMEM((D, Hn), F32), sm=pltpu.VMEM((slots, C, Hn), F32), sv=pltpu.VMEM((slots, C, Hn), F32),
        sn=pltpu.VMEM((slots, C, Hn), F32), sc=pltpu.VMEM((slots, C, Hn), BF), osem=pltpu.SemaphoreType.DMA((slots, 4)),
        asl=pltpu.VMEM((3, S, R), F32), ast=pltpu.VMEM((3, S, R), F32), asem=pltpu.SemaphoreType.DMA((6,)), s3=pltpu.VMEM((3, 1, 1), F32),
    )
    if not resident:
        args2.update(state)
        scratch2.update({k: pltpu.VMEM(s, t) for k, (s, t) in held.items()}, lsem=pltpu.SemaphoreType.DMA((6,)))
    names2 = [*args2, *outs2, *scratch2]
    new = pl.pallas_call(
        lambda *refs: update_kernel(resident, slots, C, names2, *refs),
        out_shape=[jax.ShapeDtypeStruct(s, t) for s, t, _ in outs2.values()],
        in_specs=[spec for _, spec in args2.values()],
        out_specs=[spec for _, _, spec in outs2.values()],
        scratch_shapes=list(scratch2.values()),
        compiler_params=pltpu.CompilerParams(vmem_limit_bytes=(36 if not resident else 12) * 2**20),
        name="adamw",
    )(*[v for v, _ in args2.values()])
    new = dict(zip(outs2, new))
    return (
        new["loss"].reshape(()), new["total"].reshape(()), new["normsq"].reshape(()),
        new["m1o"], new["v1o"], new["n1o"], new["c1o"],
        new["m2o"], new["v2o"], new["n2o"], new["c2o"],
        new["amo"].T, new["avo"].T, new["ano"].T,
    )


def solution(mesh):
    both = P(("wide", "narrow"))
    both2 = P(("wide", "narrow"), None)
    col = P(None, "narrow")
    return jax.shard_map(
        on_device,
        mesh=mesh,
        in_specs=(both2, both, both2, P("wide"), P("wide"), P("wide"), P(), P("wide", None), P(), P(), P())
        + (col,) * 6 + (both2,) * 3,
        out_specs=(P(), P(), P()) + (col,) * 8 + (both2,) * 3,
        check_vma=False,
    )
```

```python
import math
from types import SimpleNamespace

import jax
import jax.numpy as jnp
from jax import lax
from jax.experimental import pallas as pl
from jax.experimental.pallas import tpu as pltpu
from jax.sharding import PartitionSpec as P

STEP_NUM = 10
HIGH = lax.Precision.HIGHEST
MESH = pl.DeviceIdType.MESH
GC = math.sqrt(2.0 / math.pi)
F32 = jnp.float32
BF = jnp.bfloat16
DIRECT = 1


def gelu_pair(pre):
    square = pre * pre
    t = jnp.tanh(pre * (GC + (GC * 0.044715) * square))
    half = 0.5 * (1.0 + t)
    slope = half + 0.5 * pre * (1.0 - t * t) * (GC + (3 * GC * 0.044715) * square)
    return pre * half, slope


def dot(left, right, dims=((1,), (0,)), precision=None):
    return lax.dot_general(left, right, (dims, ((), ())), precision=precision, preferred_element_type=F32)


NT = ((1,), (1,))
TN = ((0,), (0,))


class Exchange:
    def __init__(self, size, me, where, sems, k):
        self.size, self.me, self.where, self.sems, self.k = size, me, where, sems, k

    def copy(self, src, dst, p):
        return pltpu.make_async_remote_copy(
            src_ref=src, dst_ref=dst, send_sem=self.sems.at[self.k], recv_sem=self.sems.at[self.k + 1],
            device_id=self.where(p), device_id_type=MESH)

    def loop(self, body):
        def step(k, carry):
            body(lax.rem(self.me + k, self.size))
            return carry

        lax.fori_loop(1, self.size, step, 0)

    def greet(self, barrier):
        self.loop(lambda p: pl.semaphore_signal(barrier, inc=1, device_id=self.where(p), device_id_type=MESH))

    def gather(self, buf):
        self.loop(lambda p: self.copy(buf.at[self.me], buf.at[self.me], p).start())

    def scatter(self, src, buf):
        self.loop(lambda p: self.copy(src.at[p], buf.at[self.me], p).start())

    def all(self, buf):
        others = buf.at[pl.ds(0, self.size - 1)]
        return self.copy(others, others, lax.rem(self.me + 1, self.size))

    def wait(self, buf):
        self.all(buf).wait_recv()

    def drain(self, buf):
        self.all(buf).wait_send()


WIDE_EX = ("meta", "xbw", "hgw", "bfw", "gw", "szw", "ur", "uz")
NARROW_EX = ("xbn", "hbn", "ger", "zer", "agr", "hbx", "dhr")
CHIP_EX = ("kw", "nw")


def step_kernel(W, N, resident, names, *refs):
    r = SimpleNamespace(**dict(zip(names, refs)))
    wi, ni = lax.axis_index("wide"), lax.axis_index("narrow")
    A = W // 2
    a, b = wi // 2, lax.rem(wi, 2)
    pair = wi + 1 - 2 * b
    n1 = ni + 1 - 2 * lax.rem(ni, 2)
    n2 = lax.rem(ni + 2, N)
    n3 = lax.rem(n1 + 2, N)
    xg, hid, gd, xT, dpre = r.xg, r.hid, r.gd, r.xT, r.dpre
    w1b, w2b, om = r.w1b, r.w2b, r.om
    _, R, D = xg.shape
    Bg, S = r.targets.shape
    brow = r.batch_x.shape[0]
    Hn, Fn = w1b.shape[1], w2b.shape[1]
    H, F, M = w2b.shape[0], r.omega.shape[0], r.omega.shape[1]
    Mn = M // N
    B = W * Bg
    half = D // 2
    Ck = half // A
    scale = math.sqrt(2.0 / M)
    lsem = r.lsem
    core, side = lax.rem(ni, 2), ni // 2
    groups = (
        (WIDE_EX, W, wi, lambda p: {"wide": p}),
        (NARROW_EX, N, ni, lambda p: {"narrow": p}),
        (CHIP_EX, W * N // 2, wi * (N // 2) + side, lambda p: {"wide": p // (N // 2), "narrow": lax.rem(p, N // 2) * 2 + core}),
    )
    ex, live = SimpleNamespace(), []
    for group, size, me, where in groups:
        for name in group:
            vars(ex)[name] = Exchange(size, me, where, r.es, 2 * len(live))
            live.append(name)

    own_f = pl.ds(pl.multiple_of(ni * Fn, Fn), Fn)
    own_m = pl.ds(pl.multiple_of(ni * Mn, Mn), Mn)
    loads = [
        pltpu.make_async_copy(r.w1, r.w1f, lsem.at[0]),
        pltpu.make_async_copy(r.data_x, xg.at[ni], lsem.at[1]),
        pltpu.make_async_copy(r.w2, r.w2f, lsem.at[2]),
        pltpu.make_async_copy(r.omega.at[own_f], om, lsem.at[3]),
        pltpu.make_async_copy(r.prior_wt.at[:, own_m], r.pwt, lsem.at[4]),
        pltpu.make_async_copy(r.phase.at[:, own_m], r.ph, lsem.at[9]),
    ]
    small = [
        pltpu.make_async_copy(r.batch_x, r.xbs, lsem.at[10]),
        pltpu.make_async_copy(r.targets, r.tgs, lsem.at[11]),
        pltpu.make_async_copy(r.dgroup, r.dgs, lsem.at[12]),
        pltpu.make_async_copy(r.alphat_own, r.als, lsem.at[13]),
        pltpu.make_async_copy(r.bgroup, r.sm_g, lsem.at[14]),
        pltpu.make_async_copy(r.bindex, r.sm_i, lsem.at[15]),
        pltpu.make_async_copy(r.pindex, r.sm_p, lsem.at[16]),
        pltpu.make_async_copy(r.ptable, r.sm_t, lsem.at[17]),
    ]
    for load in small[:1] + loads[:1]:
        load.start()
    barrier = pltpu.get_barrier_semaphore()
    ex.kw.greet(barrier)
    ex.xbn.greet(barrier)
    for load in small[1:] + loads[1:]:
        load.start()
    pl.semaphore_wait(barrier, W * N // 2 - 1 + N - 1)

    def xcopy(src, dst, k, p):
        return pltpu.make_async_remote_copy(
            src_ref=src, dst_ref=dst, send_sem=r.x_s.at[k], recv_sem=r.x_r.at[k],
            device_id={"narrow": p}, device_id_type=MESH)

    cuts = (0, R * 4 // 16, R * 8 // 16, R * 10 // 16, R)
    P = len(cuts) - 1

    def piece(k, src=None, slot=None):
        rows = pl.ds(cuts[k], cuts[k + 1] - cuts[k])
        slot = ni if slot is None else slot
        src = xg.at[slot, rows] if src is None else src.at[rows]
        return src, xg.at[slot, rows]

    def x_side():
        return xcopy(r.data_x, xg.at[ni], 0, n1)

    def x_over(k):
        return xcopy(*piece(k, r.data_x), 1 + k, n2)

    def x_pass(k):
        return xcopy(*piece(k, slot=n2), 1 + P + k, n1)

    small[0].wait()
    r.xbn[ni] = r.xbs[...].astype(F32)
    ex.xbn.gather(r.xbn)
    x_over(0).start()
    for load in small[1:]:
        load.wait()
    r.ad[ni, 0:S, :] = r.als[...]
    r.ad[ni, S : S + 1, :] = r.dgs[...].astype(F32)

    def ad_copy(slot, k, p):
        return xcopy(r.ad.at[slot], r.ad.at[slot], 9 + k, p)

    ad_copy(ni, 1, n2).start()
    ad_copy(ni, 0, n1).start()
    lane = lax.broadcasted_iota(jnp.int32, (1, 128), 1)
    for k in range(Bg):
        prec_k = r.sm_t[r.sm_p[k]]
        r.meta[wi, k : k + 1, :] = jnp.where(
            lane == 0, r.sm_g[k].astype(F32), jnp.where(lane == 1, r.sm_i[k].astype(F32), jnp.where(lane == 2, prec_k, 0.0)))
    r.meta[wi, :, S : 2 * S] = r.tgs[...]
    ex.meta.gather(r.meta)

    loads[0].wait()

    def cast1(k, carry):
        rows = pl.ds(pl.multiple_of(k * 128, 128), 128)
        w1b[rows, :] = r.w1f[rows, :].astype(BF)
        return carry

    lax.fori_loop(0, D // 128, cast1, 0)
    ex.xbn.wait(r.xbn)
    for n in range(N):
        r.xbg[n * brow : (n + 1) * brow, :] = r.xbn[n]
    xbg = r.xbg[...]
    hb, gb = gelu_pair(dot(xbg.astype(BF), w1b[...]))
    hb = hb.astype(BF).astype(F32)
    r.hbn[ni] = jnp.concatenate([hb[:, : Hn // 2], hb[:, Hn // 2 :]], axis=0).astype(BF)
    ex.hbn.gather(r.hbn)
    x_over(1).start()
    x_over(2).start()
    x_side().start()
    r.hgw[wi] = jnp.concatenate([hb, gb], axis=0).astype(BF)
    ex.hgw.gather(r.hgw)
    r.xbw[wi] = jnp.concatenate([xbg[:, : D // 2], xbg[:, D // 2 :]], axis=0).astype(BF)
    ex.xbw.gather(r.xbw)
    loads[2].wait()

    def cast2(k, carry):
        rows = pl.ds(pl.multiple_of(k * 128, 128), 128)
        w2b[rows, :] = r.w2f[rows, :].astype(BF)
        return carry

    lax.fori_loop(0, H // 128, cast2, 0)

    def block(q, first=0, last=P):
        base = q * R + cuts[first]
        size = cuts[last] - cuts[first]
        r.pre[:size, :] = dot(xg[q, cuts[first] : cuts[last], :], w1b[...])
        step = math.gcd(size, 32)

        def part(k, carry):
            src = pl.ds(pl.multiple_of(k * step, step), step)
            dst = pl.ds(pl.multiple_of(base + k * step, step), step)
            out, slope = gelu_pair(r.pre[src, :])
            hid[dst, :] = out.astype(BF)
            gd[dst, :] = slope
            return carry

        lax.fori_loop(0, size // step, part, 0)

    def turn(q):
        xT[:, pl.ds(pl.multiple_of(q * R, R), R)] = xg[q].T

    ex.hbn.wait(r.hbn)
    hbn = [r.hbn[n].astype(F32) for n in range(N)]
    hid_g = jnp.concatenate([h[k * Bg : (k + 1) * Bg] for h in hbn for k in range(2)], axis=1).astype(BF)
    bfeat = dot(hid_g, w2b[...]).astype(BF)
    r.bfs[...] = bfeat.astype(F32)
    gpart = dot(bfeat, w2b[...], NT)
    for n in range(N):
        g = gpart[:, n * Hn : (n + 1) * Hn]
        r.ges[n] = jnp.concatenate([g[:, : Hn // 2], g[:, Hn // 2 :]], axis=0).astype(BF)
    ex.ger.scatter(r.ges, r.ger)
    r.ger[ni] = r.ges[ni]
    loads[3].wait()
    zpart = dot(r.bfs[...].astype(BF), om[...])
    for n in range(N):
        z = zpart[:, n * Mn : (n + 1) * Mn]
        r.zes[n] = jnp.concatenate([z[:, : Mn // 2], z[:, Mn // 2 :]], axis=0).astype(BF)
    ex.zer.scatter(r.zes, r.zer)
    r.zer[ni] = r.zes[ni]
    x_over(3).start()
    later = []
    if resident:
        pairs = ((r.w1_m, r.m1), (r.w1_v, r.v1), (r.w2_m, r.m2), (r.w2_v, r.v2))
        later = [pltpu.make_async_copy(src, dst, lsem.at[5 + k]) for k, (src, dst) in enumerate(pairs)]
    for load in later:
        load.start()
    bf32 = r.bfs[...]
    r.bfw[wi] = jnp.concatenate([bf32[:, : Fn // 2], bf32[:, Fn // 2 :]], axis=0).astype(BF)
    loads[1].wait()
    block(ni)
    xcopy(r.data_x, xg.at[n1], 0, n1).wait_recv()
    block(n1)
    turn(ni)
    turn(n1)
    ex.ger.wait(r.ger)
    r.gw[wi] = jnp.sum(r.ger[...].astype(F32), axis=0).astype(BF)
    ex.gw.gather(r.gw)
    for k in range(3):
        xcopy(*piece(k, slot=n2), 1 + k, n2).wait_recv()
        x_pass(k).start()
    ad_copy(n2, 1, n2).wait_recv()
    ad_copy(n2, 2, n1).start()
    ex.zer.wait(r.zer)
    own_b = pl.ds(pl.multiple_of(wi * Bg, Bg), Bg)
    loads[5].wait()
    zeta = jnp.sum(r.zer[...].astype(F32), axis=0)
    angle = jnp.concatenate([zeta[:Bg], zeta[Bg:]], axis=1) + r.ph[...]
    r.cz[...] = jnp.zeros_like(r.cz)
    r.cz[own_b, :] = scale * jnp.cos(angle)
    sz = scale * jnp.sin(angle)
    r.szw[wi] = jnp.concatenate([sz[:, : Mn // 2], sz[:, Mn // 2 :]], axis=0).astype(BF)
    ex.szw.gather(r.szw)
    loads[4].wait()
    r.prior[...] = dot(r.pwt[...], r.cz[...], NT, HIGH)

    def x_last(k):
        xcopy(*piece(k, slot=n3), 1 + P + k, n1).wait_recv()

    block(n2, 0, 2)
    x_last(0)
    x_last(1)
    block(n3, 0, 2)
    ex.meta.wait(r.meta)
    meta = r.meta[...].reshape(B, 128)
    r.metat[...] = meta.T
    ad_copy(n1, 0, n1).wait_recv()
    ad_copy(n3, 2, n1).wait_recv()
    alphat = jnp.concatenate([r.ad[n, 0:S, :] for n in range(N)], axis=1)
    r.alphat[...] = alphat
    group = jnp.concatenate([r.ad[n, S : S + 1, :] for n in range(N)], axis=1)
    pmask = (0.5 + (meta[:, 0:1] == group).astype(F32)) / F
    r.pmask[...] = pmask
    col = lax.broadcasted_iota(jnp.int32, (1, N * R), 1) + wi * (N * R)
    first = (ni == 0).astype(F32)
    r.amat[...] = jnp.where(meta[:, 1:2] == col.astype(F32), first / meta[:, 2:3], 0.0)
    ex.gw.wait(r.gw)
    gw = r.gw[...].astype(F32)
    r.gmat[...] = jnp.concatenate([gw[:, :Bg].reshape(B, Hn // 2), gw[:, Bg:].reshape(B, Hn // 2)], axis=1).astype(BF)

    def columns(q, first=0, last=P):
        size = cuts[last] - cuts[first]
        return pl.ds(pl.multiple_of(q * R + cuts[first], size), size)

    def kernel_block(cols):
        r.amat[:, cols] = r.pmask[:, cols] * dot(r.gmat[...], hid[cols, :], NT) + r.amat[:, cols]

    def kalpha(cols):
        return dot(r.alphat[:, cols], r.amat[:, cols], NT, HIGH)

    for q in (ni, n1):
        kernel_block(columns(q))
    xcopy(*piece(3, slot=n2), 4, n2).wait_recv()
    x_pass(3).start()
    for q in (n2, n3):
        kernel_block(columns(q, 0, 2))
    block(n2, 2, 4)
    kernel_block(columns(n2, 2, 4))
    kal = r.prior[...] + (kalpha(columns(ni)) + kalpha(columns(n1))) + (kalpha(columns(n2)) + kalpha(columns(n3, 0, 2)))
    r.prior[...] = kal
    x_last(2)
    x_last(3)
    block(n3, 2, 4)

    kernel_block(columns(n3, 2, 4))
    kal = r.prior[...] + kalpha(columns(n3, 2, 4))
    fold = max(1, min(S // 8, 128 // B))
    r.kn[core] = jnp.concatenate([kal[k * (S // fold) : (k + 1) * (S // fold)] for k in range(fold)], axis=1)

    def core_copy(buf, k):
        return xcopy(buf.at[core], buf.at[core], 12 + k, n1)

    def core_sum(buf, k):
        xcopy(buf.at[1 - core], buf.at[1 - core], 12 + k, n1).wait_recv()
        return buf[0] + buf[1]

    core_copy(r.kn, 0).start()
    chip = wi * (N // 2) + side
    r.kw[chip] = core_sum(r.kn, 0)
    ex.kw.gather(r.kw)
    ex.bfw.gather(r.bfw)
    turn(n2)
    turn(n3)
    ex.hgw.wait(r.hgw)
    hg = r.hgw[...].astype(F32)
    r.hbx[ni] = hg[:, :Bg].reshape(B, Hn).astype(BF)
    r.gb[...] = hg[:, Bg:].reshape(B, Hn)
    ex.hbx.gather(r.hbx)
    ex.xbw.wait(r.xbw)
    xbw = r.xbw[...].astype(F32)
    r.xbt[...] = jnp.concatenate([xbw[:, :Bg].reshape(B, D // 2), xbw[:, Bg:].reshape(B, D // 2)], axis=1).T.astype(BF)
    prec = r.metat[2:3, :]
    total = jnp.sum(prec, axis=1, keepdims=True)
    ex.kw.wait(r.kw)
    kal = jnp.sum(r.kw[...], axis=0)
    resid = r.metat[S : 2 * S, :] - jnp.concatenate([kal[:, k * B : (k + 1) * B] for k in range(fold)], axis=0)
    grt = prec * resid / total

    ds = (-r.pmask[...] * dot(grt, r.alphat[...], TN, HIGH)).astype(BF)
    upart = dot(ds, hid[...]).reshape(W, Bg, Hn)
    r.us[...] = jnp.concatenate([upart[:, :, : Hn // 2], upart[:, :, Hn // 2 :]], axis=1).astype(BF)
    ex.ur.scatter(r.us, r.ur)
    for q in range(N):
        rows = slice(q * R, (q + 1) * R)
        dpre[rows, :] = (dot(ds[:, rows], r.gmat[...], TN) * gd[rows, :]).astype(BF)

    def wcopy(src, dst, kind, k, slot, p):
        return pltpu.make_async_remote_copy(
            src_ref=src, dst_ref=dst, send_sem=getattr(r, kind + "_s").at[k], recv_sem=getattr(r, kind + "_r").at[slot],
            device_id={"wide": p}, device_id_type=MESH)

    psend, precv, zsend, zrecv, gat = r.psend, r.precv, r.zsend, r.zrecv, r.gat

    NH = math.gcd(Ck // 16, 4)
    Hk = Ck // NH
    Q, Cq = 1, Hk

    def grad_rows(row):
        return dot(xT[pl.ds(pl.multiple_of(row, Ck), Ck), :], dpre[...])

    def target(step):
        low = a // (A // 2)
        m = a + low * (A - 1 - 2 * a)
        single = A - 1 - 2 * m
        late = (step // single + A - 1) // A
        e = step - single
        t = (1 - late) * (A - 1 - step) + late * (m + (1 - lax.rem(e + 2 * A, 2) * 2) * (m - (e + 2 * A) // 2 + A))
        return t + low * (A - 1 - 2 * t)

    def pcopy(ap, h, q):
        rows = pl.ds(pl.multiple_of(ap * Ck + h * Hk + q * Cq, Cq), Cq)
        return wcopy(psend.at[rows], precv.at[rows], "p", 0, ap * NH * Q + h * Q + q, pair)

    def rows_of(ap):
        return pl.ds(pl.multiple_of(ap * Ck, Ck), Ck)

    def pair_first(ap):
        psend[rows_of(ap), :] = grad_rows((1 - b) * half + ap * Ck).astype(BF)
        pcopy(ap, 0, 0).start()

    def pair_sends(h, first, last):
        def send(step, carry):
            pcopy(target(step), h, 0).start()
            return carry

        if h < NH:
            lax.fori_loop(min(first, A - 1), min(last, A - 1), send, 0)
            if last >= A:
                pcopy(a, h, 0).start()

    def zcopy(ap, h, q):
        rows = pl.ds(h * Hk + q * Cq, Cq)
        return wcopy(zsend.at[ap, rows], zrecv.at[a, rows], "z", 0, h, 2 * ap + b)

    def own_part(ap, carry):
        gd[rows_of(ap), :] = grad_rows(b * half + ap * Ck)
        return carry

    def z_part(ap, h):
        pcopy(ap, h, 0).wait_recv()
        rows = pl.ds(pl.multiple_of(ap * Ck + h * Hk, Hk), Hk)
        return gd[rows, :] + precv[rows, :].astype(F32)

    def z_sends(h, first, last):
        def send(step, carry):
            ap = target(step)
            zsend[ap, h * Hk : (h + 1) * Hk, :] = z_part(ap, h).astype(BF)
            zcopy(ap, h, 0).start()
            return carry

        if h < NH:
            lax.fori_loop(min(first, A - 1), min(last, A - 1), send, 0)

    def z_own(h):
        if h < NH:
            r.zf[h * Hk : (h + 1) * Hk, :] = z_part(a, h)

    def first_sends(step, carry):
        pair_first(target(step))
        return carry

    lax.fori_loop(0, A - 1, first_sends, 0)
    pair_first(a)
    pair_sends(1, 0, 2)

    loss = 0.5 * jnp.sum(jnp.sum(prec * (resid * resid), axis=1, keepdims=True), axis=0, keepdims=True)
    agt = -dot(grt, r.amat[...], precision=HIGH)
    for n in range(N):
        r.ags[n] = agt[:, n * R : (n + 1) * R]
    ex.agr.scatter(r.ags, r.agr)
    r.agr[ni] = r.ags[ni]
    ex.szw.wait(r.szw)

    def unfold(buf):
        v = buf[...].astype(F32)
        return jnp.concatenate([v[:, :Bg].reshape(B, -1), v[:, Bg:].reshape(B, -1)], axis=1)

    r.dzn[ni] = (unfold(r.szw) * dot(grt, r.pwt[...], TN, HIGH)).astype(BF)

    def dz_copy(slot, k, p):
        return xcopy(r.dzn.at[slot], r.dzn.at[slot], 17 + k, p)

    dz_copy(ni, 1, n2).start()
    dz_copy(ni, 0, n1).start()
    lax.fori_loop(0, A, own_part, 0)
    ex.ur.wait(r.ur)
    r.ur[wi] = r.us[wi]
    r.uz[wi] = jnp.sum(r.ur[...].astype(F32), axis=0).astype(BF)
    ex.uz.gather(r.uz)
    pair_sends(1, 2, A)
    for h in range(2, NH):
        pair_sends(h, 0, A)
    z_sends(0, 0, A)
    z_own(0)
    z_sends(1, 0, 1)
    ex.bfw.wait(r.bfw)
    ex.uz.wait(r.uz)
    r.uzn[ni] = unfold(r.uz).astype(BF)

    def u_copy(slot, k, p):
        return xcopy(r.uzn.at[slot], r.uzn.at[slot], 14 + k, p)

    u_copy(ni, 1, n2).start()
    u_copy(ni, 0, n1).start()
    dz_copy(n2, 1, n2).wait_recv()
    dz_copy(n2, 2, n1).start()
    z_sends(1, 1, A)
    z_own(1)

    others = pl.ds(0, A - 1)
    mine = b * A + a

    def shard(slot, h=0, q=0, count=Ck):
        return pl.ds(pl.multiple_of(slot * Ck + h * Hk + q * Cq, min(count, Cq)), count)

    def fcopy(ap, h, q):
        rows = shard(b * A + ap, h, q, Cq)
        return wcopy(gat.at[rows], gat.at[rows], "f", 0, 0, pair)

    def gcopy(ap, h, q, way):
        rows = shard(b * A + ap, h, q, Cq)
        return wcopy(gat.at[rows], gat.at[rows], "g", 0 if way > 0 else 1, (ap * NH + h) * Q + q, 2 * (a + way) + b)

    def straight(h):
        return NH > 1 and h >= NH - DIRECT

    def gdirect(ap, h, q):
        rows = shard(mine, h, q, Cq)
        return wcopy(gat.at[rows], gat.at[rows], "g", 2, (a * NH + h) * Q + q, 2 * ap + b)

    def z_done(h):
        if h >= NH:
            return
        rows = slice(h * Hk, (h + 1) * Hk)
        part = pl.ds(h * Hk, Hk)
        wcopy(zsend.at[others, part], zrecv.at[others, part], "z", 0, h, pair).wait_recv()

        def gain(k, carry):
            r.zf[rows, :] = r.zf[rows, :] + zrecv[lax.rem(a + k, A), rows, :].astype(F32)
            return carry

        lax.fori_loop(1, A, gain, 0)
        gat[shard(mine, h, 0, Hk), :] = r.zf[rows, :].astype(BF)
        for q in range(Q):
            fcopy(a, h, q).start()
        if straight(h):

            def send(step, carry):
                for q in range(Q):
                    gdirect(target(step), h, q).start()
                return carry

            lax.fori_loop(0, A - 1, send, 0)
        else:
            for q in range(Q):

                @pl.when(a + 1 < A)
                def _():
                    gcopy(a, h, q, 1).start()

                @pl.when(a > 0)
                def _():
                    gcopy(a, h, q, -1).start()

    def g_pass(h, first, last):
        if h >= NH:
            return

        def step(k, carry):
            below, above = a - 1 - k // Q, a + 1 + k // Q
            q = lax.rem(k, Q)

            @pl.when(below >= 0)
            def _():
                gcopy(below, h, q, 1).wait_recv()

                if not straight(h):

                    @pl.when(a + 1 < A)
                    def _():
                        gcopy(below, h, q, 1).start()

                fcopy(below, h, q).start()

            @pl.when(above < A)
            def _():
                gcopy(above, h, q, -1).wait_recv()

                if not straight(h):

                    @pl.when(a > 0)
                    def _():
                        gcopy(above, h, q, -1).start()

                fcopy(above, h, q).start()

            return carry

        lax.fori_loop(min(first, A - 1) * Q, min(last, A - 1) * Q, step, 0)

    z_done(0)
    z_sends(2, 0, A)
    z_own(2)
    u_copy(n2, 1, n2).wait_recv()
    u_copy(n2, 2, n1).start()
    z_done(1)
    g_pass(0, 0, 1)
    z_sends(3, 0, 2)
    z_done(2)
    z_sends(3, 2, A)
    z_own(3)
    u_copy(n1, 0, n1).wait_recv()
    u_copy(n3, 2, n1).wait_recv()
    dz_copy(n1, 0, n1).wait_recv()
    dz_copy(n3, 2, n1).wait_recv()
    acc = jnp.zeros((B, Fn), F32)
    for n in range(N):
        acc = acc + dot(r.uzn[n], w2b[n * Hn : (n + 1) * Hn, :])
        acc = acc + dot(r.dzn[n], om[:, n * Mn : (n + 1) * Mn], NT)
    r.db[...] = jnp.concatenate([acc, unfold(r.bfw)], axis=0).astype(BF)
    for n in range(N):
        r.dhs[n] = dot(r.db[:B, :], w2b[n * Hn : (n + 1) * Hn, :], NT).astype(BF)
    ex.dhr.scatter(r.dhs, r.dhr)
    r.dhr[ni] = r.dhs[ni]
    g_pass(1, 0, 1)
    g_pass(0, 1, 2)
    g_pass(2, 0, 1)
    z_done(3)
    g_pass(1, 1, 2)

    def two(v):
        return jnp.sum(jnp.sum(v * v, axis=1, keepdims=True), axis=0, keepdims=True)

    square = jnp.zeros((1, 1), F32)
    for n in range(N):
        if n == 0:
            ex.hbx.wait(r.hbx)
        hu = jnp.concatenate([r.hbx[n], r.uzn[n]], axis=0)
        g2 = dot(hu, r.db[...], TN)
        r.g2[n * Hn : (n + 1) * Hn, :] = g2
        square = square + two(g2)

    ex.agr.wait(r.agr)
    agt = jnp.sum(r.agr[...], axis=0)
    r.agrad[...] = agt
    ex.dhr.wait(r.dhr)
    r.dpb[...] = (jnp.sum(r.dhr[...].astype(F32), axis=0) * r.gb[...]).astype(BF)

    square = square * (1.0 / W) + two(r.zf[...] + dot(r.xbt[shard(mine), :], r.dpb[...])) + two(agt)
    r.nn[core] = jnp.broadcast_to(square, (8, 128))
    core_copy(r.nn, 1).start()
    g_pass(0, 2, A)
    r.nw[chip] = core_sum(r.nn, 1)
    ex.nw.gather(r.nw)
    g_pass(2, 1, 2)
    g_pass(3, 0, 1)
    g_pass(1, 2, A)
    g_pass(2, 2, A)
    g_pass(3, 1, A)
    ex.nw.wait(r.nw)
    norm = jnp.sum(r.nw[...], axis=0)
    lanes = lax.broadcasted_iota(jnp.int32, (8, 128), 1)
    r.scal[...] = jnp.where(lanes == 0, loss, jnp.where(lanes == 1, total, norm))

    theirs = pl.ds(pl.multiple_of((1 - b) * half, half), half)
    ours = pl.ds(pl.multiple_of(b * half, half), half)
    wcopy(gat.at[theirs], gat.at[theirs], "f", 0, 0, pair).wait_recv()

    for name in live:
        vars(ex)[name].drain(getattr(r, name))
    x_side().wait_send()
    for k in range(P):
        x_over(k).wait_send()
        x_pass(k).wait_send()
    for slot, k, p in ((ni, 0, n1), (ni, 1, n2), (n2, 2, n1)):
        ad_copy(slot, k, p).wait_send()
        u_copy(slot, k, p).wait_send()
        dz_copy(slot, k, p).wait_send()
    core_copy(r.kn, 0).wait_send()
    core_copy(r.nn, 1).wait_send()
    wcopy(psend, precv, "p", 0, 0, pair).wait_send()
    wcopy(gat.at[ours], gat.at[ours], "f", 0, 0, pair).wait_send()
    wcopy(zsend.at[others], zrecv.at[others], "z", 0, 0, pair).wait_send()
    straights = sum(straight(h) for h in range(NH))
    if straights:
        direct = pl.ds(0, (A - 1) * Hk * straights)
        wcopy(gat.at[direct], gat.at[direct], "g", 2, 0, pair).wait_send()
    for k in range(A):
        up, down = (pl.ds(0, n * Hk * (NH - straights)) for n in (k + 1, A - k))

        @pl.when((a == k) & (a + 1 < A))
        def _():
            wcopy(gat.at[up], gat.at[up], "g", 0, 0, pair).wait_send()

        @pl.when((a == k) & (a > 0))
        def _():
            wcopy(gat.at[down], gat.at[down], "g", 1, 0, pair).wait_send()

    for load in later:
        load.wait()


CORR1 = 1.0 - 0.9**STEP_NUM
CORR2 = 1.0 - 0.999**STEP_NUM


def adamw(weight, grad, moment, second, rate, decay):
    moment_new = 0.9 * moment + 0.1 * grad
    second_new = 0.999 * second + 0.001 * grad * grad
    step = moment_new / (jnp.sqrt(second_new) * (1.0 / math.sqrt(CORR2)) + 1e-08)
    new = weight * (1.0 - rate * decay) - (rate / CORR1) * step
    return moment_new, second_new, new


def update_kernel(resident, slots, C, names, *refs):
    r = SimpleNamespace(**dict(zip(names, refs)))
    if not resident:
        pairs = ((r.w1, r.w1f), (r.w1_m, r.m1), (r.w1_v, r.v1), (r.w2, r.w2f), (r.w2_m, r.m2), (r.w2_v, r.v2))
        loads = [pltpu.make_async_copy(src, dst, r.lsem.at[k]) for k, (src, dst) in enumerate(pairs)]
        for load in loads:
            load.start()
        for load in loads:
            load.wait()
    for k in range(3):
        r.s3[k] = r.scal[0:1, k : k + 1]
    last = [pltpu.make_async_copy(r.s3.at[k], dst, r.asem.at[3 + k]) for k, dst in enumerate((r.loss, r.total, r.normsq))]
    for copy in last:
        copy.start()
    small = [pltpu.make_async_copy(src, r.asl.at[k], r.asem.at[k]) for k, src in enumerate((r.at, r.atm, r.atv))]
    for load in small:
        load.start()
    norm = r.scal[0:1, 2:3]
    clip = jnp.minimum(1.0, 0.1 / jnp.sqrt(norm))
    ring = (r.sm, r.sv, r.sn, r.sc)

    def copies(outs, slot, rows):
        return [pltpu.make_async_copy(buf.at[slot], out.at[rows], r.osem.at[slot, k]) for k, (buf, out) in enumerate(zip(ring, outs))]

    def chunk(grad, state, outs, k, ahead):
        w, m, v = state
        slot = lax.rem(k + ahead, slots)
        base = pl.multiple_of(k * C, C)
        rows = pl.ds(base, C)

        def drain():
            for copy in copies(outs, slot, rows):
                copy.wait()

        if ahead:
            drain()
        else:
            pl.when(k >= slots)(drain)

        def part(j, carry):
            src = pl.ds(pl.multiple_of(base + j * 16, 16), 16)
            dst = pl.ds(pl.multiple_of(j * 16, 16), 16)
            mn, vn, wn = adamw(w[src, :], clip * grad[src, :], m[src, :], v[src, :], 0.03, 0.01)
            r.sm[slot, dst, :] = mn
            r.sv[slot, dst, :] = vn
            r.sn[slot, dst, :] = wn
            r.sc[slot, dst, :] = wn.astype(BF)
            return carry

        lax.fori_loop(0, C // 16, part, 0, unroll=True)
        for copy in copies(outs, slot, rows):
            copy.start()

    outs1 = (r.m1o, r.v1o, r.n1o, r.c1o)
    outs2 = (r.m2o, r.v2o, r.n2o, r.c2o)
    count1, count2 = r.w1f.shape[0] // C, r.w2f.shape[0] // C

    def step2(k, carry):
        chunk(r.g2, (r.w2f, r.m2, r.v2), outs2, k, 0)
        return carry

    def step1(k, carry):
        chunk(r.gs, (r.w1f, r.m1, r.v1), outs1, k, count2)
        return carry

    lax.fori_loop(0, count2, step2, 0)
    r.gs[...] = r.gat[...].astype(F32) + dot(r.xbt[...], r.dpb[...])
    lax.fori_loop(0, count1, step1, 0)
    for load in small:
        load.wait()
    am, av, an = adamw(r.asl[0], clip * r.agrad[...], r.asl[1], r.asl[2], 0.2, 0.0)
    for k, v in enumerate((am, av, an)):
        r.ast[k] = v
    alphas = [pltpu.make_async_copy(r.ast.at[k], dst, r.asem.at[k]) for k, dst in enumerate((r.amo, r.avo, r.ano))]
    for copy in alphas:
        copy.start()
    for k in range(slots):
        for copy in copies(outs1, k, pl.ds(0, C)):
            copy.wait()
    for copy in last + alphas:
        copy.wait()


def on_device(
    data_x, data_group, batch_x, batch_group, batch_index, prec_index, prec_table, targets,
    omega, phase, prior_w, w1_master, w1_moment, w1_second, w2_master, w2_moment, w2_second,
    alpha, alpha_moment, alpha_second,
):
    W, N = lax.axis_size("wide"), lax.axis_size("narrow")
    A = W // 2
    R, D = data_x.shape
    brow, Bg, S = batch_x.shape[0], targets.shape[0], targets.shape[1]
    F, M = omega.shape
    Hn, Fn, Mn, H = w1_master.shape[1], w2_master.shape[1], M // N, w2_master.shape[0]
    B, Ck = W * Bg, D // 2 // A
    hbm, vmem = (pl.BlockSpec(memory_space=m) for m in (pl.ANY, pltpu.VMEM))
    resident = B <= 128
    fold = max(1, min(S // 8, 128 // B))
    args = dict(
        data_x=(data_x, hbm), dgroup=(data_group.reshape(1, R), hbm), batch_x=(batch_x, hbm),
        bgroup=(batch_group, hbm), bindex=(batch_index, hbm), pindex=(prec_index, hbm),
        ptable=(prec_table, hbm), targets=(targets, hbm), omega=(omega, hbm),
        phase=(phase.reshape(1, M), hbm), prior_wt=(prior_w.T, hbm), w1=(w1_master, hbm),
        w2=(w2_master, hbm), alphat_own=(alpha.T, hbm),
    )
    state = dict(
        w1=(w1_master, hbm), w1_m=(w1_moment, hbm), w1_v=(w1_second, hbm),
        w2=(w2_master, hbm), w2_m=(w2_moment, hbm), w2_v=(w2_second, hbm),
    )
    outs = dict(
        scal=((8, 128), F32), agrad=((S, R), F32), gat=((D, Hn), BF), xbt=((D, B), BF), dpb=((B, Hn), BF),
        g2=((H, Fn), F32),
    )
    held = dict(
        w1f=((D, Hn), F32), m1=((D, Hn), F32), v1=((D, Hn), F32), w2f=((H, Fn), F32), m2=((H, Fn), F32), v2=((H, Fn), F32),
    )
    scratch = dict(
        xg=((N, R, D), BF), xT=((D, N * R), BF), hid=((N * R, Hn), BF), gd=((N * R, Hn), F32),
        dpre=((N * R, Hn), BF), pre=((R, Hn), F32), w1b=((D, Hn), BF),
        w2b=((H, Fn), BF), om=((Fn, M), BF), pwt=((S, Mn), F32),
        xbg=((Bg, D), F32), xbs=((brow, D), BF), tgs=((Bg, S), F32), dgs=((1, R), jnp.int32), als=((S, R), F32), ph=((1, Mn), F32), ges=((N, 2 * Bg, Hn // 2), BF), zes=((N, 2 * Bg, Mn // 2), BF), bfs=((Bg, Fn), F32), zf=((Ck, Hn), F32), us=((W, 2 * Bg, Hn // 2), BF), ags=((N, S, R), F32),
        dhs=((N, B, Hn), BF), cz=((B, Mn), F32), prior=((S, B), F32),
        metat=((128, B), F32), alphat=((S, N * R), F32), pmask=((B, N * R), F32), amat=((B, N * R), F32),
        gmat=((B, Hn), BF), db=((2 * B, Fn), BF),
        psend=((A * Ck, Hn), BF), precv=((A * Ck, Hn), BF), zsend=((A, Ck, Hn), BF), zrecv=((A + 1, Ck, Hn), BF),
        gb=((B, Hn), F32),
        meta=((W, Bg, 128), F32), xbw=((W, 2 * Bg, D // 2), BF), hgw=((W, 2 * Bg, Hn), BF),
        bfw=((W, 2 * Bg, Fn // 2), BF), gw=((W, 2 * Bg, Hn // 2), BF), kw=((W * N // 2, S // fold, fold * B), F32),
        ur=((W, 2 * Bg, Hn // 2), BF), uz=((W, 2 * Bg, Hn // 2), BF), szw=((W, 2 * Bg, Mn // 2), BF), nw=((W * N // 2, 8, 128), F32),
        xbn=((N, brow, D), F32), ad=((N, S + 1, R), F32), hbn=((N, 2 * Bg, Hn // 2), BF), ger=((N, 2 * Bg, Hn // 2), BF), zer=((N, 2 * Bg, Mn // 2), BF),
        kn=((2, S // fold, fold * B), F32), agr=((N, S, R), F32), uzn=((N, B, Hn), BF), dzn=((N, B, Mn), BF), hbx=((N, B, Hn), BF), dhr=((N, B, Hn), BF),
        nn=((2, 8, 128), F32),
    )
    if resident:
        args.update(state)
        outs.update(held)
    else:
        scratch.update(w1f=held["w1f"], w2f=held["w2f"])
    pieces = A * math.gcd(Ck // 16, 4)
    count = 2 * len(WIDE_EX + NARROW_EX + CHIP_EX)
    sems = [("lsem", 18), ("x_s", 20), ("x_r", 20), ("es", count), ("p_s", 1), ("p_r", pieces), ("z_s", 1), ("z_r", 4)]
    sems += [("f_s", 1), ("f_r", 1), ("g_s", 3), ("g_r", pieces)]
    smem = dict(sm_g=(Bg, jnp.int32), sm_i=(Bg, jnp.int32), sm_p=(Bg, jnp.int32), sm_t=(prec_table.shape[0], F32))
    names = [*args, *outs, *scratch, *smem] + [n for n, _ in sems]
    grads = pl.pallas_call(
        lambda *refs: step_kernel(W, N, resident, names, *refs),
        out_shape=[(pltpu.VMEM if resident else jax.ShapeDtypeStruct)(s, t) for s, t in outs.values()],
        in_specs=[spec for _, spec in args.values()],
        out_specs=[vmem] * len(outs),
        scratch_shapes=[pltpu.VMEM(s, t) for s, t in scratch.values()]
        + [pltpu.SMEM((k,), t) for k, t in smem.values()]
        + [pltpu.SemaphoreType.DMA((k,)) for _, k in sems],
        compiler_params=pltpu.CompilerParams(collective_id=0, has_side_effects=True, vmem_limit_bytes=(62 if not resident else 39) * 2**20),
        name="gradients",
    )(*[v for v, _ in args.values()])

    args2 = {k: (v, vmem) for k, v in zip(outs, grads)}
    args2.update(at=(alpha.T, hbm), atm=(alpha_moment.T, hbm), atv=(alpha_second.T, hbm))
    C, slots = 256, 4
    outs2 = dict(amo=((S, R), F32, hbm), avo=((S, R), F32, hbm), ano=((S, R), F32, hbm))
    outs2.update(loss=((1, 1), F32, hbm), total=((1, 1), F32, hbm), normsq=((1, 1), F32, hbm))
    for k, shape in (("1", (D, Hn)), ("2", (H, Fn))):
        outs2.update({"m" + k + "o": (shape, F32, hbm), "v" + k + "o": (shape, F32, hbm)})
        outs2.update({"n" + k + "o": (shape, F32, hbm), "c" + k + "o": (shape, BF, hbm)})
    scratch2 = dict(
        gs=pltpu.VMEM((D, Hn), F32), sm=pltpu.VMEM((slots, C, Hn), F32), sv=pltpu.VMEM((slots, C, Hn), F32),
        sn=pltpu.VMEM((slots, C, Hn), F32), sc=pltpu.VMEM((slots, C, Hn), BF), osem=pltpu.SemaphoreType.DMA((slots, 4)),
        asl=pltpu.VMEM((3, S, R), F32), ast=pltpu.VMEM((3, S, R), F32), asem=pltpu.SemaphoreType.DMA((6,)), s3=pltpu.VMEM((3, 1, 1), F32),
    )
    if not resident:
        args2.update(state)
        scratch2.update({k: pltpu.VMEM(s, t) for k, (s, t) in held.items()}, lsem=pltpu.SemaphoreType.DMA((6,)))
    names2 = [*args2, *outs2, *scratch2]
    new = pl.pallas_call(
        lambda *refs: update_kernel(resident, slots, C, names2, *refs),
        out_shape=[jax.ShapeDtypeStruct(s, t) for s, t, _ in outs2.values()],
        in_specs=[spec for _, spec in args2.values()],
        out_specs=[spec for _, _, spec in outs2.values()],
        scratch_shapes=list(scratch2.values()),
        compiler_params=pltpu.CompilerParams(vmem_limit_bytes=(36 if not resident else 12) * 2**20),
        name="adamw",
    )(*[v for v, _ in args2.values()])
    new = dict(zip(outs2, new))
    return (
        new["loss"].reshape(()), new["total"].reshape(()), new["normsq"].reshape(()),
        new["m1o"], new["v1o"], new["n1o"], new["c1o"],
        new["m2o"], new["v2o"], new["n2o"], new["c2o"],
        new["amo"].T, new["avo"].T, new["ano"].T,
    )


def solution(mesh):
    both = P(("wide", "narrow"))
    both2 = P(("wide", "narrow"), None)
    col = P(None, "narrow")
    return jax.shard_map(
        on_device,
        mesh=mesh,
        in_specs=(both2, both, both2, P("wide"), P("wide"), P("wide"), P(), P("wide", None), P(), P(), P())
        + (col,) * 6 + (both2,) * 3,
        out_specs=(P(), P(), P()) + (col,) * 8 + (both2,) * 3,
        check_vma=False,
    )
```

```python
import math
from types import SimpleNamespace

import jax
import jax.numpy as jnp
from jax import lax
from jax.experimental import pallas as pl
from jax.experimental.pallas import tpu as pltpu
from jax.sharding import PartitionSpec as P

STEP_NUM = 10
HIGH = lax.Precision.HIGHEST
MESH = pl.DeviceIdType.MESH
GC = math.sqrt(2.0 / math.pi)
F32 = jnp.float32
BF = jnp.bfloat16
DIRECT = 1


def gelu_pair(pre):
    square = pre * pre
    t = jnp.tanh(pre * (GC + (GC * 0.044715) * square))
    half = 0.5 * (1.0 + t)
    slope = half + 0.5 * pre * (1.0 - t * t) * (GC + (3 * GC * 0.044715) * square)
    return pre * half, slope


def dot(left, right, dims=((1,), (0,)), precision=None):
    return lax.dot_general(left, right, (dims, ((), ())), precision=precision, preferred_element_type=F32)


NT = ((1,), (1,))
TN = ((0,), (0,))


class Exchange:
    def __init__(self, size, me, where, sems, k):
        self.size, self.me, self.where, self.sems, self.k = size, me, where, sems, k

    def copy(self, src, dst, p):
        return pltpu.make_async_remote_copy(
            src_ref=src, dst_ref=dst, send_sem=self.sems.at[self.k], recv_sem=self.sems.at[self.k + 1],
            device_id=self.where(p), device_id_type=MESH)

    def loop(self, body):
        def step(k, carry):
            body(lax.rem(self.me + k, self.size))
            return carry

        lax.fori_loop(1, self.size, step, 0)

    def greet(self, barrier):
        self.loop(lambda p: pl.semaphore_signal(barrier, inc=1, device_id=self.where(p), device_id_type=MESH))

    def gather(self, buf):
        self.loop(lambda p: self.copy(buf.at[self.me], buf.at[self.me], p).start())

    def scatter(self, src, buf):
        self.loop(lambda p: self.copy(src.at[p], buf.at[self.me], p).start())

    def all(self, buf):
        others = buf.at[pl.ds(0, self.size - 1)]
        return self.copy(others, others, lax.rem(self.me + 1, self.size))

    def wait(self, buf):
        self.all(buf).wait_recv()

    def drain(self, buf):
        self.all(buf).wait_send()


WIDE_EX = ("meta", "xbw", "hgw", "bfw", "gw", "szw", "ur", "uz")
NARROW_EX = ("xbn", "hbn", "ger", "zer", "agr", "hbx", "dhr")
CHIP_EX = ("kw", "nw")


def step_kernel(W, N, resident, names, *refs):
    r = SimpleNamespace(**dict(zip(names, refs)))
    wi, ni = lax.axis_index("wide"), lax.axis_index("narrow")
    A = W // 2
    a, b = wi // 2, lax.rem(wi, 2)
    pair = wi + 1 - 2 * b
    n1 = ni + 1 - 2 * lax.rem(ni, 2)
    n2 = lax.rem(ni + 2, N)
    n3 = lax.rem(n1 + 2, N)
    xg, hid, gd, xT, dpre = r.xg, r.hid, r.gd, r.xT, r.dpre
    w1b, w2b, om = r.w1b, r.w2b, r.om
    _, R, D = xg.shape
    Bg, S = r.targets.shape
    brow = r.batch_x.shape[0]
    Hn, Fn = w1b.shape[1], w2b.shape[1]
    H, F, M = w2b.shape[0], r.omega.shape[0], r.omega.shape[1]
    Mn = M // N
    B = W * Bg
    half = D // 2
    Ck = half // A
    scale = math.sqrt(2.0 / M)
    lsem = r.lsem
    core, side = lax.rem(ni, 2), ni // 2
    groups = (
        (WIDE_EX, W, wi, lambda p: {"wide": p}),
        (NARROW_EX, N, ni, lambda p: {"narrow": p}),
        (CHIP_EX, W * N // 2, wi * (N // 2) + side, lambda p: {"wide": p // (N // 2), "narrow": lax.rem(p, N // 2) * 2 + core}),
    )
    ex, live = SimpleNamespace(), []
    for group, size, me, where in groups:
        for name in group:
            vars(ex)[name] = Exchange(size, me, where, r.es, 2 * len(live))
            live.append(name)

    own_f = pl.ds(pl.multiple_of(ni * Fn, Fn), Fn)
    own_m = pl.ds(pl.multiple_of(ni * Mn, Mn), Mn)
    loads = [
        pltpu.make_async_copy(r.w1, r.w1f, lsem.at[0]),
        pltpu.make_async_copy(r.data_x, xg.at[ni], lsem.at[1]),
        pltpu.make_async_copy(r.w2, r.w2f, lsem.at[2]),
        pltpu.make_async_copy(r.omega.at[own_f], om, lsem.at[3]),
        pltpu.make_async_copy(r.prior_wt.at[:, own_m], r.pwt, lsem.at[4]),
        pltpu.make_async_copy(r.phase.at[:, own_m], r.ph, lsem.at[9]),
    ]
    small = [
        pltpu.make_async_copy(r.batch_x, r.xbs, lsem.at[10]),
        pltpu.make_async_copy(r.targets, r.tgs, lsem.at[11]),
        pltpu.make_async_copy(r.dgroup, r.dgs, lsem.at[12]),
        pltpu.make_async_copy(r.alphat_own, r.als, lsem.at[13]),
        pltpu.make_async_copy(r.bgroup, r.sm_g, lsem.at[14]),
        pltpu.make_async_copy(r.bindex, r.sm_i, lsem.at[15]),
        pltpu.make_async_copy(r.pindex, r.sm_p, lsem.at[16]),
        pltpu.make_async_copy(r.ptable, r.sm_t, lsem.at[17]),
    ]
    for load in small[:1] + loads[:1]:
        load.start()
    barrier = pltpu.get_barrier_semaphore()
    ex.kw.greet(barrier)
    ex.xbn.greet(barrier)
    for load in small[1:] + loads[1:]:
        load.start()
    pl.semaphore_wait(barrier, W * N // 2 - 1 + N - 1)

    def xcopy(src, dst, k, p):
        return pltpu.make_async_remote_copy(
            src_ref=src, dst_ref=dst, send_sem=r.x_s.at[k], recv_sem=r.x_r.at[k],
            device_id={"narrow": p}, device_id_type=MESH)

    cuts = (0, R * 4 // 16, R * 8 // 16, R * 10 // 16, R)
    P = len(cuts) - 1

    def piece(k, src=None, slot=None):
        rows = pl.ds(cuts[k], cuts[k + 1] - cuts[k])
        slot = ni if slot is None else slot
        src = xg.at[slot, rows] if src is None else src.at[rows]
        return src, xg.at[slot, rows]

    def x_side():
        return xcopy(r.data_x, xg.at[ni], 0, n1)

    def x_over(k):
        return xcopy(*piece(k, r.data_x), 1 + k, n2)

    def x_pass(k):
        return xcopy(*piece(k, slot=n2), 1 + P + k, n1)

    small[0].wait()
    r.xbn[ni] = r.xbs[...].astype(F32)
    ex.xbn.gather(r.xbn)
    x_over(0).start()
    for load in small[1:]:
        load.wait()
    r.ad[ni, 0:S, :] = r.als[...]
    r.ad[ni, S : S + 1, :] = r.dgs[...].astype(F32)

    def ad_copy(slot, k, p):
        return xcopy(r.ad.at[slot], r.ad.at[slot], 9 + k, p)

    ad_copy(ni, 1, n2).start()
    ad_copy(ni, 0, n1).start()
    lane = lax.broadcasted_iota(jnp.int32, (1, 128), 1)
    for k in range(Bg):
        prec_k = r.sm_t[r.sm_p[k]]
        r.meta[wi, k : k + 1, :] = jnp.where(
            lane == 0, r.sm_g[k].astype(F32), jnp.where(lane == 1, r.sm_i[k].astype(F32), jnp.where(lane == 2, prec_k, 0.0)))
    r.meta[wi, :, S : 2 * S] = r.tgs[...]
    ex.meta.gather(r.meta)

    loads[0].wait()

    def cast1(k, carry):
        rows = pl.ds(pl.multiple_of(k * 128, 128), 128)
        w1b[rows, :] = r.w1f[rows, :].astype(BF)
        return carry

    lax.fori_loop(0, D // 128, cast1, 0)
    ex.xbn.wait(r.xbn)
    for n in range(N):
        r.xbg[n * brow : (n + 1) * brow, :] = r.xbn[n]
    xbg = r.xbg[...]
    hb, gb = gelu_pair(dot(xbg.astype(BF), w1b[...]))
    hb = hb.astype(BF).astype(F32)
    r.hbn[ni] = jnp.concatenate([hb[:, : Hn // 2], hb[:, Hn // 2 :]], axis=0).astype(BF)
    ex.hbn.gather(r.hbn)
    x_over(1).start()
    x_over(2).start()
    x_side().start()
    r.hgw[wi] = jnp.concatenate([hb, gb], axis=0).astype(BF)
    ex.hgw.gather(r.hgw)
    r.xbw[wi] = jnp.concatenate([xbg[:, : D // 2], xbg[:, D // 2 :]], axis=0).astype(BF)
    ex.xbw.gather(r.xbw)
    loads[2].wait()

    def cast2(k, carry):
        rows = pl.ds(pl.multiple_of(k * 128, 128), 128)
        w2b[rows, :] = r.w2f[rows, :].astype(BF)
        return carry

    lax.fori_loop(0, H // 128, cast2, 0)

    def block(q, first=0, last=P):
        base = q * R + cuts[first]
        size = cuts[last] - cuts[first]
        r.pre[:size, :] = dot(xg[q, cuts[first] : cuts[last], :], w1b[...])
        step = math.gcd(size, 32)

        def part(k, carry):
            src = pl.ds(pl.multiple_of(k * step, step), step)
            dst = pl.ds(pl.multiple_of(base + k * step, step), step)
            out, slope = gelu_pair(r.pre[src, :])
            hid[dst, :] = out.astype(BF)
            gd[dst, :] = slope
            return carry

        lax.fori_loop(0, size // step, part, 0)

    def turn(q):
        xT[:, pl.ds(pl.multiple_of(q * R, R), R)] = xg[q].T

    ex.hbn.wait(r.hbn)
    hbn = [r.hbn[n].astype(F32) for n in range(N)]
    hid_g = jnp.concatenate([h[k * Bg : (k + 1) * Bg] for h in hbn for k in range(2)], axis=1).astype(BF)
    bfeat = dot(hid_g, w2b[...]).astype(BF)
    r.bfs[...] = bfeat.astype(F32)
    gpart = dot(bfeat, w2b[...], NT)
    for n in range(N):
        g = gpart[:, n * Hn : (n + 1) * Hn]
        r.ges[n] = jnp.concatenate([g[:, : Hn // 2], g[:, Hn // 2 :]], axis=0).astype(BF)
    ex.ger.scatter(r.ges, r.ger)
    r.ger[ni] = r.ges[ni]
    loads[3].wait()
    zpart = dot(r.bfs[...].astype(BF), om[...])
    for n in range(N):
        z = zpart[:, n * Mn : (n + 1) * Mn]
        r.zes[n] = jnp.concatenate([z[:, : Mn // 2], z[:, Mn // 2 :]], axis=0).astype(BF)
    ex.zer.scatter(r.zes, r.zer)
    r.zer[ni] = r.zes[ni]
    x_over(3).start()
    later = []
    if resident:
        pairs = ((r.w1_m, r.m1), (r.w1_v, r.v1), (r.w2_m, r.m2), (r.w2_v, r.v2))
        later = [pltpu.make_async_copy(src, dst, lsem.at[5 + k]) for k, (src, dst) in enumerate(pairs)]
    for load in later:
        load.start()
    bf32 = r.bfs[...]
    r.bfw[wi] = jnp.concatenate([bf32[:, : Fn // 2], bf32[:, Fn // 2 :]], axis=0).astype(BF)
    loads[1].wait()
    block(ni)
    xcopy(r.data_x, xg.at[n1], 0, n1).wait_recv()
    block(n1)
    turn(ni)
    turn(n1)
    ex.ger.wait(r.ger)
    r.gw[wi] = jnp.sum(r.ger[...].astype(F32), axis=0).astype(BF)
    ex.gw.gather(r.gw)
    for k in range(3):
        xcopy(*piece(k, slot=n2), 1 + k, n2).wait_recv()
        x_pass(k).start()
    ad_copy(n2, 1, n2).wait_recv()
    ad_copy(n2, 2, n1).start()
    ex.zer.wait(r.zer)
    own_b = pl.ds(pl.multiple_of(wi * Bg, Bg), Bg)
    loads[5].wait()
    zeta = jnp.sum(r.zer[...].astype(F32), axis=0)
    angle = jnp.concatenate([zeta[:Bg], zeta[Bg:]], axis=1) + r.ph[...]
    r.cz[...] = jnp.zeros_like(r.cz)
    r.cz[own_b, :] = scale * jnp.cos(angle)
    sz = scale * jnp.sin(angle)
    r.szw[wi] = jnp.concatenate([sz[:, : Mn // 2], sz[:, Mn // 2 :]], axis=0).astype(BF)
    ex.szw.gather(r.szw)
    loads[4].wait()
    r.prior[...] = dot(r.pwt[...], r.cz[...], NT, HIGH)

    def x_last(k):
        xcopy(*piece(k, slot=n3), 1 + P + k, n1).wait_recv()

    block(n2, 0, 2)
    x_last(0)
    x_last(1)
    block(n3, 0, 2)
    ex.meta.wait(r.meta)
    meta = r.meta[...].reshape(B, 128)
    r.metat[...] = meta.T
    ad_copy(n1, 0, n1).wait_recv()
    ad_copy(n3, 2, n1).wait_recv()
    alphat = jnp.concatenate([r.ad[n, 0:S, :] for n in range(N)], axis=1)
    r.alphat[...] = alphat
    group = jnp.concatenate([r.ad[n, S : S + 1, :] for n in range(N)], axis=1)
    pmask = (0.5 + (meta[:, 0:1] == group).astype(F32)) / F
    r.pmask[...] = pmask
    col = lax.broadcasted_iota(jnp.int32, (1, N * R), 1) + wi * (N * R)
    first = (ni == 0).astype(F32)
    r.amat[...] = jnp.where(meta[:, 1:2] == col.astype(F32), first / meta[:, 2:3], 0.0)
    ex.gw.wait(r.gw)
    gw = r.gw[...].astype(F32)
    r.gmat[...] = jnp.concatenate([gw[:, :Bg].reshape(B, Hn // 2), gw[:, Bg:].reshape(B, Hn // 2)], axis=1).astype(BF)

    def columns(q, first=0, last=P):
        size = cuts[last] - cuts[first]
        return pl.ds(pl.multiple_of(q * R + cuts[first], size), size)

    def kernel_block(cols):
        r.amat[:, cols] = r.pmask[:, cols] * dot(r.gmat[...], hid[cols, :], NT) + r.amat[:, cols]

    def kalpha(cols):
        return dot(r.alphat[:, cols], r.amat[:, cols], NT, HIGH)

    for q in (ni, n1):
        kernel_block(columns(q))
    xcopy(*piece(3, slot=n2), 4, n2).wait_recv()
    x_pass(3).start()
    for q in (n2, n3):
        kernel_block(columns(q, 0, 2))
    block(n2, 2, 4)
    kernel_block(columns(n2, 2, 4))
    kal = r.prior[...] + (kalpha(columns(ni)) + kalpha(columns(n1))) + (kalpha(columns(n2)) + kalpha(columns(n3, 0, 2)))
    r.prior[...] = kal
    x_last(2)
    x_last(3)
    block(n3, 2, 4)

    kernel_block(columns(n3, 2, 4))
    kal = r.prior[...] + kalpha(columns(n3, 2, 4))
    fold = max(1, min(S // 8, 128 // B))
    r.kn[core] = jnp.concatenate([kal[k * (S // fold) : (k + 1) * (S // fold)] for k in range(fold)], axis=1)

    def core_copy(buf, k):
        return xcopy(buf.at[core], buf.at[core], 12 + k, n1)

    def core_sum(buf, k):
        xcopy(buf.at[1 - core], buf.at[1 - core], 12 + k, n1).wait_recv()
        return buf[0] + buf[1]

    core_copy(r.kn, 0).start()
    chip = wi * (N // 2) + side
    r.kw[chip] = core_sum(r.kn, 0)
    ex.kw.gather(r.kw)
    ex.bfw.gather(r.bfw)
    turn(n2)
    turn(n3)
    ex.hgw.wait(r.hgw)
    hg = r.hgw[...].astype(F32)
    r.hbx[ni] = hg[:, :Bg].reshape(B, Hn).astype(BF)
    r.gb[...] = hg[:, Bg:].reshape(B, Hn)
    ex.hbx.gather(r.hbx)
    ex.xbw.wait(r.xbw)
    xbw = r.xbw[...].astype(F32)
    r.xbt[...] = jnp.concatenate([xbw[:, :Bg].reshape(B, D // 2), xbw[:, Bg:].reshape(B, D // 2)], axis=1).T.astype(BF)
    prec = r.metat[2:3, :]
    total = jnp.sum(prec, axis=1, keepdims=True)
    ex.kw.wait(r.kw)
    kal = jnp.sum(r.kw[...], axis=0)
    resid = r.metat[S : 2 * S, :] - jnp.concatenate([kal[:, k * B : (k + 1) * B] for k in range(fold)], axis=0)
    grt = prec * resid / total

    ds = (-r.pmask[...] * dot(grt, r.alphat[...], TN, HIGH)).astype(BF)
    upart = dot(ds, hid[...]).reshape(W, Bg, Hn)
    r.us[...] = jnp.concatenate([upart[:, :, : Hn // 2], upart[:, :, Hn // 2 :]], axis=1).astype(BF)
    ex.ur.scatter(r.us, r.ur)
    for q in range(N):
        rows = slice(q * R, (q + 1) * R)
        dpre[rows, :] = (dot(ds[:, rows], r.gmat[...], TN) * gd[rows, :]).astype(BF)

    def wcopy(src, dst, kind, k, slot, p):
        return pltpu.make_async_remote_copy(
            src_ref=src, dst_ref=dst, send_sem=getattr(r, kind + "_s").at[k], recv_sem=getattr(r, kind + "_r").at[slot],
            device_id={"wide": p}, device_id_type=MESH)

    psend, precv, zsend, zrecv, gat = r.psend, r.precv, r.zsend, r.zrecv, r.gat

    NH = math.gcd(Ck // 16, 4)
    Hk = Ck // NH
    Q, Cq = 1, Hk

    def grad_rows(row):
        return dot(xT[pl.ds(pl.multiple_of(row, Ck), Ck), :], dpre[...])

    def target(step):
        low = a // (A // 2)
        m = a + low * (A - 1 - 2 * a)
        single = A - 1 - 2 * m
        late = (step // single + A - 1) // A
        e = step - single
        t = (1 - late) * (A - 1 - step) + late * (m + (1 - lax.rem(e + 2 * A, 2) * 2) * (m - (e + 2 * A) // 2 + A))
        return t + low * (A - 1 - 2 * t)

    def pcopy(ap, h, q):
        rows = pl.ds(pl.multiple_of(ap * Ck + h * Hk + q * Cq, Cq), Cq)
        return wcopy(psend.at[rows], precv.at[rows], "p", 0, ap * NH * Q + h * Q + q, pair)

    def rows_of(ap):
        return pl.ds(pl.multiple_of(ap * Ck, Ck), Ck)

    def pair_first(ap):
        psend[rows_of(ap), :] = grad_rows((1 - b) * half + ap * Ck).astype(BF)
        pcopy(ap, 0, 0).start()

    def pair_sends(h, first, last):
        def send(step, carry):
            pcopy(target(step), h, 0).start()
            return carry

        if h < NH:
            lax.fori_loop(min(first, A - 1), min(last, A - 1), send, 0)
            if last >= A:
                pcopy(a, h, 0).start()

    def zcopy(ap, h, q):
        rows = pl.ds(h * Hk + q * Cq, Cq)
        return wcopy(zsend.at[ap, rows], zrecv.at[a, rows], "z", 0, h, 2 * ap + b)

    def own_part(ap, carry):
        gd[rows_of(ap), :] = grad_rows(b * half + ap * Ck)
        return carry

    def z_part(ap, h):
        pcopy(ap, h, 0).wait_recv()
        rows = pl.ds(pl.multiple_of(ap * Ck + h * Hk, Hk), Hk)
        return gd[rows, :] + precv[rows, :].astype(F32)

    def z_sends(h, first, last):
        def send(step, carry):
            ap = target(step)
            zsend[ap, h * Hk : (h + 1) * Hk, :] = z_part(ap, h).astype(BF)
            zcopy(ap, h, 0).start()
            return carry

        if h < NH:
            lax.fori_loop(min(first, A - 1), min(last, A - 1), send, 0)

    def z_own(h):
        if h < NH:
            r.zf[h * Hk : (h + 1) * Hk, :] = z_part(a, h)

    def first_sends(step, carry):
        pair_first(target(step))
        return carry

    lax.fori_loop(0, A - 1, first_sends, 0)
    pair_first(a)
    pair_sends(1, 0, 2)

    loss = 0.5 * jnp.sum(jnp.sum(prec * (resid * resid), axis=1, keepdims=True), axis=0, keepdims=True)
    agt = -dot(grt, r.amat[...], precision=HIGH)
    for n in range(N):
        r.ags[n] = agt[:, n * R : (n + 1) * R]
    ex.agr.scatter(r.ags, r.agr)
    r.agr[ni] = r.ags[ni]
    ex.szw.wait(r.szw)

    def unfold(buf):
        v = buf[...].astype(F32)
        return jnp.concatenate([v[:, :Bg].reshape(B, -1), v[:, Bg:].reshape(B, -1)], axis=1)

    r.dzn[ni] = (unfold(r.szw) * dot(grt, r.pwt[...], TN, HIGH)).astype(BF)

    def dz_copy(slot, k, p):
        return xcopy(r.dzn.at[slot], r.dzn.at[slot], 17 + k, p)

    dz_copy(ni, 1, n2).start()
    dz_copy(ni, 0, n1).start()
    lax.fori_loop(0, A, own_part, 0)
    ex.ur.wait(r.ur)
    r.ur[wi] = r.us[wi]
    r.uz[wi] = jnp.sum(r.ur[...].astype(F32), axis=0).astype(BF)
    ex.uz.gather(r.uz)
    pair_sends(1, 2, A)
    for h in range(2, NH):
        pair_sends(h, 0, A)
    z_sends(0, 0, A)
    z_own(0)
    z_sends(1, 0, 1)
    ex.bfw.wait(r.bfw)
    ex.uz.wait(r.uz)
    r.uzn[ni] = unfold(r.uz).astype(BF)

    def u_copy(slot, k, p):
        return xcopy(r.uzn.at[slot], r.uzn.at[slot], 14 + k, p)

    u_copy(ni, 1, n2).start()
    u_copy(ni, 0, n1).start()
    dz_copy(n2, 1, n2).wait_recv()
    dz_copy(n2, 2, n1).start()
    z_sends(1, 1, A)
    z_own(1)

    others = pl.ds(0, A - 1)
    mine = b * A + a

    def shard(slot, h=0, q=0, count=Ck):
        return pl.ds(pl.multiple_of(slot * Ck + h * Hk + q * Cq, min(count, Cq)), count)

    def fcopy(ap, h, q):
        rows = shard(b * A + ap, h, q, Cq)
        return wcopy(gat.at[rows], gat.at[rows], "f", 0, 0, pair)

    def gcopy(ap, h, q, way):
        rows = shard(b * A + ap, h, q, Cq)
        return wcopy(gat.at[rows], gat.at[rows], "g", 0 if way > 0 else 1, (ap * NH + h) * Q + q, 2 * (a + way) + b)

    def straight(h):
        return NH > 1 and h >= NH - DIRECT

    def gdirect(ap, h, q):
        rows = shard(mine, h, q, Cq)
        return wcopy(gat.at[rows], gat.at[rows], "g", 2, (a * NH + h) * Q + q, 2 * ap + b)

    def z_done(h):
        if h >= NH:
            return
        rows = slice(h * Hk, (h + 1) * Hk)
        part = pl.ds(h * Hk, Hk)
        wcopy(zsend.at[others, part], zrecv.at[others, part], "z", 0, h, pair).wait_recv()

        def gain(k, carry):
            r.zf[rows, :] = r.zf[rows, :] + zrecv[lax.rem(a + k, A), rows, :].astype(F32)
            return carry

        lax.fori_loop(1, A, gain, 0)
        gat[shard(mine, h, 0, Hk), :] = r.zf[rows, :].astype(BF)
        for q in range(Q):
            fcopy(a, h, q).start()
        if straight(h):

            def send(step, carry):
                for q in range(Q):
                    gdirect(target(step), h, q).start()
                return carry

            lax.fori_loop(0, A - 1, send, 0)
        else:
            for q in range(Q):

                @pl.when(a + 1 < A)
                def _():
                    gcopy(a, h, q, 1).start()

                @pl.when(a > 0)
                def _():
                    gcopy(a, h, q, -1).start()

    def g_pass(h, first, last):
        if h >= NH:
            return

        def step(k, carry):
            below, above = a - 1 - k // Q, a + 1 + k // Q
            q = lax.rem(k, Q)

            @pl.when(below >= 0)
            def _():
                gcopy(below, h, q, 1).wait_recv()

                if not straight(h):

                    @pl.when(a + 1 < A)
                    def _():
                        gcopy(below, h, q, 1).start()

                fcopy(below, h, q).start()

            @pl.when(above < A)
            def _():
                gcopy(above, h, q, -1).wait_recv()

                if not straight(h):

                    @pl.when(a > 0)
                    def _():
                        gcopy(above, h, q, -1).start()

                fcopy(above, h, q).start()

            return carry

        lax.fori_loop(min(first, A - 1) * Q, min(last, A - 1) * Q, step, 0)

    z_done(0)
    z_sends(2, 0, A)
    z_own(2)
    u_copy(n2, 1, n2).wait_recv()
    u_copy(n2, 2, n1).start()
    z_done(1)
    g_pass(0, 0, 1)
    z_sends(3, 0, 2)
    z_done(2)
    z_sends(3, 2, A)
    z_own(3)
    u_copy(n1, 0, n1).wait_recv()
    u_copy(n3, 2, n1).wait_recv()
    dz_copy(n1, 0, n1).wait_recv()
    dz_copy(n3, 2, n1).wait_recv()
    acc = jnp.zeros((B, Fn), F32)
    for n in range(N):
        acc = acc + dot(r.uzn[n], w2b[n * Hn : (n + 1) * Hn, :])
        acc = acc + dot(r.dzn[n], om[:, n * Mn : (n + 1) * Mn], NT)
    r.db[...] = jnp.concatenate([acc, unfold(r.bfw)], axis=0).astype(BF)
    for n in range(N):
        r.dhs[n] = dot(r.db[:B, :], w2b[n * Hn : (n + 1) * Hn, :], NT).astype(BF)
    ex.dhr.scatter(r.dhs, r.dhr)
    r.dhr[ni] = r.dhs[ni]
    g_pass(1, 0, 1)
    g_pass(0, 1, 2)
    g_pass(2, 0, 1)
    z_done(3)
    g_pass(1, 1, 2)

    def two(v):
        return jnp.sum(jnp.sum(v * v, axis=1, keepdims=True), axis=0, keepdims=True)

    square = jnp.zeros((1, 1), F32)
    for n in range(N):
        if n == 0:
            ex.hbx.wait(r.hbx)
        hu = jnp.concatenate([r.hbx[n], r.uzn[n]], axis=0)
        g2 = dot(hu, r.db[...], TN)
        r.g2[n * Hn : (n + 1) * Hn, :] = g2
        square = square + two(g2)

    ex.agr.wait(r.agr)
    agt = jnp.sum(r.agr[...], axis=0)
    r.agrad[...] = agt
    ex.dhr.wait(r.dhr)
    r.dpb[...] = (jnp.sum(r.dhr[...].astype(F32), axis=0) * r.gb[...]).astype(BF)

    square = square * (1.0 / W) + two(r.zf[...] + dot(r.xbt[shard(mine), :], r.dpb[...])) + two(agt)
    r.nn[core] = jnp.broadcast_to(square, (8, 128))
    core_copy(r.nn, 1).start()
    g_pass(0, 2, A)
    r.nw[chip] = core_sum(r.nn, 1)
    ex.nw.gather(r.nw)
    g_pass(2, 1, 2)
    g_pass(3, 0, 1)
    g_pass(1, 2, A)
    g_pass(2, 2, A)
    g_pass(3, 1, A)
    ex.nw.wait(r.nw)
    norm = jnp.sum(r.nw[...], axis=0)
    lanes = lax.broadcasted_iota(jnp.int32, (8, 128), 1)
    r.scal[...] = jnp.where(lanes == 0, loss, jnp.where(lanes == 1, total, norm))

    theirs = pl.ds(pl.multiple_of((1 - b) * half, half), half)
    ours = pl.ds(pl.multiple_of(b * half, half), half)
    wcopy(gat.at[theirs], gat.at[theirs], "f", 0, 0, pair).wait_recv()

    for name in live:
        vars(ex)[name].drain(getattr(r, name))
    x_side().wait_send()
    for k in range(P):
        x_over(k).wait_send()
        x_pass(k).wait_send()
    for slot, k, p in ((ni, 0, n1), (ni, 1, n2), (n2, 2, n1)):
        ad_copy(slot, k, p).wait_send()
        u_copy(slot, k, p).wait_send()
        dz_copy(slot, k, p).wait_send()
    core_copy(r.kn, 0).wait_send()
    core_copy(r.nn, 1).wait_send()
    wcopy(psend, precv, "p", 0, 0, pair).wait_send()
    wcopy(gat.at[ours], gat.at[ours], "f", 0, 0, pair).wait_send()
    wcopy(zsend.at[others], zrecv.at[others], "z", 0, 0, pair).wait_send()
    straights = sum(straight(h) for h in range(NH))
    if straights:
        direct = pl.ds(0, (A - 1) * Hk * straights)
        wcopy(gat.at[direct], gat.at[direct], "g", 2, 0, pair).wait_send()
    for k in range(A):
        up, down = (pl.ds(0, n * Hk * (NH - straights)) for n in (k + 1, A - k))

        @pl.when((a == k) & (a + 1 < A))
        def _():
            wcopy(gat.at[up], gat.at[up], "g", 0, 0, pair).wait_send()

        @pl.when((a == k) & (a > 0))
        def _():
            wcopy(gat.at[down], gat.at[down], "g", 1, 0, pair).wait_send()

    for load in later:
        load.wait()


CORR1 = 1.0 - 0.9**STEP_NUM
CORR2 = 1.0 - 0.999**STEP_NUM


def adamw(weight, grad, moment, second, rate, decay):
    moment_new = 0.9 * moment + 0.1 * grad
    second_new = 0.999 * second + 0.001 * grad * grad
    step = moment_new / (jnp.sqrt(second_new) * (1.0 / math.sqrt(CORR2)) + 1e-08)
    new = weight * (1.0 - rate * decay) - (rate / CORR1) * step
    return moment_new, second_new, new


def update_kernel(resident, slots, C, names, *refs):
    r = SimpleNamespace(**dict(zip(names, refs)))
    if not resident:
        pairs = ((r.w1, r.w1f), (r.w1_m, r.m1), (r.w1_v, r.v1), (r.w2, r.w2f), (r.w2_m, r.m2), (r.w2_v, r.v2))
        loads = [pltpu.make_async_copy(src, dst, r.lsem.at[k]) for k, (src, dst) in enumerate(pairs)]
        for load in loads:
            load.start()
        for load in loads:
            load.wait()
    for k in range(3):
        r.s3[k] = r.scal[0:1, k : k + 1]
    last = [pltpu.make_async_copy(r.s3.at[k], dst, r.asem.at[3 + k]) for k, dst in enumerate((r.loss, r.total, r.normsq))]
    for copy in last:
        copy.start()
    small = [pltpu.make_async_copy(src, r.asl.at[k], r.asem.at[k]) for k, src in enumerate((r.at, r.atm, r.atv))]
    for load in small:
        load.start()
    norm = r.scal[0:1, 2:3]
    clip = jnp.minimum(1.0, 0.1 / jnp.sqrt(norm))
    ring = (r.sm, r.sv, r.sn, r.sc)

    def copies(outs, slot, rows):
        return [pltpu.make_async_copy(buf.at[slot], out.at[rows], r.osem.at[slot, k]) for k, (buf, out) in enumerate(zip(ring, outs))]

    def chunk(grad, state, outs, k, ahead, split=1):
        w, m, v = state
        slot = lax.rem(k + ahead, slots)
        base = pl.multiple_of(k * C, C)
        rows = pl.ds(base, C)

        def drain():
            for copy in copies(outs, slot, rows):
                copy.wait()

        if ahead:
            drain()
        elif split == 1:
            pl.when(k >= slots)(drain)

        def part(j, carry):
            src = pl.ds(pl.multiple_of(base + j * 16, 16), 16)
            dst = pl.ds(pl.multiple_of(j * 16, 16), 16)
            mn, vn, wn = adamw(w[src, :], clip * grad[src, :], m[src, :], v[src, :], 0.03, 0.01)
            r.sm[slot, dst, :] = mn
            r.sv[slot, dst, :] = vn
            r.sn[slot, dst, :] = wn
            r.sc[slot, dst, :] = wn.astype(BF)
            return carry

        if split == 1:
            lax.fori_loop(0, C // 16, part, 0, unroll=True)
            for copy in copies(outs, slot, rows):
                copy.start()
            return
        size = C // split
        for n in range(split):
            lax.fori_loop(n * size // 16, (n + 1) * size // 16, part, 0, unroll=True)
            here = pl.ds(n * size, size)
            for i, (buf, out) in enumerate(zip(ring, outs)):
                pltpu.make_async_copy(buf.at[slot, here], out.at[here], r.osem.at[slot, i]).start()

    outs1 = (r.m1o, r.v1o, r.n1o, r.c1o)
    outs2 = (r.m2o, r.v2o, r.n2o, r.c2o)
    count1, count2 = r.w1f.shape[0] // C, r.w2f.shape[0] // C

    def step2(k, carry):
        chunk(r.g2, (r.w2f, r.m2, r.v2), outs2, k, 0)
        return carry

    def step1(k, carry):
        chunk(r.gs, (r.w1f, r.m1, r.v1), outs1, k, count2)
        return carry

    chunk(r.g2, (r.w2f, r.m2, r.v2), outs2, 0, 0, split=C // 64)
    lax.fori_loop(1, count2, step2, 0)
    r.gs[...] = r.gat[...].astype(F32) + dot(r.xbt[...], r.dpb[...])
    lax.fori_loop(0, count1, step1, 0)
    for load in small:
        load.wait()
    am, av, an = adamw(r.asl[0], clip * r.agrad[...], r.asl[1], r.asl[2], 0.2, 0.0)
    for k, v in enumerate((am, av, an)):
        r.ast[k] = v
    alphas = [pltpu.make_async_copy(r.ast.at[k], dst, r.asem.at[k]) for k, dst in enumerate((r.amo, r.avo, r.ano))]
    for copy in alphas:
        copy.start()
    for k in range(slots):
        for copy in copies(outs1, k, pl.ds(0, C)):
            copy.wait()
    for copy in last + alphas:
        copy.wait()


def on_device(
    data_x, data_group, batch_x, batch_group, batch_index, prec_index, prec_table, targets,
    omega, phase, prior_w, w1_master, w1_moment, w1_second, w2_master, w2_moment, w2_second,
    alpha, alpha_moment, alpha_second,
):
    W, N = lax.axis_size("wide"), lax.axis_size("narrow")
    A = W // 2
    R, D = data_x.shape
    brow, Bg, S = batch_x.shape[0], targets.shape[0], targets.shape[1]
    F, M = omega.shape
    Hn, Fn, Mn, H = w1_master.shape[1], w2_master.shape[1], M // N, w2_master.shape[0]
    B, Ck = W * Bg, D // 2 // A
    hbm, vmem = (pl.BlockSpec(memory_space=m) for m in (pl.ANY, pltpu.VMEM))
    resident = B <= 128
    fold = max(1, min(S // 8, 128 // B))
    args = dict(
        data_x=(data_x, hbm), dgroup=(data_group.reshape(1, R), hbm), batch_x=(batch_x, hbm),
        bgroup=(batch_group, hbm), bindex=(batch_index, hbm), pindex=(prec_index, hbm),
        ptable=(prec_table, hbm), targets=(targets, hbm), omega=(omega, hbm),
        phase=(phase.reshape(1, M), hbm), prior_wt=(prior_w.T, hbm), w1=(w1_master, hbm),
        w2=(w2_master, hbm), alphat_own=(alpha.T, hbm),
    )
    state = dict(
        w1=(w1_master, hbm), w1_m=(w1_moment, hbm), w1_v=(w1_second, hbm),
        w2=(w2_master, hbm), w2_m=(w2_moment, hbm), w2_v=(w2_second, hbm),
    )
    outs = dict(
        scal=((8, 128), F32), agrad=((S, R), F32), gat=((D, Hn), BF), xbt=((D, B), BF), dpb=((B, Hn), BF),
        g2=((H, Fn), F32),
    )
    held = dict(
        w1f=((D, Hn), F32), m1=((D, Hn), F32), v1=((D, Hn), F32), w2f=((H, Fn), F32), m2=((H, Fn), F32), v2=((H, Fn), F32),
    )
    scratch = dict(
        xg=((N, R, D), BF), xT=((D, N * R), BF), hid=((N * R, Hn), BF), gd=((N * R, Hn), F32),
        dpre=((N * R, Hn), BF), pre=((R, Hn), F32), w1b=((D, Hn), BF),
        w2b=((H, Fn), BF), om=((Fn, M), BF), pwt=((S, Mn), F32),
        xbg=((Bg, D), F32), xbs=((brow, D), BF), tgs=((Bg, S), F32), dgs=((1, R), jnp.int32), als=((S, R), F32), ph=((1, Mn), F32), ges=((N, 2 * Bg, Hn // 2), BF), zes=((N, 2 * Bg, Mn // 2), BF), bfs=((Bg, Fn), F32), zf=((Ck, Hn), F32), us=((W, 2 * Bg, Hn // 2), BF), ags=((N, S, R), F32),
        dhs=((N, B, Hn), BF), cz=((B, Mn), F32), prior=((S, B), F32),
        metat=((128, B), F32), alphat=((S, N * R), F32), pmask=((B, N * R), F32), amat=((B, N * R), F32),
        gmat=((B, Hn), BF), db=((2 * B, Fn), BF),
        psend=((A * Ck, Hn), BF), precv=((A * Ck, Hn), BF), zsend=((A, Ck, Hn), BF), zrecv=((A + 1, Ck, Hn), BF),
        gb=((B, Hn), F32),
        meta=((W, Bg, 128), F32), xbw=((W, 2 * Bg, D // 2), BF), hgw=((W, 2 * Bg, Hn), BF),
        bfw=((W, 2 * Bg, Fn // 2), BF), gw=((W, 2 * Bg, Hn // 2), BF), kw=((W * N // 2, S // fold, fold * B), F32),
        ur=((W, 2 * Bg, Hn // 2), BF), uz=((W, 2 * Bg, Hn // 2), BF), szw=((W, 2 * Bg, Mn // 2), BF), nw=((W * N // 2, 8, 128), F32),
        xbn=((N, brow, D), F32), ad=((N, S + 1, R), F32), hbn=((N, 2 * Bg, Hn // 2), BF), ger=((N, 2 * Bg, Hn // 2), BF), zer=((N, 2 * Bg, Mn // 2), BF),
        kn=((2, S // fold, fold * B), F32), agr=((N, S, R), F32), uzn=((N, B, Hn), BF), dzn=((N, B, Mn), BF), hbx=((N, B, Hn), BF), dhr=((N, B, Hn), BF),
        nn=((2, 8, 128), F32),
    )
    if resident:
        args.update(state)
        outs.update(held)
    else:
        scratch.update(w1f=held["w1f"], w2f=held["w2f"])
    pieces = A * math.gcd(Ck // 16, 4)
    count = 2 * len(WIDE_EX + NARROW_EX + CHIP_EX)
    sems = [("lsem", 18), ("x_s", 20), ("x_r", 20), ("es", count), ("p_s", 1), ("p_r", pieces), ("z_s", 1), ("z_r", 4)]
    sems += [("f_s", 1), ("f_r", 1), ("g_s", 3), ("g_r", pieces)]
    smem = dict(sm_g=(Bg, jnp.int32), sm_i=(Bg, jnp.int32), sm_p=(Bg, jnp.int32), sm_t=(prec_table.shape[0], F32))
    names = [*args, *outs, *scratch, *smem] + [n for n, _ in sems]
    grads = pl.pallas_call(
        lambda *refs: step_kernel(W, N, resident, names, *refs),
        out_shape=[(pltpu.VMEM if resident else jax.ShapeDtypeStruct)(s, t) for s, t in outs.values()],
        in_specs=[spec for _, spec in args.values()],
        out_specs=[vmem] * len(outs),
        scratch_shapes=[pltpu.VMEM(s, t) for s, t in scratch.values()]
        + [pltpu.SMEM((k,), t) for k, t in smem.values()]
        + [pltpu.SemaphoreType.DMA((k,)) for _, k in sems],
        compiler_params=pltpu.CompilerParams(collective_id=0, has_side_effects=True, vmem_limit_bytes=(62 if not resident else 39) * 2**20),
        name="gradients",
    )(*[v for v, _ in args.values()])

    args2 = {k: (v, vmem) for k, v in zip(outs, grads)}
    args2.update(at=(alpha.T, hbm), atm=(alpha_moment.T, hbm), atv=(alpha_second.T, hbm))
    C, slots = 256, 4
    outs2 = dict(amo=((S, R), F32, hbm), avo=((S, R), F32, hbm), ano=((S, R), F32, hbm))
    outs2.update(loss=((1, 1), F32, hbm), total=((1, 1), F32, hbm), normsq=((1, 1), F32, hbm))
    for k, shape in (("1", (D, Hn)), ("2", (H, Fn))):
        outs2.update({"m" + k + "o": (shape, F32, hbm), "v" + k + "o": (shape, F32, hbm)})
        outs2.update({"n" + k + "o": (shape, F32, hbm), "c" + k + "o": (shape, BF, hbm)})
    scratch2 = dict(
        gs=pltpu.VMEM((D, Hn), F32), sm=pltpu.VMEM((slots, C, Hn), F32), sv=pltpu.VMEM((slots, C, Hn), F32),
        sn=pltpu.VMEM((slots, C, Hn), F32), sc=pltpu.VMEM((slots, C, Hn), BF), osem=pltpu.SemaphoreType.DMA((slots, 4)),
        asl=pltpu.VMEM((3, S, R), F32), ast=pltpu.VMEM((3, S, R), F32), asem=pltpu.SemaphoreType.DMA((6,)), s3=pltpu.VMEM((3, 1, 1), F32),
    )
    if not resident:
        args2.update(state)
        scratch2.update({k: pltpu.VMEM(s, t) for k, (s, t) in held.items()}, lsem=pltpu.SemaphoreType.DMA((6,)))
    names2 = [*args2, *outs2, *scratch2]
    new = pl.pallas_call(
        lambda *refs: update_kernel(resident, slots, C, names2, *refs),
        out_shape=[jax.ShapeDtypeStruct(s, t) for s, t, _ in outs2.values()],
        in_specs=[spec for _, spec in args2.values()],
        out_specs=[spec for _, _, spec in outs2.values()],
        scratch_shapes=list(scratch2.values()),
        compiler_params=pltpu.CompilerParams(vmem_limit_bytes=(36 if not resident else 12) * 2**20),
        name="adamw",
    )(*[v for v, _ in args2.values()])
    new = dict(zip(outs2, new))
    return (
        new["loss"].reshape(()), new["total"].reshape(()), new["normsq"].reshape(()),
        new["m1o"], new["v1o"], new["n1o"], new["c1o"],
        new["m2o"], new["v2o"], new["n2o"], new["c2o"],
        new["amo"].T, new["avo"].T, new["ano"].T,
    )


def solution(mesh):
    both = P(("wide", "narrow"))
    both2 = P(("wide", "narrow"), None)
    col = P(None, "narrow")
    return jax.shard_map(
        on_device,
        mesh=mesh,
        in_specs=(both2, both, both2, P("wide"), P("wide"), P("wide"), P(), P("wide", None), P(), P(), P())
        + (col,) * 6 + (both2,) * 3,
        out_specs=(P(), P(), P()) + (col,) * 8 + (both2,) * 3,
        check_vma=False,
    )
```

```python
import math
from types import SimpleNamespace

import jax
import jax.numpy as jnp
from jax import lax
from jax.experimental import pallas as pl
from jax.experimental.pallas import tpu as pltpu
from jax.sharding import PartitionSpec as P

STEP_NUM = 10
HIGH = lax.Precision.HIGHEST
MESH = pl.DeviceIdType.MESH
GC = math.sqrt(2.0 / math.pi)
F32 = jnp.float32
BF = jnp.bfloat16
DIRECT = 1


def gelu_pair(pre):
    square = pre * pre
    t = jnp.tanh(pre * (GC + (GC * 0.044715) * square))
    half = 0.5 * (1.0 + t)
    slope = half + 0.5 * pre * (1.0 - t * t) * (GC + (3 * GC * 0.044715) * square)
    return pre * half, slope


def dot(left, right, dims=((1,), (0,)), precision=None):
    return lax.dot_general(left, right, (dims, ((), ())), precision=precision, preferred_element_type=F32)


NT = ((1,), (1,))
TN = ((0,), (0,))


class Exchange:
    def __init__(self, size, me, where, sems, k):
        self.size, self.me, self.where, self.sems, self.k = size, me, where, sems, k

    def copy(self, src, dst, p):
        return pltpu.make_async_remote_copy(
            src_ref=src, dst_ref=dst, send_sem=self.sems.at[self.k], recv_sem=self.sems.at[self.k + 1],
            device_id=self.where(p), device_id_type=MESH)

    def loop(self, body):
        def step(k, carry):
            body(lax.rem(self.me + k, self.size))
            return carry

        lax.fori_loop(1, self.size, step, 0)

    def greet(self, barrier):
        self.loop(lambda p: pl.semaphore_signal(barrier, inc=1, device_id=self.where(p), device_id_type=MESH))

    def gather(self, buf):
        self.loop(lambda p: self.copy(buf.at[self.me], buf.at[self.me], p).start())

    def scatter(self, src, buf):
        self.loop(lambda p: self.copy(src.at[p], buf.at[self.me], p).start())

    def all(self, buf):
        others = buf.at[pl.ds(0, self.size - 1)]
        return self.copy(others, others, lax.rem(self.me + 1, self.size))

    def wait(self, buf):
        self.all(buf).wait_recv()

    def drain(self, buf):
        self.all(buf).wait_send()


WIDE_EX = ("meta", "xbw", "hgw", "bfw", "gw", "szw", "ur", "uz")
NARROW_EX = ("xbn", "hbn", "ger", "zer", "agr", "hbx", "dhr")
CHIP_EX = ("kw", "nw")


def step_kernel(W, N, resident, names, *refs):
    r = SimpleNamespace(**dict(zip(names, refs)))
    wi, ni = lax.axis_index("wide"), lax.axis_index("narrow")
    A = W // 2
    a, b = wi // 2, lax.rem(wi, 2)
    pair = wi + 1 - 2 * b
    n1 = ni + 1 - 2 * lax.rem(ni, 2)
    n2 = lax.rem(ni + 2, N)
    n3 = lax.rem(n1 + 2, N)
    xg, hid, gd, xT, dpre = r.xg, r.hid, r.gd, r.xT, r.dpre
    w1b, w2b, om = r.w1b, r.w2b, r.om
    _, R, D = xg.shape
    Bg, S = r.targets.shape
    brow = r.batch_x.shape[0]
    Hn, Fn = w1b.shape[1], w2b.shape[1]
    H, F, M = w2b.shape[0], r.omega.shape[0], r.omega.shape[1]
    Mn = M // N
    B = W * Bg
    half = D // 2
    Ck = half // A
    scale = math.sqrt(2.0 / M)
    lsem = r.lsem
    core, side = lax.rem(ni, 2), ni // 2
    groups = (
        (WIDE_EX, W, wi, lambda p: {"wide": p}),
        (NARROW_EX, N, ni, lambda p: {"narrow": p}),
        (CHIP_EX, W * N // 2, wi * (N // 2) + side, lambda p: {"wide": p // (N // 2), "narrow": lax.rem(p, N // 2) * 2 + core}),
    )
    ex, live = SimpleNamespace(), []
    for group, size, me, where in groups:
        for name in group:
            vars(ex)[name] = Exchange(size, me, where, r.es, 2 * len(live))
            live.append(name)

    own_f = pl.ds(pl.multiple_of(ni * Fn, Fn), Fn)
    own_m = pl.ds(pl.multiple_of(ni * Mn, Mn), Mn)
    loads = [
        pltpu.make_async_copy(r.w1, r.w1f, lsem.at[0]),
        pltpu.make_async_copy(r.data_x, xg.at[ni], lsem.at[1]),
        pltpu.make_async_copy(r.w2, r.w2f, lsem.at[2]),
        pltpu.make_async_copy(r.omega.at[own_f], om, lsem.at[3]),
        pltpu.make_async_copy(r.prior_wt.at[:, own_m], r.pwt, lsem.at[4]),
        pltpu.make_async_copy(r.phase.at[:, own_m], r.ph, lsem.at[9]),
    ]
    small = [
        pltpu.make_async_copy(r.batch_x, r.xbs, lsem.at[10]),
        pltpu.make_async_copy(r.targets, r.tgs, lsem.at[11]),
        pltpu.make_async_copy(r.dgroup, r.dgs, lsem.at[12]),
        pltpu.make_async_copy(r.alphat_own, r.als, lsem.at[13]),
        pltpu.make_async_copy(r.bgroup, r.sm_g, lsem.at[14]),
        pltpu.make_async_copy(r.bindex, r.sm_i, lsem.at[15]),
        pltpu.make_async_copy(r.pindex, r.sm_p, lsem.at[16]),
        pltpu.make_async_copy(r.ptable, r.sm_t, lsem.at[17]),
    ]
    for load in small[:1] + loads[:1]:
        load.start()
    barrier = pltpu.get_barrier_semaphore()
    ex.kw.greet(barrier)
    ex.xbn.greet(barrier)
    for load in small[1:] + loads[1:]:
        load.start()
    pl.semaphore_wait(barrier, W * N // 2 - 1 + N - 1)

    def kind_of(k):
        return 0 if k < 9 else 1 if k < 12 else k - 10 if k < 14 else 4 if k < 17 else 5

    def xcopy(src, dst, k, p):
        return pltpu.make_async_remote_copy(
            src_ref=src, dst_ref=dst, send_sem=r.x_s.at[kind_of(k)], recv_sem=r.x_r.at[k],
            device_id={"narrow": p}, device_id_type=MESH)

    cuts = (0, R * 4 // 16, R * 8 // 16, R * 10 // 16, R)
    P = len(cuts) - 1

    def piece(k, src=None, slot=None):
        rows = pl.ds(cuts[k], cuts[k + 1] - cuts[k])
        slot = ni if slot is None else slot
        src = xg.at[slot, rows] if src is None else src.at[rows]
        return src, xg.at[slot, rows]

    def x_side():
        return xcopy(r.data_x, xg.at[ni], 0, n1)

    def x_over(k):
        return xcopy(*piece(k, r.data_x), 1 + k, n2)

    def x_pass(k):
        return xcopy(*piece(k, slot=n2), 1 + P + k, n1)

    small[0].wait()
    r.xbn[ni] = r.xbs[...].astype(F32)
    ex.xbn.gather(r.xbn)
    x_over(0).start()
    for load in small[1:]:
        load.wait()
    r.ad[ni, 0:S, :] = r.als[...]
    r.ad[ni, S : S + 1, :] = r.dgs[...].astype(F32)

    def ad_copy(slot, k, p):
        return xcopy(r.ad.at[slot], r.ad.at[slot], 9 + k, p)

    ad_copy(ni, 1, n2).start()
    ad_copy(ni, 0, n1).start()
    lane = lax.broadcasted_iota(jnp.int32, (1, 128), 1)
    for k in range(Bg):
        prec_k = r.sm_t[r.sm_p[k]]
        r.meta[wi, k : k + 1, :] = jnp.where(
            lane == 0, r.sm_g[k].astype(F32), jnp.where(lane == 1, r.sm_i[k].astype(F32), jnp.where(lane == 2, prec_k, 0.0)))
    r.meta[wi, :, S : 2 * S] = r.tgs[...]
    ex.meta.gather(r.meta)

    loads[0].wait()

    def cast1(k, carry):
        rows = pl.ds(pl.multiple_of(k * 128, 128), 128)
        w1b[rows, :] = r.w1f[rows, :].astype(BF)
        return carry

    lax.fori_loop(0, D // 128, cast1, 0)
    ex.xbn.wait(r.xbn)
    for n in range(N):
        r.xbg[n * brow : (n + 1) * brow, :] = r.xbn[n]
    xbg = r.xbg[...]
    hb, gb = gelu_pair(dot(xbg.astype(BF), w1b[...]))
    hb = hb.astype(BF).astype(F32)
    r.hbn[ni] = jnp.concatenate([hb[:, : Hn // 2], hb[:, Hn // 2 :]], axis=0).astype(BF)
    ex.hbn.gather(r.hbn)
    x_over(1).start()
    x_over(2).start()
    x_side().start()
    r.hgw[wi] = jnp.concatenate([hb, gb], axis=0).astype(BF)
    ex.hgw.gather(r.hgw)
    r.xbw[wi] = jnp.concatenate([xbg[:, : D // 2], xbg[:, D // 2 :]], axis=0).astype(BF)
    ex.xbw.gather(r.xbw)
    loads[2].wait()

    def cast2(k, carry):
        rows = pl.ds(pl.multiple_of(k * 128, 128), 128)
        w2b[rows, :] = r.w2f[rows, :].astype(BF)
        return carry

    lax.fori_loop(0, H // 128, cast2, 0)

    def block(q, first=0, last=P):
        base = q * R + cuts[first]
        size = cuts[last] - cuts[first]
        r.pre[:size, :] = dot(xg[q, cuts[first] : cuts[last], :], w1b[...])
        step = math.gcd(size, 32)

        def part(k, carry):
            src = pl.ds(pl.multiple_of(k * step, step), step)
            dst = pl.ds(pl.multiple_of(base + k * step, step), step)
            out, slope = gelu_pair(r.pre[src, :])
            hid[dst, :] = out.astype(BF)
            gd[dst, :] = slope
            return carry

        lax.fori_loop(0, size // step, part, 0)

    def turn(q):
        xT[:, pl.ds(pl.multiple_of(q * R, R), R)] = xg[q].T

    ex.hbn.wait(r.hbn)
    hbn = [r.hbn[n].astype(F32) for n in range(N)]
    hid_g = jnp.concatenate([h[k * Bg : (k + 1) * Bg] for h in hbn for k in range(2)], axis=1).astype(BF)
    bfeat = dot(hid_g, w2b[...]).astype(BF)
    r.bfs[...] = bfeat.astype(F32)
    gpart = dot(bfeat, w2b[...], NT)
    for n in range(N):
        g = gpart[:, n * Hn : (n + 1) * Hn]
        r.ges[n] = jnp.concatenate([g[:, : Hn // 2], g[:, Hn // 2 :]], axis=0).astype(BF)
    ex.ger.scatter(r.ges, r.ger)
    r.ger[ni] = r.ges[ni]
    loads[3].wait()
    zpart = dot(r.bfs[...].astype(BF), om[...])
    for n in range(N):
        z = zpart[:, n * Mn : (n + 1) * Mn]
        r.zes[n] = jnp.concatenate([z[:, : Mn // 2], z[:, Mn // 2 :]], axis=0).astype(BF)
    ex.zer.scatter(r.zes, r.zer)
    r.zer[ni] = r.zes[ni]
    x_over(3).start()
    later = []
    if resident:
        pairs = ((r.w1_m, r.m1), (r.w1_v, r.v1), (r.w2_m, r.m2), (r.w2_v, r.v2))
        later = [pltpu.make_async_copy(src, dst, lsem.at[5 + k]) for k, (src, dst) in enumerate(pairs)]
    for load in later:
        load.start()
    bf32 = r.bfs[...]
    r.bfw[wi] = jnp.concatenate([bf32[:, : Fn // 2], bf32[:, Fn // 2 :]], axis=0).astype(BF)
    loads[1].wait()
    block(ni)
    xcopy(r.data_x, xg.at[n1], 0, n1).wait_recv()
    block(n1)
    turn(ni)
    turn(n1)
    ex.ger.wait(r.ger)
    r.gw[wi] = jnp.sum(r.ger[...].astype(F32), axis=0).astype(BF)
    ex.gw.gather(r.gw)
    for k in range(3):
        xcopy(*piece(k, slot=n2), 1 + k, n2).wait_recv()
        x_pass(k).start()
    ad_copy(n2, 1, n2).wait_recv()
    ad_copy(n2, 2, n1).start()
    ex.zer.wait(r.zer)
    own_b = pl.ds(pl.multiple_of(wi * Bg, Bg), Bg)
    loads[5].wait()
    zeta = jnp.sum(r.zer[...].astype(F32), axis=0)
    angle = jnp.concatenate([zeta[:Bg], zeta[Bg:]], axis=1) + r.ph[...]
    r.cz[...] = jnp.zeros_like(r.cz)
    r.cz[own_b, :] = scale * jnp.cos(angle)
    sz = scale * jnp.sin(angle)
    r.szw[wi] = jnp.concatenate([sz[:, : Mn // 2], sz[:, Mn // 2 :]], axis=0).astype(BF)
    ex.szw.gather(r.szw)
    loads[4].wait()
    r.prior[...] = dot(r.pwt[...], r.cz[...], NT, HIGH)

    def x_last(k):
        xcopy(*piece(k, slot=n3), 1 + P + k, n1).wait_recv()

    block(n2, 0, 2)
    x_last(0)
    x_last(1)
    block(n3, 0, 2)
    ex.meta.wait(r.meta)
    meta = r.meta[...].reshape(B, 128)
    r.metat[...] = meta.T
    ad_copy(n1, 0, n1).wait_recv()
    ad_copy(n3, 2, n1).wait_recv()
    alphat = jnp.concatenate([r.ad[n, 0:S, :] for n in range(N)], axis=1)
    r.alphat[...] = alphat
    group = jnp.concatenate([r.ad[n, S : S + 1, :] for n in range(N)], axis=1)
    pmask = (0.5 + (meta[:, 0:1] == group).astype(F32)) / F
    r.pmask[...] = pmask
    col = lax.broadcasted_iota(jnp.int32, (1, N * R), 1) + wi * (N * R)
    first = (ni == 0).astype(F32)
    r.amat[...] = jnp.where(meta[:, 1:2] == col.astype(F32), first / meta[:, 2:3], 0.0)
    ex.gw.wait(r.gw)
    gw = r.gw[...].astype(F32)
    r.gmat[...] = jnp.concatenate([gw[:, :Bg].reshape(B, Hn // 2), gw[:, Bg:].reshape(B, Hn // 2)], axis=1).astype(BF)

    def columns(q, first=0, last=P):
        size = cuts[last] - cuts[first]
        return pl.ds(pl.multiple_of(q * R + cuts[first], size), size)

    def kernel_block(cols):
        r.amat[:, cols] = r.pmask[:, cols] * dot(r.gmat[...], hid[cols, :], NT) + r.amat[:, cols]

    def kalpha(cols):
        return dot(r.alphat[:, cols], r.amat[:, cols], NT, HIGH)

    for q in (ni, n1):
        kernel_block(columns(q))
    xcopy(*piece(3, slot=n2), 4, n2).wait_recv()
    x_pass(3).start()
    for q in (n2, n3):
        kernel_block(columns(q, 0, 2))
    block(n2, 2, 4)
    kernel_block(columns(n2, 2, 4))
    kal = r.prior[...] + (kalpha(columns(ni)) + kalpha(columns(n1))) + (kalpha(columns(n2)) + kalpha(columns(n3, 0, 2)))
    r.prior[...] = kal
    x_last(2)
    x_last(3)
    block(n3, 2, 4)

    kernel_block(columns(n3, 2, 4))
    kal = r.prior[...] + kalpha(columns(n3, 2, 4))
    fold = max(1, min(S // 8, 128 // B))
    r.kn[core] = jnp.concatenate([kal[k * (S // fold) : (k + 1) * (S // fold)] for k in range(fold)], axis=1)

    def core_copy(buf, k):
        return xcopy(buf.at[core], buf.at[core], 12 + k, n1)

    def core_sum(buf, k):
        xcopy(buf.at[1 - core], buf.at[1 - core], 12 + k, n1).wait_recv()
        return buf[0] + buf[1]

    core_copy(r.kn, 0).start()
    chip = wi * (N // 2) + side
    r.kw[chip] = core_sum(r.kn, 0)
    ex.kw.gather(r.kw)
    ex.bfw.gather(r.bfw)
    turn(n2)
    turn(n3)
    ex.hgw.wait(r.hgw)
    hg = r.hgw[...].astype(F32)
    r.hbx[ni] = hg[:, :Bg].reshape(B, Hn).astype(BF)
    r.gb[...] = hg[:, Bg:].reshape(B, Hn)
    ex.hbx.gather(r.hbx)
    ex.xbw.wait(r.xbw)
    xbw = r.xbw[...].astype(F32)
    r.xbt[...] = jnp.concatenate([xbw[:, :Bg].reshape(B, D // 2), xbw[:, Bg:].reshape(B, D // 2)], axis=1).T.astype(BF)
    prec = r.metat[2:3, :]
    total = jnp.sum(prec, axis=1, keepdims=True)
    ex.kw.wait(r.kw)
    kal = jnp.sum(r.kw[...], axis=0)
    resid = r.metat[S : 2 * S, :] - jnp.concatenate([kal[:, k * B : (k + 1) * B] for k in range(fold)], axis=0)
    grt = prec * resid / total

    ds = (-r.pmask[...] * dot(grt, r.alphat[...], TN, HIGH)).astype(BF)
    upart = dot(ds, hid[...]).reshape(W, Bg, Hn)
    r.us[...] = jnp.concatenate([upart[:, :, : Hn // 2], upart[:, :, Hn // 2 :]], axis=1).astype(BF)
    ex.ur.scatter(r.us, r.ur)
    for q in range(N):
        rows = slice(q * R, (q + 1) * R)
        dpre[rows, :] = (dot(ds[:, rows], r.gmat[...], TN) * gd[rows, :]).astype(BF)

    def wcopy(src, dst, kind, k, slot, p):
        return pltpu.make_async_remote_copy(
            src_ref=src, dst_ref=dst, send_sem=getattr(r, kind + "_s").at[k], recv_sem=getattr(r, kind + "_r").at[slot],
            device_id={"wide": p}, device_id_type=MESH)

    psend, precv, zsend, zrecv, gat = r.psend, r.precv, r.zsend, r.zrecv, r.gat

    NH = math.gcd(Ck // 16, 4)
    Hk = Ck // NH
    Q, Cq = 1, Hk

    def grad_rows(row):
        return dot(xT[pl.ds(pl.multiple_of(row, Ck), Ck), :], dpre[...])

    def target(step):
        low = a // (A // 2)
        m = a + low * (A - 1 - 2 * a)
        single = A - 1 - 2 * m
        late = (step // single + A - 1) // A
        e = step - single
        t = (1 - late) * (A - 1 - step) + late * (m + (1 - lax.rem(e + 2 * A, 2) * 2) * (m - (e + 2 * A) // 2 + A))
        return t + low * (A - 1 - 2 * t)

    def pcopy(ap, h, q):
        rows = pl.ds(pl.multiple_of(ap * Ck + h * Hk + q * Cq, Cq), Cq)
        return wcopy(psend.at[rows], precv.at[rows], "p", 0, ap * NH * Q + h * Q + q, pair)

    def rows_of(ap):
        return pl.ds(pl.multiple_of(ap * Ck, Ck), Ck)

    def pair_first(ap):
        psend[rows_of(ap), :] = grad_rows((1 - b) * half + ap * Ck).astype(BF)
        pcopy(ap, 0, 0).start()

    def pair_sends(h, first, last):
        def send(step, carry):
            pcopy(target(step), h, 0).start()
            return carry

        if h < NH:
            lax.fori_loop(min(first, A - 1), min(last, A - 1), send, 0)
            if last >= A:
                pcopy(a, h, 0).start()

    def zcopy(ap, h, q):
        rows = pl.ds(h * Hk + q * Cq, Cq)
        return wcopy(zsend.at[ap, rows], zrecv.at[a, rows], "z", 0, h, 2 * ap + b)

    def own_part(ap, carry):
        gd[rows_of(ap), :] = grad_rows(b * half + ap * Ck)
        return carry

    def z_part(ap, h):
        pcopy(ap, h, 0).wait_recv()
        rows = pl.ds(pl.multiple_of(ap * Ck + h * Hk, Hk), Hk)
        return gd[rows, :] + precv[rows, :].astype(F32)

    def z_sends(h, first, last):
        def send(step, carry):
            ap = target(step)
            zsend[ap, h * Hk : (h + 1) * Hk, :] = z_part(ap, h).astype(BF)
            zcopy(ap, h, 0).start()
            return carry

        if h < NH:
            lax.fori_loop(min(first, A - 1), min(last, A - 1), send, 0)

    def z_own(h):
        if h < NH:
            r.zf[h * Hk : (h + 1) * Hk, :] = z_part(a, h)

    def first_sends(step, carry):
        pair_first(target(step))
        return carry

    lax.fori_loop(0, A - 1, first_sends, 0)
    pair_first(a)
    pair_sends(1, 0, 2)

    loss = 0.5 * jnp.sum(jnp.sum(prec * (resid * resid), axis=1, keepdims=True), axis=0, keepdims=True)
    agt = -dot(grt, r.amat[...], precision=HIGH)
    for n in range(N):
        r.ags[n] = agt[:, n * R : (n + 1) * R]
    ex.agr.scatter(r.ags, r.agr)
    r.agr[ni] = r.ags[ni]
    ex.szw.wait(r.szw)

    def unfold(buf):
        v = buf[...].astype(F32)
        return jnp.concatenate([v[:, :Bg].reshape(B, -1), v[:, Bg:].reshape(B, -1)], axis=1)

    r.dzn[ni] = (unfold(r.szw) * dot(grt, r.pwt[...], TN, HIGH)).astype(BF)

    def dz_copy(slot, k, p):
        return xcopy(r.dzn.at[slot], r.dzn.at[slot], 17 + k, p)

    dz_copy(ni, 1, n2).start()
    dz_copy(ni, 0, n1).start()
    lax.fori_loop(0, A, own_part, 0)
    ex.ur.wait(r.ur)
    r.ur[wi] = r.us[wi]
    r.uz[wi] = jnp.sum(r.ur[...].astype(F32), axis=0).astype(BF)
    ex.uz.gather(r.uz)
    pair_sends(1, 2, A)
    for h in range(2, NH):
        pair_sends(h, 0, A)
    z_sends(0, 0, A)
    z_own(0)
    z_sends(1, 0, 1)
    ex.bfw.wait(r.bfw)
    ex.uz.wait(r.uz)
    r.uzn[ni] = unfold(r.uz).astype(BF)

    def u_copy(slot, k, p):
        return xcopy(r.uzn.at[slot], r.uzn.at[slot], 14 + k, p)

    u_copy(ni, 1, n2).start()
    u_copy(ni, 0, n1).start()
    dz_copy(n2, 1, n2).wait_recv()
    dz_copy(n2, 2, n1).start()
    z_sends(1, 1, A)
    z_own(1)

    others = pl.ds(0, A - 1)
    mine = b * A + a

    def shard(slot, h=0, q=0, count=Ck):
        return pl.ds(pl.multiple_of(slot * Ck + h * Hk + q * Cq, min(count, Cq)), count)

    def fcopy(ap, h, q):
        rows = shard(b * A + ap, h, q, Cq)
        return wcopy(gat.at[rows], gat.at[rows], "f", 0, 0, pair)

    def gcopy(ap, h, q, way):
        rows = shard(b * A + ap, h, q, Cq)
        return wcopy(gat.at[rows], gat.at[rows], "g", 0 if way > 0 else 1, (ap * NH + h) * Q + q, 2 * (a + way) + b)

    def straight(h):
        return NH > 1 and h >= NH - DIRECT

    def gdirect(ap, h, q):
        rows = shard(mine, h, q, Cq)
        return wcopy(gat.at[rows], gat.at[rows], "g", 2, (a * NH + h) * Q + q, 2 * ap + b)

    def z_done(h):
        if h >= NH:
            return
        rows = slice(h * Hk, (h + 1) * Hk)
        part = pl.ds(h * Hk, Hk)
        wcopy(zsend.at[others, part], zrecv.at[others, part], "z", 0, h, pair).wait_recv()

        def gain(k, carry):
            r.zf[rows, :] = r.zf[rows, :] + zrecv[lax.rem(a + k, A), rows, :].astype(F32)
            return carry

        lax.fori_loop(1, A, gain, 0)
        gat[shard(mine, h, 0, Hk), :] = r.zf[rows, :].astype(BF)
        for q in range(Q):
            fcopy(a, h, q).start()
        if straight(h):

            def send(step, carry):
                for q in range(Q):
                    gdirect(target(step), h, q).start()
                return carry

            lax.fori_loop(0, A - 1, send, 0)
        else:
            for q in range(Q):

                @pl.when(a + 1 < A)
                def _():
                    gcopy(a, h, q, 1).start()

                @pl.when(a > 0)
                def _():
                    gcopy(a, h, q, -1).start()

    def g_pass(h, first, last):
        if h >= NH:
            return

        def step(k, carry):
            below, above = a - 1 - k // Q, a + 1 + k // Q
            q = lax.rem(k, Q)

            @pl.when(below >= 0)
            def _():
                gcopy(below, h, q, 1).wait_recv()

                if not straight(h):

                    @pl.when(a + 1 < A)
                    def _():
                        gcopy(below, h, q, 1).start()

                fcopy(below, h, q).start()

            @pl.when(above < A)
            def _():
                gcopy(above, h, q, -1).wait_recv()

                if not straight(h):

                    @pl.when(a > 0)
                    def _():
                        gcopy(above, h, q, -1).start()

                fcopy(above, h, q).start()

            return carry

        lax.fori_loop(min(first, A - 1) * Q, min(last, A - 1) * Q, step, 0)

    z_done(0)
    z_sends(2, 0, A)
    z_own(2)
    u_copy(n2, 1, n2).wait_recv()
    u_copy(n2, 2, n1).start()
    z_done(1)
    g_pass(0, 0, 1)
    z_sends(3, 0, 2)
    z_done(2)
    z_sends(3, 2, A)
    z_own(3)
    u_copy(n1, 0, n1).wait_recv()
    u_copy(n3, 2, n1).wait_recv()
    dz_copy(n1, 0, n1).wait_recv()
    dz_copy(n3, 2, n1).wait_recv()
    acc = jnp.zeros((B, Fn), F32)
    for n in range(N):
        acc = acc + dot(r.uzn[n], w2b[n * Hn : (n + 1) * Hn, :])
        acc = acc + dot(r.dzn[n], om[:, n * Mn : (n + 1) * Mn], NT)
    r.db[...] = jnp.concatenate([acc, unfold(r.bfw)], axis=0).astype(BF)
    for n in range(N):
        r.dhs[n] = dot(r.db[:B, :], w2b[n * Hn : (n + 1) * Hn, :], NT).astype(BF)
    ex.dhr.scatter(r.dhs, r.dhr)
    r.dhr[ni] = r.dhs[ni]
    g_pass(1, 0, 1)
    g_pass(0, 1, 2)
    g_pass(2, 0, 1)
    z_done(3)
    g_pass(1, 1, 2)

    def two(v):
        return jnp.sum(jnp.sum(v * v, axis=1, keepdims=True), axis=0, keepdims=True)

    square = jnp.zeros((1, 1), F32)
    for n in range(N):
        if n == 0:
            ex.hbx.wait(r.hbx)
        hu = jnp.concatenate([r.hbx[n], r.uzn[n]], axis=0)
        g2 = dot(hu, r.db[...], TN)
        r.g2[n * Hn : (n + 1) * Hn, :] = g2
        square = square + two(g2)

    ex.agr.wait(r.agr)
    agt = jnp.sum(r.agr[...], axis=0)
    r.agrad[...] = agt
    ex.dhr.wait(r.dhr)
    r.dpb[...] = (jnp.sum(r.dhr[...].astype(F32), axis=0) * r.gb[...]).astype(BF)

    square = square * (1.0 / W) + two(r.zf[...] + dot(r.xbt[shard(mine), :], r.dpb[...])) + two(agt)
    r.nn[core] = jnp.broadcast_to(square, (8, 128))
    core_copy(r.nn, 1).start()
    g_pass(0, 2, A)
    r.nw[chip] = core_sum(r.nn, 1)
    ex.nw.gather(r.nw)
    g_pass(2, 1, 2)
    g_pass(3, 0, 1)
    g_pass(1, 2, A)
    g_pass(2, 2, A)
    g_pass(3, 1, A)
    ex.nw.wait(r.nw)
    norm = jnp.sum(r.nw[...], axis=0)
    lanes = lax.broadcasted_iota(jnp.int32, (8, 128), 1)
    r.scal[...] = jnp.where(lanes == 0, loss, jnp.where(lanes == 1, total, norm))

    theirs = pl.ds(pl.multiple_of((1 - b) * half, half), half)
    ours = pl.ds(pl.multiple_of(b * half, half), half)
    wcopy(gat.at[theirs], gat.at[theirs], "f", 0, 0, pair).wait_recv()

    for name in live:
        vars(ex)[name].drain(getattr(r, name))
    for buf, k in ((xg, 0), (r.ad, 9), (r.uzn, 14), (r.dzn, 17)):
        xcopy(buf.at[pl.ds(0, 3)], buf.at[pl.ds(0, 3)], k, n1).wait_send()
    core_copy(r.kn, 0).wait_send()
    core_copy(r.nn, 1).wait_send()
    wcopy(psend, precv, "p", 0, 0, pair).wait_send()
    wcopy(gat.at[ours], gat.at[ours], "f", 0, 0, pair).wait_send()
    wcopy(zsend.at[others], zrecv.at[others], "z", 0, 0, pair).wait_send()
    straights = sum(straight(h) for h in range(NH))
    if straights:
        direct = pl.ds(0, (A - 1) * Hk * straights)
        wcopy(gat.at[direct], gat.at[direct], "g", 2, 0, pair).wait_send()
    for k in range(A):
        up, down = (pl.ds(0, n * Hk * (NH - straights)) for n in (k + 1, A - k))

        @pl.when((a == k) & (a + 1 < A))
        def _():
            wcopy(gat.at[up], gat.at[up], "g", 0, 0, pair).wait_send()

        @pl.when((a == k) & (a > 0))
        def _():
            wcopy(gat.at[down], gat.at[down], "g", 1, 0, pair).wait_send()

    for load in later:
        load.wait()


CORR1 = 1.0 - 0.9**STEP_NUM
CORR2 = 1.0 - 0.999**STEP_NUM


def adamw(weight, grad, moment, second, rate, decay):
    moment_new = 0.9 * moment + 0.1 * grad
    second_new = 0.999 * second + 0.001 * grad * grad
    step = moment_new / (jnp.sqrt(second_new) * (1.0 / math.sqrt(CORR2)) + 1e-08)
    new = weight * (1.0 - rate * decay) - (rate / CORR1) * step
    return moment_new, second_new, new


def update_kernel(resident, slots, C, names, *refs):
    r = SimpleNamespace(**dict(zip(names, refs)))
    if not resident:
        pairs = ((r.w1, r.w1f), (r.w1_m, r.m1), (r.w1_v, r.v1), (r.w2, r.w2f), (r.w2_m, r.m2), (r.w2_v, r.v2))
        loads = [pltpu.make_async_copy(src, dst, r.lsem.at[k]) for k, (src, dst) in enumerate(pairs)]
        for load in loads:
            load.start()
        for load in loads:
            load.wait()
    for k in range(3):
        r.s3[k] = r.scal[0:1, k : k + 1]
    last = [pltpu.make_async_copy(r.s3.at[k], dst, r.asem.at[3 + k]) for k, dst in enumerate((r.loss, r.total, r.normsq))]
    for copy in last:
        copy.start()
    small = [pltpu.make_async_copy(src, r.asl.at[k], r.asem.at[k]) for k, src in enumerate((r.at, r.atm, r.atv))]
    for load in small:
        load.start()
    norm = r.scal[0:1, 2:3]
    clip = jnp.minimum(1.0, 0.1 / jnp.sqrt(norm))
    ring = (r.sm, r.sv, r.sn, r.sc)

    def copies(outs, slot, rows):
        return [pltpu.make_async_copy(buf.at[slot], out.at[rows], r.osem.at[slot, k]) for k, (buf, out) in enumerate(zip(ring, outs))]

    def chunk(grad, state, outs, k, ahead):
        w, m, v = state
        slot = lax.rem(k + ahead, slots)
        base = pl.multiple_of(k * C, C)
        rows = pl.ds(base, C)

        def drain():
            for copy in copies(outs, slot, rows):
                copy.wait()

        if ahead:
            drain()
        else:
            pl.when(k >= slots)(drain)

        def part(j, carry):
            src = pl.ds(pl.multiple_of(base + j * 16, 16), 16)
            dst = pl.ds(pl.multiple_of(j * 16, 16), 16)
            mn, vn, wn = adamw(w[src, :], clip * grad[src, :], m[src, :], v[src, :], 0.03, 0.01)
            r.sm[slot, dst, :] = mn
            r.sv[slot, dst, :] = vn
            r.sn[slot, dst, :] = wn
            r.sc[slot, dst, :] = wn.astype(BF)
            return carry

        lax.fori_loop(0, C // 16, part, 0, unroll=True)
        for copy in copies(outs, slot, rows):
            copy.start()

    outs1 = (r.m1o, r.v1o, r.n1o, r.c1o)
    outs2 = (r.m2o, r.v2o, r.n2o, r.c2o)
    count1, count2 = r.w1f.shape[0] // C, r.w2f.shape[0] // C

    def step2(k, carry):
        chunk(r.g2, (r.w2f, r.m2, r.v2), outs2, k, 0)
        return carry

    def step1(k, carry):
        chunk(r.gs, (r.w1f, r.m1, r.v1), outs1, k, count2)
        return carry

    lax.fori_loop(0, count2, step2, 0)
    r.gs[...] = r.gat[...].astype(F32) + dot(r.xbt[...], r.dpb[...])
    lax.fori_loop(0, count1, step1, 0)
    for load in small:
        load.wait()
    am, av, an = adamw(r.asl[0], clip * r.agrad[...], r.asl[1], r.asl[2], 0.2, 0.0)
    for k, v in enumerate((am, av, an)):
        r.ast[k] = v
    alphas = [pltpu.make_async_copy(r.ast.at[k], dst, r.asem.at[k]) for k, dst in enumerate((r.amo, r.avo, r.ano))]
    for copy in alphas:
        copy.start()
    for k in range(slots):
        for copy in copies(outs1, k, pl.ds(0, C)):
            copy.wait()
    for copy in last + alphas:
        copy.wait()


def on_device(
    data_x, data_group, batch_x, batch_group, batch_index, prec_index, prec_table, targets,
    omega, phase, prior_w, w1_master, w1_moment, w1_second, w2_master, w2_moment, w2_second,
    alpha, alpha_moment, alpha_second,
):
    W, N = lax.axis_size("wide"), lax.axis_size("narrow")
    A = W // 2
    R, D = data_x.shape
    brow, Bg, S = batch_x.shape[0], targets.shape[0], targets.shape[1]
    F, M = omega.shape
    Hn, Fn, Mn, H = w1_master.shape[1], w2_master.shape[1], M // N, w2_master.shape[0]
    B, Ck = W * Bg, D // 2 // A
    hbm, vmem = (pl.BlockSpec(memory_space=m) for m in (pl.ANY, pltpu.VMEM))
    resident = B <= 128
    fold = max(1, min(S // 8, 128 // B))
    args = dict(
        data_x=(data_x, hbm), dgroup=(data_group.reshape(1, R), hbm), batch_x=(batch_x, hbm),
        bgroup=(batch_group, hbm), bindex=(batch_index, hbm), pindex=(prec_index, hbm),
        ptable=(prec_table, hbm), targets=(targets, hbm), omega=(omega, hbm),
        phase=(phase.reshape(1, M), hbm), prior_wt=(prior_w.T, hbm), w1=(w1_master, hbm),
        w2=(w2_master, hbm), alphat_own=(alpha.T, hbm),
    )
    state = dict(
        w1=(w1_master, hbm), w1_m=(w1_moment, hbm), w1_v=(w1_second, hbm),
        w2=(w2_master, hbm), w2_m=(w2_moment, hbm), w2_v=(w2_second, hbm),
    )
    outs = dict(
        scal=((8, 128), F32), agrad=((S, R), F32), gat=((D, Hn), BF), xbt=((D, B), BF), dpb=((B, Hn), BF),
        g2=((H, Fn), F32),
    )
    held = dict(
        w1f=((D, Hn), F32), m1=((D, Hn), F32), v1=((D, Hn), F32), w2f=((H, Fn), F32), m2=((H, Fn), F32), v2=((H, Fn), F32),
    )
    scratch = dict(
        xg=((N, R, D), BF), xT=((D, N * R), BF), hid=((N * R, Hn), BF), gd=((N * R, Hn), F32),
        dpre=((N * R, Hn), BF), pre=((R, Hn), F32), w1b=((D, Hn), BF),
        w2b=((H, Fn), BF), om=((Fn, M), BF), pwt=((S, Mn), F32),
        xbg=((Bg, D), F32), xbs=((brow, D), BF), tgs=((Bg, S), F32), dgs=((1, R), jnp.int32), als=((S, R), F32), ph=((1, Mn), F32), ges=((N, 2 * Bg, Hn // 2), BF), zes=((N, 2 * Bg, Mn // 2), BF), bfs=((Bg, Fn), F32), zf=((Ck, Hn), F32), us=((W, 2 * Bg, Hn // 2), BF), ags=((N, S, R), F32),
        dhs=((N, B, Hn), BF), cz=((B, Mn), F32), prior=((S, B), F32),
        metat=((128, B), F32), alphat=((S, N * R), F32), pmask=((B, N * R), F32), amat=((B, N * R), F32),
        gmat=((B, Hn), BF), db=((2 * B, Fn), BF),
        psend=((A * Ck, Hn), BF), precv=((A * Ck, Hn), BF), zsend=((A, Ck, Hn), BF), zrecv=((A + 1, Ck, Hn), BF),
        gb=((B, Hn), F32),
        meta=((W, Bg, 128), F32), xbw=((W, 2 * Bg, D // 2), BF), hgw=((W, 2 * Bg, Hn), BF),
        bfw=((W, 2 * Bg, Fn // 2), BF), gw=((W, 2 * Bg, Hn // 2), BF), kw=((W * N // 2, S // fold, fold * B), F32),
        ur=((W, 2 * Bg, Hn // 2), BF), uz=((W, 2 * Bg, Hn // 2), BF), szw=((W, 2 * Bg, Mn // 2), BF), nw=((W * N // 2, 8, 128), F32),
        xbn=((N, brow, D), F32), ad=((N, S + 1, R), F32), hbn=((N, 2 * Bg, Hn // 2), BF), ger=((N, 2 * Bg, Hn // 2), BF), zer=((N, 2 * Bg, Mn // 2), BF),
        kn=((2, S // fold, fold * B), F32), agr=((N, S, R), F32), uzn=((N, B, Hn), BF), dzn=((N, B, Mn), BF), hbx=((N, B, Hn), BF), dhr=((N, B, Hn), BF),
        nn=((2, 8, 128), F32),
    )
    if resident:
        args.update(state)
        outs.update(held)
    else:
        scratch.update(w1f=held["w1f"], w2f=held["w2f"])
    pieces = A * math.gcd(Ck // 16, 4)
    count = 2 * len(WIDE_EX + NARROW_EX + CHIP_EX)
    sems = [("lsem", 18), ("x_s", 6), ("x_r", 20), ("es", count), ("p_s", 1), ("p_r", pieces), ("z_s", 1), ("z_r", 4)]
    sems += [("f_s", 1), ("f_r", 1), ("g_s", 3), ("g_r", pieces)]
    smem = dict(sm_g=(Bg, jnp.int32), sm_i=(Bg, jnp.int32), sm_p=(Bg, jnp.int32), sm_t=(prec_table.shape[0], F32))
    names = [*args, *outs, *scratch, *smem] + [n for n, _ in sems]
    grads = pl.pallas_call(
        lambda *refs: step_kernel(W, N, resident, names, *refs),
        out_shape=[(pltpu.VMEM if resident else jax.ShapeDtypeStruct)(s, t) for s, t in outs.values()],
        in_specs=[spec for _, spec in args.values()],
        out_specs=[vmem] * len(outs),
        scratch_shapes=[pltpu.VMEM(s, t) for s, t in scratch.values()]
        + [pltpu.SMEM((k,), t) for k, t in smem.values()]
        + [pltpu.SemaphoreType.DMA((k,)) for _, k in sems],
        compiler_params=pltpu.CompilerParams(collective_id=0, has_side_effects=True, vmem_limit_bytes=(62 if not resident else 39) * 2**20),
        name="gradients",
    )(*[v for v, _ in args.values()])

    args2 = {k: (v, vmem) for k, v in zip(outs, grads)}
    args2.update(at=(alpha.T, hbm), atm=(alpha_moment.T, hbm), atv=(alpha_second.T, hbm))
    C, slots = 256, 4
    outs2 = dict(amo=((S, R), F32, hbm), avo=((S, R), F32, hbm), ano=((S, R), F32, hbm))
    outs2.update(loss=((1, 1), F32, hbm), total=((1, 1), F32, hbm), normsq=((1, 1), F32, hbm))
    for k, shape in (("1", (D, Hn)), ("2", (H, Fn))):
        outs2.update({"m" + k + "o": (shape, F32, hbm), "v" + k + "o": (shape, F32, hbm)})
        outs2.update({"n" + k + "o": (shape, F32, hbm), "c" + k + "o": (shape, BF, hbm)})
    scratch2 = dict(
        gs=pltpu.VMEM((D, Hn), F32), sm=pltpu.VMEM((slots, C, Hn), F32), sv=pltpu.VMEM((slots, C, Hn), F32),
        sn=pltpu.VMEM((slots, C, Hn), F32), sc=pltpu.VMEM((slots, C, Hn), BF), osem=pltpu.SemaphoreType.DMA((slots, 4)),
        asl=pltpu.VMEM((3, S, R), F32), ast=pltpu.VMEM((3, S, R), F32), asem=pltpu.SemaphoreType.DMA((6,)), s3=pltpu.VMEM((3, 1, 1), F32),
    )
    if not resident:
        args2.update(state)
        scratch2.update({k: pltpu.VMEM(s, t) for k, (s, t) in held.items()}, lsem=pltpu.SemaphoreType.DMA((6,)))
    names2 = [*args2, *outs2, *scratch2]
    new = pl.pallas_call(
        lambda *refs: update_kernel(resident, slots, C, names2, *refs),
        out_shape=[jax.ShapeDtypeStruct(s, t) for s, t, _ in outs2.values()],
        in_specs=[spec for _, spec in args2.values()],
        out_specs=[spec for _, _, spec in outs2.values()],
        scratch_shapes=list(scratch2.values()),
        compiler_params=pltpu.CompilerParams(vmem_limit_bytes=(36 if not resident else 12) * 2**20),
        name="adamw",
    )(*[v for v, _ in args2.values()])
    new = dict(zip(outs2, new))
    return (
        new["loss"].reshape(()), new["total"].reshape(()), new["normsq"].reshape(()),
        new["m1o"], new["v1o"], new["n1o"], new["c1o"],
        new["m2o"], new["v2o"], new["n2o"], new["c2o"],
        new["amo"].T, new["avo"].T, new["ano"].T,
    )


def solution(mesh):
    both = P(("wide", "narrow"))
    both2 = P(("wide", "narrow"), None)
    col = P(None, "narrow")
    return jax.shard_map(
        on_device,
        mesh=mesh,
        in_specs=(both2, both, both2, P("wide"), P("wide"), P("wide"), P(), P("wide", None), P(), P(), P())
        + (col,) * 6 + (both2,) * 3,
        out_specs=(P(), P(), P()) + (col,) * 8 + (both2,) * 3,
        check_vma=False,
    )
```
